32 devices in a mesh: row: 4 (over y, x), col: 8 (over z, core).
Axes of the slice: x: 2, y: 2, z: 4, core: 2. Of those that a mesh axis runs over, the one named last changes fastest.
Arguments:
- layer_stack: bfloat16 [8, 8192, 2048], P(None, ('row', 'col')), may hold values from -6 to 6
- mix_coeffs: float32 [8192, 4, 8], P(('row', 'col')), may hold values from -3 to 3
- prefix: int32 [8], P('row'), may hold values from 0 to 1024
- ln_gain: float32 [4, 2048], replicated, may hold values from 0.5 to 1.5
- ln_bias: float32 [4, 2048], replicated, may hold values from -0.3 to 0.3
- qkv_weight: bfloat16 [3, 2048, 2048], P(None, 'row', 'col'), may hold values from -0.125 to 0.125
- qkv_bias: float32 [3, 2048], P(None, 'col'), may hold values from -0.15 to 0.15
- out_weight: bfloat16 [2048, 2048], P('col', 'row'), may hold values from -3 to 3
- out_bias: float32 [2048], replicated, may hold values from -0.6 to 0.6
- up_weight: bfloat16 [2048, 8192], P('row', 'col'), may hold values from -0.125 to 0.125
- up_bias: float32 [8192], P('col'), may hold values from -1.5 to 1.5
- down_weight: bfloat16 [8192, 2048], P('col', 'row'), may hold values from -0.0625 to 0.0625
- down_bias: float32 [2048], replicated, may hold values from -1.5 to 1.5
- mix_gain: float32 [2048], replicated, may hold values from 0.5 to 1.5
- mix_in: float32 [2048, 36], replicated, may hold values from -0.125 to 0.125
- mix_out: float32 [36, 36], replicated, may hold values from -1 to 1
- out_grad: bfloat16 [8192, 2048], P(('row', 'col')), may hold values from -6 to 6
- coeff_grad: float32 [8192, 36], P(('row', 'col')), may hold values from -6 to 6
Outputs:
- layer_out: float32 [8192, 2048], P(('row', 'col'))
- coeff_out: float32 [8192, 36], P(('row', 'col'))
- stack_grad: float32 [8, 8192, 2048], P(None, ('row', 'col'))
- coeffs_grad: float32 [8192, 4, 8], P(('row', 'col'))
- ln_gain_grad: float32 [4, 2048], replicated
- ln_bias_grad: float32 [4, 2048], replicated
- qkv_weight_grad: float32 [3, 2048, 2048], P(None, 'row', 'col')
- qkv_bias_grad: float32 [3, 2048], P(None, 'col')
- out_weight_grad: float32 [2048, 2048], P('col', 'row')
- out_bias_grad: float32 [2048], replicated
- up_weight_grad: float32 [2048, 8192], P('row', 'col')
- up_bias_grad: float32 [8192], P('col')
- down_weight_grad: float32 [8192, 2048], P('col', 'row')
- down_bias_grad: float32 [2048], replicated
- mix_gain_grad: float32 [2048], replicated
- mix_in_grad: float32 [2048, 36], replicated
- mix_out_grad: float32 [36, 36], replicated
The draws below stay inside these ranges and needn't reach their ends.
Inputs may be any that keep to these rules, and one draw needn't show every extreme that they name: prefix[b] leading tokens of sequence b see each other in both directions; the rest see only earlier tokens and that prefix.
All inputs are finite; a program needn't handle non-finite values.
Results may differ from the reference program's by a relative error of at most 0.039.
Values may be sent and summed in bfloat16 or wider, within the bound.
No kernel may reach another device: no remote copies, remote signals or barrier semaphores. Data moves between devices by JAX's collectives and lax.ppermute only.
A program may use at most 384 MiB of HBM per device.

```python
import jax
import jax.numpy as jnp
from jax import lax

D = 2048
HEADS = 16
HD = 128
FF = 8192
ROT = 32
NIN = 8
NC = 36
MIXH = 36
LEN = 1024
SEQS = 8
TOKENS = 8192


def set_ends(entries, rng, smallest, top_value):
    longest = entries.shape.index(max(entries.shape))
    spots = []
    for shift in (0, 1):
        where = [jax.random.randint(jax.random.fold_in(rng, axis), (), 0, length) for axis, length in enumerate(entries.shape)]
        where[longest] = (where[longest] + shift) % entries.shape[longest]
        spots.append(tuple(where))
    return entries.at[spots[0]].set(smallest).at[spots[1]].set(top_value)


def block_scale(rng, shape, cuts, least, largest):
    def one(axis_at, parts):
        heights = jax.random.uniform(jax.random.fold_in(jax.random.fold_in(rng, 6), axis_at), (parts,), jnp.float32, least / len(cuts), largest / len(cuts))
        return jnp.repeat(jnp.exp(heights), shape[axis_at] // parts).reshape((-1,) + (1,) * (len(shape) - axis_at - 1))

    level = one(*cuts[0])
    for cut in cuts[1:]:
        level = level * one(*cut)
    return level


def scatter_about(rng, dims, scale, most, cuts=(), kind=jnp.bfloat16):
    result = scale * jax.random.normal(rng, dims, jnp.float32)
    if cuts:
        result = result * block_scale(rng, dims, cuts, -0.22, 0.18)
    return jnp.clip(result, -most, most).astype(kind)


def setup_inputs(seed: int = 0) -> dict:
    streams_of = jax.random.split(jax.random.key(seed), 19)
    layer_stack = scatter_about(streams_of[0], (NIN, TOKENS, D), 1.0, 6.0, ((1, 32),))
    mix_coeffs = scatter_about(streams_of[1], (TOKENS, 4, NIN), 0.5, 3.0, ((0, 32),), jnp.float32)
    prefix = set_ends(jax.random.randint(streams_of[2], (SEQS,), 0, LEN + 1), jax.random.fold_in(streams_of[2], 1), 0, LEN).astype(jnp.int32)
    ln_gain = jnp.clip(1.0 + 0.1 * jax.random.normal(streams_of[3], (4, D), jnp.float32), 0.5, 1.5)
    ln_bias = scatter_about(streams_of[4], (4, D), 0.05, 0.3, (), jnp.float32)
    qkv_weight = scatter_about(streams_of[5], (3, D, D), D ** -0.5, 0.125, ((1, 4), (2, 8)))
    qkv_bias = scatter_about(streams_of[6], (3, D), 0.02, 0.15, ((1, 8),), jnp.float32)
    out_weight = scatter_about(streams_of[7], (D, D), (max(2 * D // LEN, 1)) ** -0.5, 3.0, ((0, 8), (1, 4)))
    out_bias = scatter_about(streams_of[8], (D,), 0.1, 0.6, (), jnp.float32)
    up_weight = scatter_about(streams_of[9], (D, FF), D ** -0.5, 0.125, ((0, 4), (1, 8)))
    up_bias = scatter_about(streams_of[10], (FF,), 0.3, 1.5, ((0, 8),), jnp.float32)
    down_weight = scatter_about(streams_of[11], (FF, D), FF ** -0.5, 0.0625, ((0, 8), (1, 4)))
    down_bias = scatter_about(streams_of[12], (D,), 0.3, 1.5, (), jnp.float32)
    mix_gain = jnp.clip(1.0 + 0.1 * jax.random.normal(streams_of[13], (D,), jnp.float32), 0.5, 1.5)
    mix_in = scatter_about(streams_of[14], (D, MIXH), D ** -0.5, 0.125, (), jnp.float32)
    mix_out = scatter_about(streams_of[15], (MIXH, NC), MIXH ** -0.5, 1.0, (), jnp.float32)
    out_grad = scatter_about(streams_of[16], (TOKENS, D), 1.0, 6.0, ((0, 32),))
    coeff_grad = scatter_about(streams_of[17], (TOKENS, NC), 1.0, 6.0, ((0, 32),), jnp.float32)
    return dict(layer_stack=layer_stack, mix_coeffs=mix_coeffs, prefix=prefix, ln_gain=ln_gain, ln_bias=ln_bias, qkv_weight=qkv_weight, qkv_bias=qkv_bias, out_weight=out_weight, out_bias=out_bias, up_weight=up_weight, up_bias=up_bias, down_weight=down_weight, down_bias=down_bias, mix_gain=mix_gain, mix_in=mix_in, mix_out=mix_out, out_grad=out_grad, coeff_grad=coeff_grad)


@jax.custom_vjp
def low(v):
    return lax.optimization_barrier(v.astype(jnp.bfloat16)).astype(jnp.float32)

@jax.custom_vjp
def low_back(v):
    return v

def low_keep(v):
    return (low(v), None)

def low_pass(kept, grad):
    return (grad,)

def back_keep(v):
    return (v, None)

def back_low(kept, grad):
    return (low(grad),)
low.defvjp(low_keep, low_pass)
low_back.defvjp(back_keep, back_low)
eps_layer = 1e-05
eps_rms = 1e-06
finest = lax.Precision.HIGHEST

def layer_norm(values, norm_gain, norm_bias):
    centred = values - lax.optimization_barrier(jnp.mean(values, axis=-1, keepdims=True))
    spread = lax.optimization_barrier(jnp.mean(centred * centred, axis=-1, keepdims=True))
    return centred * lax.rsqrt(spread + eps_layer) * norm_gain + norm_bias

def rotary(seq_length):
    half_rot = ROT // 2
    inv_freq = 10000.0 ** (-(jnp.arange(half_rot, dtype=jnp.float32) * 2.0) / ROT)
    angles = jnp.arange(seq_length, dtype=jnp.float32)[:, None] * inv_freq[None, :]
    angles = jnp.concatenate([angles, angles], axis=1)
    return (jnp.cos(angles), jnp.sin(angles))

def rotate(values, cos_table, sine_table):
    half_rot = ROT // 2
    turned = jnp.concatenate([-values[..., half_rot:ROT], values[..., :half_rot]], axis=-1)
    rotated = values[..., :ROT] * cos_table[:, None, :] + turned * sine_table[:, None, :]
    return jnp.concatenate([rotated, values[..., ROT:]], axis=-1)

def attend(block_items):
    queries, key_rows, value_rows, prefix_len = block_items
    positions = jnp.arange(LEN, dtype=jnp.int32)
    allowed = (positions[None, :] <= positions[:, None]) | (positions[None, :] < prefix_len)
    raw_scores = jnp.einsum('qhd,khd->hqk', queries, key_rows, precision=finest) * HD ** (-0.5)
    raw_scores = low_back(raw_scores)
    raw_scores = jnp.where(allowed[None], raw_scores, -1e+30)
    row_max = lax.optimization_barrier(jnp.max(raw_scores, axis=-1, keepdims=True))
    exp_scores = jnp.exp(raw_scores - row_max)
    probs_low = low(exp_scores / lax.optimization_barrier(jnp.sum(exp_scores, axis=-1, keepdims=True)))
    return jnp.einsum('hqk,khd->qhd', probs_low, value_rows, precision=finest)

def mixing(layer_out, mix_gain, mix_in, mix_out):
    scaled = layer_out * lax.rsqrt(lax.optimization_barrier(jnp.mean(layer_out * layer_out, axis=-1, keepdims=True)) + eps_rms) * mix_gain
    middle_act = jax.nn.gelu(jnp.dot(scaled, mix_in, precision=finest, preferred_element_type=jnp.float32), approximate=False)
    return jnp.dot(middle_act, mix_out, precision=finest, preferred_element_type=jnp.float32)

def forward(layer_stack, mix_coeffs, ln_gain, ln_bias, qkv_weight, qkv_bias, out_weight, out_bias, up_weight, up_bias, down_weight, down_bias, mix_gain, mix_in, mix_out, prefix):
    streams = jnp.einsum('tsj,jtd->tsd', mix_coeffs, layer_stack, precision=finest)
    normed = low(low_back(layer_norm(streams[:, :3], ln_gain[:3], ln_bias[:3])))
    projected = jnp.einsum('tsd,sde->tse', normed, qkv_weight, precision=finest) + qkv_bias
    projected = low_back(projected).reshape(SEQS, LEN, 3, HEADS, HD)
    cos_table, sine_table = rotary(LEN)
    query_rot = low(rotate(projected[:, :, 0], cos_table, sine_table))
    key_rot = low(rotate(projected[:, :, 1], cos_table, sine_table))
    value_rows = low(projected[:, :, 2])
    head_out = lax.map(jax.checkpoint(attend), (query_rot, key_rot, value_rows, prefix))
    head_out = low(low_back(head_out.reshape(TOKENS, D)))
    attn_out = low(low_back(jnp.dot(head_out, out_weight, precision=finest, preferred_element_type=jnp.float32) + out_bias))
    hidden = streams[:, 3] + attn_out
    normed2 = low(low_back(layer_norm(hidden, ln_gain[3], ln_bias[3])))
    up_pre = low_back(jnp.dot(normed2, up_weight, precision=finest, preferred_element_type=jnp.float32) + up_bias)
    act_out = low(jax.nn.gelu(up_pre, approximate=False))
    down_out = low(low_back(jnp.dot(act_out, down_weight, precision=finest, preferred_element_type=jnp.float32) + down_bias))
    layer_out = hidden + down_out
    return (layer_out, mixing(layer_out, mix_gain, mix_in, mix_out))

def reference(layer_stack, mix_coeffs, prefix, ln_gain, ln_bias, qkv_weight, qkv_bias, out_weight, out_bias, up_weight, up_bias, down_weight, down_bias, mix_gain, mix_in, mix_out, out_grad, coeff_grad):

    def run(stack_f, coeffs_f, gain_f, bias_f, qkv_w, qkv_b, out_w, out_b, up_w, up_b, down_w, down_b, mgain_f, mixin_f, mixout_f):
        return forward(stack_f, coeffs_f, gain_f, bias_f, qkv_w, qkv_b, out_w, out_b, up_w, up_b, down_w, down_b, mgain_f, mixin_f, mixout_f, prefix)
    (layer_out, coeff_out), pull_back = jax.vjp(run, layer_stack.astype(jnp.float32), mix_coeffs, ln_gain, ln_bias, qkv_weight.astype(jnp.float32), qkv_bias, out_weight.astype(jnp.float32), out_bias, up_weight.astype(jnp.float32), up_bias, down_weight.astype(jnp.float32), down_bias, mix_gain, mix_in, mix_out)
    gradients = pull_back((out_grad.astype(jnp.float32), coeff_grad))
    return (layer_out, coeff_out, gradients[0], gradients[1], gradients[2], gradients[3], gradients[4], gradients[5], gradients[6], gradients[7], gradients[8], gradients[9], gradients[10], gradients[11], gradients[12], gradients[13], gradients[14])
```

```python
import functools

import jax
import jax.numpy as jnp
from jax import lax
from jax.experimental import pallas as pl
from jax.experimental.pallas import tpu as pltpu
from jax.sharding import Mesh, PartitionSpec as P

HD = 128
ROT = 32
LEN = 1024
EPS_LAYER = 1e-05
EPS_RMS = 1e-06
BF = jnp.bfloat16
F32 = jnp.float32
FINEST = lax.Precision.HIGHEST
LOG2E = 1.4426950408889634
SCALE = HD**-0.5
VMEM_CAP = 56 * 1024 * 1024
ALL = ("row", "zh", "zl", "core")

NN = (((1,), (0,)), ((), ()))
NT = (((1,), (1,)), ((), ()))
TN = (((0,), (0,)), ((), ()))


def dot(a, b, dims, precision=None):
    return lax.dot_general(a, b, dims, precision=precision, preferred_element_type=F32)


def params():
    return pltpu.CompilerParams(vmem_limit_bytes=VMEM_CAP)


def cost(flops, arrays, extra=0):
    moved = sum(int(a.size) * a.dtype.itemsize for a in arrays)
    return pl.CostEstimate(flops=int(flops), bytes_accessed=int(moved), transcendentals=int(extra))


def sds(shape, dtype):
    return jax.ShapeDtypeStruct(shape, dtype)


def mix_stream(stack_ref, coeffs, s, rows):
    total = None
    for j in range(8):
        term = coeffs[:, 8 * s + j : 8 * s + j + 1] * stack_ref[j, rows, :].astype(F32)
        total = term if total is None else total + term
    return total


def centre(values):
    centred = values - jnp.mean(values, axis=-1, keepdims=True)
    spread = jnp.mean(centred * centred, axis=-1, keepdims=True)
    return centred, lax.rsqrt(spread + EPS_LAYER)


def front_kernel(stack_ref, mix_ref, gain_ref, bias_ref, q_ref, k_ref, v_ref, res_ref):
    chunk = 16

    def step(i, carry):
        rows = pl.ds(pl.multiple_of(i * chunk, chunk), chunk)
        coeffs = mix_ref[rows, :]
        for s, out_ref in enumerate((q_ref, k_ref, v_ref)):
            centred, rstd = centre(mix_stream(stack_ref, coeffs, s, rows))
            out_ref[rows, :] = (
                centred * rstd * gain_ref[s : s + 1, :] + bias_ref[s : s + 1, :]
            ).astype(BF)
        res_ref[rows, :] = mix_stream(stack_ref, coeffs, 3, rows)
        return carry

    lax.fori_loop(0, stack_ref.shape[1] // chunk, step, 0)


def front(stack, mix, gain, bias):
    n_in, tokens, width = stack.shape
    tile = 64
    row_block = lambda i: (i, 0)
    outs = [sds((tokens, width), BF)] * 3 + [sds((tokens, width), F32)]
    return pl.pallas_call(
        front_kernel,
        grid=(tokens // tile,),
        in_specs=[
            pl.BlockSpec((n_in, tile, width), lambda i: (0, i, 0)),
            pl.BlockSpec((tile, mix.shape[1]), row_block),
            pl.BlockSpec(gain.shape, lambda i: (0, 0)),
            pl.BlockSpec(bias.shape, lambda i: (0, 0)),
        ],
        out_specs=[pl.BlockSpec((tile, width), row_block)] * 4,
        out_shape=outs,
        compiler_params=params(),
        cost_estimate=cost(70 * tokens * width, [stack, *outs]),
        name="front",
    )(stack, mix, gain, bias)


def front_back_kernel(pieces, *refs):
    grads = [refs[s * pieces : (s + 1) * pieces] for s in range(3)]
    hid_ref, stack_ref, mix_ref, gain_ref = refs[3 * pieces : 3 * pieces + 4]
    stack_out, coeff_out, gain_out, bias_out, held = refs[3 * pieces + 4 :]
    chunk = 16
    width = hid_ref.shape[1]

    @pl.when(pl.program_id(0) == 0)
    def _():
        gain_out[...] = jnp.zeros_like(gain_out)
        bias_out[...] = jnp.zeros_like(bias_out)

    def step(i, carry):
        rows = pl.ds(pl.multiple_of(i * chunk, chunk), chunk)
        coeffs = mix_ref[rows, :]
        for s in range(3):
            centred, rstd = centre(mix_stream(stack_ref, coeffs, s, rows))
            hat = centred * rstd
            grad = grads[s][0][rows, :].astype(F32)
            for piece in grads[s][1:]:
                grad = grad + piece[rows, :].astype(F32)
            grad = grad.astype(BF).astype(F32)
            gain_out[8 * s : 8 * s + 8, :] += jnp.sum(
                (grad * hat).reshape(chunk // 8, 8, width), axis=0
            )
            bias_out[8 * s : 8 * s + 8, :] += jnp.sum(grad.reshape(chunk // 8, 8, width), axis=0)
            scaled = grad * gain_ref[s : s + 1, :]
            held[s] = rstd * (
                scaled
                - jnp.mean(scaled, axis=-1, keepdims=True)
                - hat * jnp.mean(scaled * hat, axis=-1, keepdims=True)
            )
        held[3] = hid_ref[rows, :]
        lanes = lax.broadcasted_iota(jnp.int32, (chunk, mix_ref.shape[1]), 1)
        gathered = jnp.zeros((chunk, mix_ref.shape[1]), F32)
        for j in range(8):
            given = stack_ref[j, rows, :].astype(F32)
            total = None
            for s in range(4):
                grad = held[s]
                term = coeffs[:, 8 * s + j : 8 * s + j + 1] * grad
                total = term if total is None else total + term
                inner = jnp.sum(grad * given, axis=-1, keepdims=True)
                gathered = jnp.where(lanes == 8 * s + j, inner, gathered)
            stack_out[j, rows, :] = total
        coeff_out[rows, :] = gathered
        return carry

    lax.fori_loop(0, hid_ref.shape[0] // chunk, step, 0)


def front_back(grad_pieces, grad_hidden, stack, mix, gain):
    n_in, tokens, width = stack.shape
    tile = 32
    pieces = len(grad_pieces[0])
    row_block = lambda i: (i, 0)
    fixed = lambda i: (0, 0)
    outs = [
        sds(stack.shape, F32),
        sds(mix.shape, F32),
        sds((24, width), F32),
        sds((24, width), F32),
    ]
    flat = [piece for group in grad_pieces for piece in group]
    return pl.pallas_call(
        functools.partial(front_back_kernel, pieces),
        grid=(tokens // tile,),
        in_specs=[pl.BlockSpec((tile, width), row_block)] * (3 * pieces + 1)
        + [
            pl.BlockSpec((n_in, tile, width), lambda i: (0, i, 0)),
            pl.BlockSpec((tile, mix.shape[1]), row_block),
            pl.BlockSpec(gain.shape, fixed),
        ],
        out_specs=[
            pl.BlockSpec((n_in, tile, width), lambda i: (0, i, 0)),
            pl.BlockSpec((tile, mix.shape[1]), row_block),
            pl.BlockSpec((24, width), fixed),
            pl.BlockSpec((24, width), fixed),
        ],
        out_shape=outs,
        scratch_shapes=[pltpu.VMEM((4, 16, width), F32)],
        compiler_params=params(),
        cost_estimate=cost(250 * tokens * width, [stack, grad_hidden, *flat, *outs]),
        name="front_back",
    )(*flat, grad_hidden, stack, mix, gain)


def turn(values, cos_table, sine_table):
    lanes = lax.broadcasted_iota(jnp.int32, values.shape, 1)
    half = ROT // 2
    swapped = jnp.where(
        lanes < half, pltpu.roll(values, HD - half, 1), pltpu.roll(values, half, 1)
    )
    return values * cos_table + swapped * sine_table


def proj_kernel(blocks, rotary, *refs):
    x_refs = refs[:blocks]
    if rotary:
        weight_ref, bias_ref, cos_ref, sine_ref, out_ref = refs[blocks:]
    else:
        weight_ref, bias_ref, out_ref = refs[blocks:]
    rows = x_refs[0].shape[0]
    for b, x_ref in enumerate(x_refs):
        here = slice(b * rows, (b + 1) * rows)
        total = dot(x_ref[...], weight_ref[...], NN) + bias_ref[...]
        if not rotary:
            out_ref[here, :] = total.astype(BF)
            continue
        for h in range(total.shape[1] // HD):
            heads = slice(h * HD, (h + 1) * HD)
            out_ref[here, heads] = turn(
                total[:, heads], cos_ref[here, :], sine_ref[here, :]
            ).astype(BF)


def proj(x_blocks, weight, part, bias, tables=None):
    blocks = len(x_blocks)
    rows, width = x_blocks[0].shape
    cols = bias.shape[1]
    out = sds((blocks * rows, cols), BF)
    whole = lambda a: pl.BlockSpec(a.shape, lambda i: (0, 0))
    rest = [bias] + list(tables or ())
    return pl.pallas_call(
        functools.partial(proj_kernel, blocks, tables is not None),
        grid=(1,),
        in_specs=[whole(x) for x in x_blocks]
        + [pl.BlockSpec((width, cols), lambda i: (0, part))]
        + [whole(a) for a in rest],
        out_specs=whole(out),
        out_shape=out,
        compiler_params=params(),
        cost_estimate=cost(2 * blocks * rows * width * cols, [*x_blocks, bias, out]),
        name="proj",
    )(*x_blocks, weight, *rest)


def unproj_kernel(halves, *refs):
    a_refs, weight_refs, outs = refs[:halves], refs[halves : 2 * halves], refs[2 * halves :]
    rows = outs[0].shape[0]
    for b, out_ref in enumerate(outs):
        total = None
        for a_ref, weight_ref in zip(a_refs, weight_refs):
            term = dot(a_ref[b * rows : (b + 1) * rows, :], weight_ref[...], NT)
            total = term if total is None else total + term
        out_ref[...] = total.astype(BF)


def unproj(parts, weights, part, blocks):
    halves = len(parts)
    tokens, cols = parts[0].shape
    width = weights[0].shape[0]
    tile = min(width, 512)
    outs = [sds((tokens // blocks, width), BF)] * blocks
    return pl.pallas_call(
        functools.partial(unproj_kernel, halves),
        grid=(width // tile,),
        in_specs=[pl.BlockSpec((tokens, cols), lambda i: (0, 0))] * halves
        + [pl.BlockSpec((tile, cols), lambda i: (i, part))] * halves,
        out_specs=[pl.BlockSpec((tokens // blocks, tile), lambda i: (0, i))] * blocks,
        out_shape=outs,
        compiler_params=params(),
        cost_estimate=cost(2 * halves * tokens * cols * width, [*parts, *outs]),
        name="unproj",
    )(*parts, *weights)


def masked_scores(scalars, keys, query, block, blocks):
    rows = query.shape[0]
    raw = dot(keys, query, NT)
    lanes = lax.broadcasted_iota(jnp.int32, (1, rows), 1)
    limit = jnp.maximum(lanes + scalars[block], scalars[blocks] - 1)
    places = lax.broadcasted_iota(jnp.int32, (rows, rows), 0)
    kept = []
    for b in range(blocks):
        allowed = places <= limit - scalars[b]
        kept.append(jnp.where(allowed, raw[b * rows : (b + 1) * rows, :], -1e30))
    return jnp.concatenate(kept, axis=0)


def attend_kernel(blocks, scalars, q_ref, k_ref, v_ref, out_ref, log_ref):
    rows = q_ref.shape[0] // blocks
    factor = SCALE * LOG2E
    for b in range(blocks):
        here = slice(b * rows, (b + 1) * rows)
        scores = masked_scores(scalars, k_ref[...], q_ref[here, :], b, blocks)
        top = jnp.max(scores, axis=0, keepdims=True)
        probs = jnp.exp2((scores - top) * factor)
        total = jnp.sum(probs, axis=0, keepdims=True)
        mixed = dot(v_ref[...], probs.astype(BF), TN) / total
        out_ref[here, :] = mixed.T.astype(BF)
        log_ref[0, :, here] = top * factor + jnp.log2(total)


def attend(scalars, query, key, value, blocks):
    tokens, cols = query.shape
    heads = cols // HD
    head_block = pl.BlockSpec((tokens, HD), lambda h: (0, h))
    outs = [sds((tokens, cols), BF), sds((heads, 1, tokens), F32)]
    return pl.pallas_call(
        functools.partial(attend_kernel, blocks),
        grid=(heads,),
        in_specs=[pl.BlockSpec(memory_space=pltpu.SMEM)] + [head_block] * 3,
        out_specs=[head_block, pl.BlockSpec((1, 1, tokens), lambda h: (h, 0, 0))],
        out_shape=outs,
        compiler_params=params(),
        cost_estimate=cost(8 * heads * tokens * tokens * HD, [query, key, value, *outs]),
        name="attend",
    )(scalars, query, key, value)


def attend_back_kernel(
    blocks, scalars, q_ref, k_ref, v_ref, g_ref, log_ref, cos_ref, sine_ref,
    gq_ref, gk_ref, gv_ref, sums_ref, key_acc, value_acc,
):
    rows = q_ref.shape[0] // blocks
    factor = SCALE * LOG2E
    sums = []
    query_sum = jnp.zeros((1, HD), F32)
    for b in range(blocks):
        here = slice(b * rows, (b + 1) * rows)
        query, grad = q_ref[here, :], g_ref[here, :]
        scores = masked_scores(scalars, k_ref[...], query, b, blocks)
        probs = jnp.exp2(scores * factor - log_ref[0, :, here])
        grad_probs = dot(v_ref[...], grad, NT)
        inner = jnp.sum(probs * grad_probs, axis=0, keepdims=True)
        grad_scores = (probs * (grad_probs - inner)).astype(BF)
        key_term = dot(grad_scores, query, NN)
        value_term = dot(probs.astype(BF), grad, NN)
        if b == 0:
            key_acc[...] = key_term
            value_acc[...] = value_term
        else:
            key_acc[...] += key_term
            value_acc[...] += value_term
        grad_query = dot(k_ref[...], grad_scores, TN).T * SCALE
        low = turn(grad_query, cos_ref[here, :], -sine_ref[here, :]).astype(BF)
        gq_ref[here, :] = low
        query_sum = query_sum + jnp.sum(low.astype(F32), axis=0, keepdims=True)
    low_key = turn(key_acc[...] * SCALE, cos_ref[...], -sine_ref[...]).astype(BF)
    gk_ref[...] = low_key
    low_value = value_acc[...].astype(BF)
    gv_ref[...] = low_value
    sums_ref[0, 0:1, :] = query_sum
    sums_ref[0, 1:2, :] = jnp.sum(low_key.astype(F32), axis=0, keepdims=True)
    sums_ref[0, 2:3, :] = jnp.sum(low_value.astype(F32), axis=0, keepdims=True)


def attend_back(scalars, query, key, value, grad, log_total, tables, blocks):
    tokens, cols = query.shape
    heads = cols // HD
    head_block = pl.BlockSpec((tokens, HD), lambda h: (0, h))
    fixed = pl.BlockSpec((tokens, HD), lambda h: (0, 0))
    outs = [sds((tokens, cols), BF)] * 3 + [sds((heads, 8, HD), F32)]
    return pl.pallas_call(
        functools.partial(attend_back_kernel, blocks),
        grid=(heads,),
        in_specs=[pl.BlockSpec(memory_space=pltpu.SMEM)]
        + [head_block] * 4
        + [pl.BlockSpec((1, 1, tokens), lambda h: (h, 0, 0)), fixed, fixed],
        out_specs=[head_block] * 3 + [pl.BlockSpec((1, 8, HD), lambda h: (h, 0, 0))],
        out_shape=outs,
        scratch_shapes=[pltpu.VMEM((tokens, HD), F32)] * 2,
        compiler_params=params(),
        cost_estimate=cost(16 * heads * tokens * tokens * HD, [query, key, value, grad, *outs]),
        name="attend_back",
    )(scalars, query, key, value, grad, log_total, *tables)


def total_of(refs, rows=slice(None)):
    total = refs[0][rows, :].astype(F32)
    for ref in refs[1:]:
        total = total + ref[rows, :].astype(F32)
    return total


def middle_kernel(pieces, *refs):
    parts = refs[:pieces]
    res_ref, out_bias_ref, gain_ref, bias_ref, hid_ref, norm_ref = refs[pieces:]
    attn = (total_of(parts) + out_bias_ref[...]).astype(BF)
    hidden = res_ref[...] + attn.astype(F32)
    hid_ref[...] = hidden
    centred, rstd = centre(hidden)
    norm_ref[...] = (centred * rstd * gain_ref[3:4, :] + bias_ref[3:4, :]).astype(BF)


def middle(parts, residual, out_bias, gain, bias):
    tokens, width = residual.shape
    tile = 64
    block = pl.BlockSpec((tile, width), lambda i: (i, 0))
    whole = lambda a: pl.BlockSpec(a.shape, lambda i: (0, 0))
    outs = [sds((tokens, width), F32), sds((tokens, width), BF)]
    return pl.pallas_call(
        functools.partial(middle_kernel, len(parts)),
        grid=(tokens // tile,),
        in_specs=[block] * (len(parts) + 1) + [whole(out_bias), whole(gain), whole(bias)],
        out_specs=[block] * 2,
        out_shape=outs,
        compiler_params=params(),
        cost_estimate=cost(20 * tokens * width, [*parts, residual, *outs]),
        name="middle",
    )(*parts, residual, out_bias, gain, bias)


def middle_back_kernel(pieces, *refs):
    parts = refs[:pieces]
    hid_ref, layer_ref, gain_ref = refs[pieces : pieces + 3]
    grad_ref, low_ref, sums_ref = refs[pieces + 3 :]
    grad = total_of(parts).astype(BF).astype(F32)
    centred, rstd = centre(hid_ref[...])
    hat = centred * rstd
    scaled = grad * gain_ref[3:4, :]
    grad_hidden = layer_ref[...] + rstd * (
        scaled
        - jnp.mean(scaled, axis=-1, keepdims=True)
        - hat * jnp.mean(scaled * hat, axis=-1, keepdims=True)
    )
    grad_ref[...] = grad_hidden
    low = grad_hidden.astype(BF)
    low_ref[...] = low

    @pl.when(pl.program_id(0) == 0)
    def _():
        sums_ref[...] = jnp.zeros_like(sums_ref)

    sums_ref[0:1, :] += jnp.sum(grad * hat, axis=0, keepdims=True)
    sums_ref[1:2, :] += jnp.sum(grad, axis=0, keepdims=True)
    sums_ref[2:3, :] += jnp.sum(low.astype(F32), axis=0, keepdims=True)


def middle_back(parts, hidden, grad_layer, gain):
    tokens, width = hidden.shape
    tile = 64
    block = pl.BlockSpec((tile, width), lambda i: (i, 0))
    outs = [sds((tokens, width), F32), sds((tokens, width), BF), sds((8, width), F32)]
    return pl.pallas_call(
        functools.partial(middle_back_kernel, len(parts)),
        grid=(tokens // tile,),
        in_specs=[block] * (len(parts) + 2) + [pl.BlockSpec(gain.shape, lambda i: (0, 0))],
        out_specs=[block] * 2 + [pl.BlockSpec((8, width), lambda i: (0, 0))],
        out_shape=outs,
        compiler_params=params(),
        cost_estimate=cost(30 * tokens * width, [*parts, hidden, grad_layer, *outs]),
        name="middle_back",
    )(*parts, hidden, grad_layer, gain)


def gelu_pair(values):
    tail = 0.5 * (1.0 + lax.erf(values * (0.5**0.5)))
    slope = tail + values * jnp.exp2(values * values * (-0.5 * LOG2E)) * 0.3989422804014327
    return values * tail, slope


def feed_kernel(blocks, back, *refs):
    x_refs = refs[:blocks]
    if back:
        first_ref, second_ref, slope_ref = refs[blocks : blocks + 3]
        act_ref, sums_ref = refs[blocks + 3 : blocks + 5]
    else:
        first_ref, second_ref, bias_ref = refs[blocks : blocks + 3]
        act_ref, slope_ref = refs[blocks + 3 : blocks + 5]
    outs = refs[blocks + 5 : 2 * blocks + 5]
    acc = refs[2 * blocks + 5]
    rows = x_refs[0].shape[0]
    step, last = pl.program_id(0), pl.num_programs(0) - 1
    total = None
    for b, x_ref in enumerate(x_refs):
        here = slice(b * rows, (b + 1) * rows)
        up = dot(x_ref[...], first_ref[...], NN)
        if back:
            low = (up * slope_ref[here, :].astype(F32)).astype(BF)
            part = jnp.sum(low.astype(F32), axis=0, keepdims=True)
            total = part if total is None else total + part
        else:
            act, slope = gelu_pair(up + bias_ref[...])
            low = act.astype(BF)
            slope_ref[here, :] = slope.astype(BF)
        act_ref[here, :] = low
        term = dot(low, second_ref[...], NT)

        @pl.when(step == 0)
        def _():
            acc[here, :] = term

        @pl.when(step > 0)
        def _():
            acc[here, :] += term

    if back:
        sums_ref[...] = total

    @pl.when(step == last)
    def _():
        for b, out_ref in enumerate(outs):
            out_ref[...] = acc[b * rows : (b + 1) * rows, :].astype(BF)


def feed(x_blocks, first, second, extra, back):
    blocks = len(x_blocks)
    rows, width = x_blocks[0].shape
    tokens = blocks * rows
    hidden = first.shape[1]
    tile = 256
    whole = pl.BlockSpec((rows, width), lambda i: (0, 0))
    weight = pl.BlockSpec((width, tile), lambda i: (0, i))
    line = pl.BlockSpec((1, tile), lambda i: (0, i))
    column = pl.BlockSpec((tokens, tile), lambda i: (0, i))
    outs = [
        sds((tokens, hidden), BF),
        sds((1, hidden), F32) if back else sds((tokens, hidden), BF),
    ] + [sds((rows, width), BF)] * blocks
    return pl.pallas_call(
        functools.partial(feed_kernel, blocks, back),
        grid=(hidden // tile,),
        in_specs=[whole] * blocks + [weight, weight, column if back else line],
        out_specs=[column, line if back else column] + [whole] * blocks,
        out_shape=outs,
        scratch_shapes=[pltpu.VMEM((tokens, width), F32)],
        compiler_params=params(),
        cost_estimate=cost(4 * tokens * width * hidden, [*x_blocks, first, second, extra, *outs]),
        name="feed_back" if back else "feed",
    )(*x_blocks, first, second, extra)


def mixing_kernel(pieces, *refs):
    parts = refs[:pieces]
    hid_ref, down_bias_ref, gain_ref, in_ref, out_w_ref, og_ref, cg_ref = refs[
        pieces : pieces + 7
    ]
    layer_ref, coeff_ref, grad_ref, low_ref, sums_ref, in_grad_ref, out_grad_ref = refs[
        pieces + 7 :
    ]
    down = (total_of(parts) + down_bias_ref[...]).astype(BF)
    layer = hid_ref[...] + down.astype(F32)
    layer_ref[...] = layer
    rms = lax.rsqrt(jnp.mean(layer * layer, axis=-1, keepdims=True) + EPS_RMS)
    unit = layer * rms
    gain = gain_ref[...]
    scaled = unit * gain
    act, slope = gelu_pair(dot(scaled, in_ref[...], NN, FINEST))
    coeff_ref[...] = dot(act, out_w_ref[...], NN, FINEST)
    coeff_grad = cg_ref[...]
    grad_pre = dot(coeff_grad, out_w_ref[...], NT, FINEST) * slope
    grad_scaled = dot(grad_pre, in_ref[...], NT, FINEST)
    grad_unit = grad_scaled * gain
    grad_layer = (
        rms * (grad_unit - unit * jnp.mean(grad_unit * unit, axis=-1, keepdims=True))
        + og_ref[...].astype(F32)
    )
    grad_ref[...] = grad_layer
    low = grad_layer.astype(BF)
    low_ref[...] = low

    @pl.when(pl.program_id(0) == 0)
    def _():
        sums_ref[...] = jnp.zeros_like(sums_ref)
        in_grad_ref[...] = jnp.zeros_like(in_grad_ref)
        out_grad_ref[...] = jnp.zeros_like(out_grad_ref)

    sums_ref[0:1, :] += jnp.sum(low.astype(F32), axis=0, keepdims=True)
    sums_ref[1:2, :] += jnp.sum(grad_scaled * unit, axis=0, keepdims=True)
    in_grad_ref[...] += dot(grad_pre, scaled, TN, FINEST)
    out_grad_ref[...] += dot(act, coeff_grad, TN, FINEST)


def mixing(parts, hidden, down_bias, gain, mix_in, mix_out, out_grad, coeff_grad):
    tokens, width = hidden.shape
    tile = 128
    block = pl.BlockSpec((tile, width), lambda i: (i, 0))
    whole = lambda a: pl.BlockSpec(a.shape, lambda i: (0, 0))
    narrow = pl.BlockSpec((tile, coeff_grad.shape[1]), lambda i: (i, 0))
    outs = [
        sds((tokens, width), F32),
        sds(coeff_grad.shape, F32),
        sds((tokens, width), F32),
        sds((tokens, width), BF),
        sds((8, width), F32),
        sds((mix_in.shape[1], width), F32),
        sds(mix_out.shape, F32),
    ]
    return pl.pallas_call(
        functools.partial(mixing_kernel, len(parts)),
        grid=(tokens // tile,),
        in_specs=[block] * (len(parts) + 1)
        + [whole(a) for a in (down_bias, gain, mix_in, mix_out)]
        + [block, narrow],
        out_specs=[block, narrow, block, block] + [whole(a) for a in outs[4:]],
        out_shape=outs,
        compiler_params=params(),
        cost_estimate=cost(3000 * tokens * width, [*parts, hidden, out_grad, *outs]),
        name="mixing",
    )(*parts, hidden, down_bias, gain, mix_in, mix_out, out_grad, coeff_grad)


def swap(values, axis, bits):
    size = lax.axis_size(axis)
    return lax.ppermute(values, axis, [(i, i ^ bits) for i in range(size)])


def gather_tokens(values):
    blocks = []
    for k in range(lax.axis_size("zl")):
        held = swap(values, "zl", k) if k else values
        blocks += [held, swap(held, "core", 1)]
    return blocks


def scatter_tokens(blocks):
    terms = [blocks[0], swap(blocks[1], "core", 1)]
    for k in range(1, lax.axis_size("zl")):
        other = swap(blocks[2 * k + 1], "core", 1)
        chip_sum = (blocks[2 * k].astype(F32) + other.astype(F32)).astype(BF)
        terms.append(swap(chip_sum, "zl", k))
    return terms


def halves_of(values):
    return [values] + [swap(values, "zh", h) for h in range(1, lax.axis_size("zh"))]


def sum_everywhere(values):
    for axis in ("core", "zl", "row", "zh"):
        bit = 1
        while bit < lax.axis_size(axis):
            values = values + swap(values, axis, bit)
            bit *= 2
    return values


def sum_groups(values, axes):
    for axis in axes:
        bit = 1
        while bit < lax.axis_size(axis):
            values = values + swap(values, axis, bit)
            bit *= 2
    return values


def gather_weight(values):
    return lax.all_gather(values, "row", axis=0, tiled=True)


def scatter_weight(grad, halves):
    mine = lax.psum_scatter(grad, "row", scatter_dimension=0, tiled=True)
    cols = grad.shape[1] // halves
    total = mine[:, :cols].astype(F32)
    for h in range(1, halves):
        total = total + swap(mine[:, h * cols : (h + 1) * cols], "zh", h).astype(F32)
    return total


def on_device(
    layer_stack, mix_coeffs, prefix, ln_gain, ln_bias, qkv_weight, qkv_bias, out_weight,
    out_bias, up_weight, up_bias, down_weight, down_bias, mix_gain, mix_in, mix_out, out_grad,
    coeff_grad,
):
    tokens, width = layer_stack.shape[1:]
    halves = lax.axis_size("zh")
    group = lax.axis_size("zl") * 2
    cols = qkv_bias.shape[1]
    feats = qkv_weight.shape[1]
    place = lax.axis_index("zl") * 2 + lax.axis_index("core")

    attn_local = jnp.concatenate(
        [qkv_weight[s] for s in range(3)] + [out_weight.T], axis=1
    )
    attn_halves = halves_of(attn_local)
    up_local = jnp.concatenate(halves_of(up_weight), axis=1)
    down_local = jnp.concatenate(halves_of(down_weight.T), axis=1)
    attn_full = [gather_weight(w) for w in attn_halves]
    up_full = gather_weight(up_local)
    down_full = gather_weight(down_local)
    qkv_biases = halves_of(qkv_bias)
    up_bias_full = jnp.concatenate(halves_of(up_bias.reshape(1, -1)), axis=1)

    bases = (place ^ jnp.arange(group, dtype=jnp.int32)) * tokens
    prefix_here = lax.dynamic_slice_in_dim(prefix, lax.axis_index("zh"), 1, 0)
    scalars = jnp.concatenate([bases, prefix_here])
    positions = (bases[:, None] + jnp.arange(tokens, dtype=jnp.int32)[None, :]).reshape(-1)
    inv_freq = 10000.0 ** (-(jnp.arange(ROT // 2, dtype=F32) * 2.0) / ROT)
    angles = positions.astype(F32)[:, None] * inv_freq[None, :]
    cos_half, sine_half = jnp.cos(angles), jnp.sin(angles)
    rest = jnp.zeros((positions.shape[0], HD - ROT), F32)
    tables = (
        jnp.concatenate([cos_half, cos_half, rest + 1.0], axis=1),
        jnp.concatenate([-sine_half, sine_half, rest], axis=1),
    )

    mix_flat = mix_coeffs.reshape(tokens, -1)
    *normed, residual = front(layer_stack, mix_flat, ln_gain, ln_bias)
    normed_all = [gather_tokens(n) for n in normed]
    q, k, v, head, log_total = [], [], [], [], []
    for h in range(halves):
        bias = [qkv_biases[h][s : s + 1] for s in range(3)]
        q.append(proj(normed_all[0], attn_full[h], 0, bias[0], tables))
        k.append(proj(normed_all[1], attn_full[h], 1, bias[1], tables))
        v.append(proj(normed_all[2], attn_full[h], 2, bias[2]))
        out, log = attend(scalars, q[h], k[h], v[h], group)
        head.append(out)
        log_total.append(log)
    attn_terms = scatter_tokens(unproj(head, attn_full, 3, group))
    hidden, normed2 = middle(attn_terms, residual, out_bias.reshape(1, -1), ln_gain, ln_bias)
    normed2_all = gather_tokens(normed2)
    act, slope, *down_parts = feed(normed2_all, up_full, down_full, up_bias_full, False)
    down_terms = scatter_tokens(down_parts)
    layer_out, coeff_out, grad_layer, grad_down, mix_sums, mix_in_part, mix_out_part = mixing(
        down_terms, hidden, down_bias.reshape(1, -1), mix_gain.reshape(1, -1), mix_in, mix_out,
        out_grad, coeff_grad,
    )

    grad_down_all = gather_tokens(grad_down)
    grad_up, up_bias_part, *norm2_parts = feed(grad_down_all, down_full, up_full, slope, True)
    down_grad = scatter_weight(
        dot(jnp.concatenate(grad_down_all, axis=0), act, TN).astype(BF), halves
    ).T
    norm2_terms = scatter_tokens(norm2_parts)
    up_grad = scatter_weight(
        dot(jnp.concatenate(normed2_all, axis=0), grad_up, TN).astype(BF), halves
    )
    grad_hidden, grad_attn, mid_sums = middle_back(norm2_terms, hidden, grad_layer, ln_gain)
    grad_attn_all = gather_tokens(grad_attn)
    no_bias = jnp.zeros((1, cols), F32)
    grads = [[], [], []]
    bias_sums = []
    for h in range(halves):
        grad_heads = proj(grad_attn_all, attn_full[h], 3, no_bias)
        *parts, sums = attend_back(
            scalars, q[h], k[h], v[h], grad_heads, log_total[h], tables, group
        )
        for s in range(3):
            grads[s].append(parts[s])
        bias_sums.append(sums[:, :3].transpose(1, 0, 2).reshape(3, cols))
    norm_terms = [scatter_tokens(unproj(grads[s], attn_full, s, group)) for s in range(3)]
    grad_attn_cat = jnp.concatenate(grad_attn_all, axis=0)
    wide = [
        dot(jnp.concatenate(normed_all[s], axis=0), jnp.concatenate(grads[s], axis=1), TN)
        for s in range(3)
    ] + [dot(grad_attn_cat, jnp.concatenate(head, axis=1), TN)]
    attn_grad = scatter_weight(
        jnp.concatenate(
            [w[:, h * cols : (h + 1) * cols] for h in range(halves) for w in wide], axis=1
        ).astype(BF),
        halves,
    )
    qkv_grad = attn_grad[:, : 3 * cols].reshape(feats, 3, cols).transpose(1, 0, 2)
    out_w_grad = attn_grad[:, 3 * cols :].T
    stack_grad, coeffs_grad, gain_part, bias_part = front_back(
        norm_terms, grad_hidden, layer_stack, mix_flat, ln_gain
    )

    up_half = up_bias.shape[0]
    up_bias_grad = up_bias_part[0, :up_half]
    qkv_bias_grad = bias_sums[0]
    for h in range(1, halves):
        up_bias_grad = up_bias_grad + swap(
            up_bias_part[0, h * up_half : (h + 1) * up_half], "zh", h
        )
        qkv_bias_grad = qkv_bias_grad + swap(bias_sums[h], "zh", h)
    up_bias_grad = sum_groups(up_bias_grad, ("row",))
    qkv_bias_grad = sum_groups(qkv_bias_grad, ("row",))
    early = sum_everywhere(jnp.concatenate([mix_in_part, mix_sums[:2]], axis=0))
    mix_in_grad = early[: mix_in_part.shape[0]].T
    down_bias_grad, mix_gain_grad = early[-2], early[-1]
    mix_out_grad = sum_everywhere(mix_out_part)
    late = sum_everywhere(
        jnp.concatenate(
            [
                gain_part.reshape(3, 8, width).sum(axis=1),
                mid_sums[0:1],
                bias_part.reshape(3, 8, width).sum(axis=1),
                mid_sums[1:3],
            ],
            axis=0,
        )
    )
    return (
        layer_out,
        coeff_out,
        stack_grad,
        coeffs_grad.reshape(mix_coeffs.shape),
        late[0:4],
        late[4:8],
        qkv_grad,
        qkv_bias_grad,
        out_w_grad,
        late[8],
        up_grad,
        up_bias_grad,
        down_grad,
        down_bias_grad,
        mix_gain_grad,
        mix_in_grad,
        mix_out_grad,
    )


def solution(mesh):
    rows, cols = mesh.shape["row"], mesh.shape["col"]
    col = ("zh", "zl", "core")

    def run(*args):
        seqs = args[2].shape[0] // rows
        fine = Mesh(mesh.devices.reshape(rows, seqs, cols // (2 * seqs), 2), ALL)
        in_specs = (
            P(None, ALL, None),
            P(ALL, None, None),
            P("row"),
            P(),
            P(),
            P(None, "row", col),
            P(None, col),
            P(col, "row"),
            P(),
            P("row", col),
            P(col),
            P(col, "row"),
            P(),
            P(),
            P(),
            P(),
            P(ALL, None),
            P(ALL, None),
        )
        out_specs = (
            P(ALL, None),
            P(ALL, None),
            P(None, ALL, None),
            P(ALL, None, None),
            P(),
            P(),
            P(None, "row", col),
            P(None, col),
            P(col, "row"),
            P(),
            P("row", col),
            P(col),
            P(col, "row"),
            P(),
            P(),
            P(),
            P(),
        )
        return jax.shard_map(
            on_device, mesh=fine, in_specs=in_specs, out_specs=out_specs, check_vma=False
        )(*args)

    return run
```

```python
import functools

import jax
import jax.numpy as jnp
from jax import lax
from jax.experimental import pallas as pl
from jax.experimental.pallas import tpu as pltpu
from jax.sharding import Mesh, PartitionSpec as P

HD = 128
ROT = 32
LEN = 1024
EPS_LAYER = 1e-05
EPS_RMS = 1e-06
BF = jnp.bfloat16
F32 = jnp.float32
FINEST = lax.Precision.HIGHEST
LOG2E = 1.4426950408889634
SCALE = HD**-0.5
VMEM_CAP = 56 * 1024 * 1024
ALL = ("row", "zh", "zl", "core")

NN = (((1,), (0,)), ((), ()))
NT = (((1,), (1,)), ((), ()))
TN = (((0,), (0,)), ((), ()))


def dot(a, b, dims, precision=None):
    return lax.dot_general(a, b, dims, precision=precision, preferred_element_type=F32)


def params():
    return pltpu.CompilerParams(vmem_limit_bytes=VMEM_CAP)


def cost(flops, arrays, extra=0):
    moved = sum(int(a.size) * a.dtype.itemsize for a in arrays)
    return pl.CostEstimate(flops=int(flops), bytes_accessed=int(moved), transcendentals=int(extra))


def sds(shape, dtype):
    return jax.ShapeDtypeStruct(shape, dtype)


def mix_stream(stack_ref, coeffs, s, rows):
    total = None
    for j in range(8):
        term = coeffs[:, 8 * s + j : 8 * s + j + 1] * stack_ref[j, rows, :].astype(F32)
        total = term if total is None else total + term
    return total


def centre(values):
    centred = values - jnp.mean(values, axis=-1, keepdims=True)
    spread = jnp.mean(centred * centred, axis=-1, keepdims=True)
    return centred, lax.rsqrt(spread + EPS_LAYER)


def front_kernel(stack_ref, mix_ref, gain_ref, bias_ref, first_ref, rest_ref, res_ref):
    chunk = 16

    def step(i, carry):
        rows = pl.ds(pl.multiple_of(i * chunk, chunk), chunk)
        coeffs = mix_ref[rows, :]
        for s in range(3):
            centred, rstd = centre(mix_stream(stack_ref, coeffs, s, rows))
            normed = centred * rstd * gain_ref[s : s + 1, :] + bias_ref[s : s + 1, :]
            if s == 0:
                first_ref[0, rows, :] = normed.astype(BF)
            else:
                rest_ref[s - 1, rows, :] = normed.astype(BF)
        res_ref[rows, :] = mix_stream(stack_ref, coeffs, 3, rows)
        return carry

    lax.fori_loop(0, stack_ref.shape[1] // chunk, step, 0)


def front(stack, mix, gain, bias):
    n_in, tokens, width = stack.shape
    tile = 32
    row_block = lambda i: (i, 0)
    outs = [sds((n, tokens, width), BF) for n in (1, 2)] + [sds((tokens, width), F32)]
    return pl.pallas_call(
        front_kernel,
        grid=(tokens // tile,),
        in_specs=[
            pl.BlockSpec((n_in, tile, width), lambda i: (0, i, 0)),
            pl.BlockSpec((tile, mix.shape[1]), row_block),
            pl.BlockSpec(gain.shape, lambda i: (0, 0)),
            pl.BlockSpec(bias.shape, lambda i: (0, 0)),
        ],
        out_specs=[
            pl.BlockSpec((1, tile, width), lambda i: (0, i, 0)),
            pl.BlockSpec((2, tile, width), lambda i: (0, i, 0)),
            pl.BlockSpec((tile, width), row_block),
        ],
        out_shape=outs,
        compiler_params=params(),
        cost_estimate=cost(70 * tokens * width, [stack, *outs]),
        name="front",
    )(stack, mix, gain, bias)


def norm_back_kernel(streams, pieces, *refs):
    parts = refs[:pieces]
    stack_ref, mix_ref, gain_ref, grad_ref, sums_ref = refs[pieces:]
    chunk = 16
    width = grad_ref.shape[2]

    @pl.when(pl.program_id(0) == 0)
    def _():
        sums_ref[...] = jnp.zeros_like(sums_ref)

    def step(i, carry):
        rows = pl.ds(pl.multiple_of(i * chunk, chunk), chunk)
        coeffs = mix_ref[rows, :]
        for n, s in enumerate(streams):
            centred, rstd = centre(mix_stream(stack_ref, coeffs, s, rows))
            hat = centred * rstd
            grad = None
            for part in parts:
                term = (part[n, 0, rows, :] if len(part.shape) == 4 else part[n, rows, :]).astype(
                    F32
                )
                grad = term if grad is None else grad + term
            grad = grad.astype(BF).astype(F32)
            sums_ref[n, 0:8, :] += jnp.sum((grad * hat).reshape(chunk // 8, 8, width), axis=0)
            sums_ref[n, 8:16, :] += jnp.sum(grad.reshape(chunk // 8, 8, width), axis=0)
            scaled = grad * gain_ref[s : s + 1, :]
            grad_ref[n, rows, :] = rstd * (
                scaled
                - jnp.mean(scaled, axis=-1, keepdims=True)
                - hat * jnp.mean(scaled * hat, axis=-1, keepdims=True)
            )
        return carry

    lax.fori_loop(0, grad_ref.shape[1] // chunk, step, 0)


def norm_back(streams, parts, stack, mix, gain):
    n_in, tokens, width = stack.shape
    count = len(streams)
    tile = 32
    row_block = lambda i: (i, 0)
    outs = [sds((count, tokens, width), F32), sds((count, 16, width), F32)]
    specs = [
        pl.BlockSpec((count, 1, tile, width), lambda i: (0, 0, i, 0))
        if len(p.shape) == 4
        else pl.BlockSpec((count, tile, width), lambda i: (0, i, 0))
        for p in parts
    ]
    return pl.pallas_call(
        functools.partial(norm_back_kernel, streams, len(parts)),
        grid=(tokens // tile,),
        in_specs=specs
        + [
            pl.BlockSpec((n_in, tile, width), lambda i: (0, i, 0)),
            pl.BlockSpec((tile, mix.shape[1]), row_block),
            pl.BlockSpec(gain.shape, lambda i: (0, 0)),
        ],
        out_specs=[
            pl.BlockSpec((count, tile, width), lambda i: (0, i, 0)),
            pl.BlockSpec((count, 16, width), lambda i: (0, 0, 0)),
        ],
        out_shape=outs,
        compiler_params=params(),
        cost_estimate=cost(40 * count * tokens * width, [stack, *parts, *outs]),
        name="norm_back",
    )(*parts, stack, mix, gain)


def stack_back_kernel(*refs):
    first_ref, rest_ref, last_ref = refs[:3]
    grads = [first_ref.at[0], rest_ref.at[0], rest_ref.at[1], last_ref]
    stack_ref, mix_ref, stack_out, coeff_out = refs[3:]
    chunk = 8

    def step(i, carry):
        rows = pl.ds(pl.multiple_of(i * 2 * chunk, 2 * chunk), 2 * chunk)
        for part in range(2):
            own = pl.ds(pl.multiple_of(i * 2 * chunk + part * chunk, chunk), chunk)
            coeffs = mix_ref[own, :]
            lanes = lax.broadcasted_iota(jnp.int32, coeffs.shape, 1)
            gathered = jnp.zeros(coeffs.shape, F32)
            for j in range(8):
                given = stack_ref[j, rows, :].astype(F32)[part * chunk : (part + 1) * chunk]
                total = None
                for s in range(4):
                    grad = grads[s][own, :]
                    term = coeffs[:, 8 * s + j : 8 * s + j + 1] * grad
                    total = term if total is None else total + term
                    inner = jnp.sum(grad * given, axis=-1, keepdims=True)
                    gathered = jnp.where(lanes == 8 * s + j, inner, gathered)
                stack_out[j, own, :] = total
            coeff_out[own, :] = gathered
        return carry

    lax.fori_loop(0, coeff_out.shape[0] // (2 * chunk), step, 0)


def stack_back(grads, stack, mix):
    n_in, tokens, width = stack.shape
    tile = 32
    row_block = lambda i: (i, 0)
    outs = [sds(stack.shape, F32), sds(mix.shape, F32)]
    return pl.pallas_call(
        stack_back_kernel,
        grid=(tokens // tile,),
        in_specs=[
            pl.BlockSpec((1, tile, width), lambda i: (0, i, 0)),
            pl.BlockSpec((2, tile, width), lambda i: (0, i, 0)),
            pl.BlockSpec((tile, width), row_block),
        ]
        + [
            pl.BlockSpec((n_in, tile, width), lambda i: (0, i, 0)),
            pl.BlockSpec((tile, mix.shape[1]), row_block),
        ],
        out_specs=[
            pl.BlockSpec((n_in, tile, width), lambda i: (0, i, 0)),
            pl.BlockSpec((tile, mix.shape[1]), row_block),
        ],
        out_shape=outs,
        compiler_params=params(),
        cost_estimate=cost(130 * tokens * width, [stack, *grads, *outs]),
        name="stack_back",
    )(*grads, stack, mix)


def turn(values, cos_table, sine_table):
    lanes = lax.broadcasted_iota(jnp.int32, values.shape, 1)
    half = ROT // 2
    swapped = jnp.where(
        lanes < half, pltpu.roll(values, HD - half, 1), pltpu.roll(values, half, 1)
    )
    return values * cos_table + swapped * sine_table


def qkv_kernel(blocks, halves, first, count, *refs):
    x_refs, weights, biases = refs[:blocks], refs[blocks : blocks + halves], refs[blocks + halves : blocks + 2 * halves]
    cos_ref, sine_ref, out_ref = refs[blocks + 2 * halves :]
    rows = x_refs[0].shape[1]
    cols = weights[0].shape[1]
    step = pl.program_id(0)

    def work(rotary):
        for b, x_ref in enumerate(x_refs):
            here = slice(b * rows, (b + 1) * rows)
            for h in range(halves):
                total = dot(x_ref[0], weights[h][...], NN) + biases[h][0]
                for n in range(cols // HD):
                    values = total[:, n * HD : (n + 1) * HD]
                    if rotary:
                        values = turn(values, cos_ref[here, :], sine_ref[here, :])
                    start = h * cols + n * HD
                    out_ref[0, here, start : start + HD] = values.astype(BF)

    for n in range(count):
        pl.when(step == n)(lambda n=n: work(first + n < 2))


def qkv_proj(x_blocks, weights, first, biases, tables):
    blocks, halves = len(x_blocks), len(weights)
    count, rows, width = x_blocks[0].shape
    cols = biases[0].shape[2]
    tokens = blocks * rows
    out = sds((count, tokens, halves * cols), BF)
    table = pl.BlockSpec((tokens, HD), lambda s: (0, 0))
    return pl.pallas_call(
        functools.partial(qkv_kernel, blocks, halves, first, count),
        grid=(count,),
        in_specs=[pl.BlockSpec((1, rows, width), lambda s: (s, 0, 0))] * blocks
        + [pl.BlockSpec((width, cols), lambda s: (0, first + s))] * halves
        + [pl.BlockSpec((1, 1, cols), lambda s: (first + s, 0, 0))] * halves
        + [table, table],
        out_specs=pl.BlockSpec((1, tokens, halves * cols), lambda s: (s, 0, 0)),
        out_shape=out,
        compiler_params=params(),
        cost_estimate=cost(2 * count * halves * tokens * width * cols, [*x_blocks, out]),
        name="qkv_proj",
    )(*x_blocks, *weights, *biases, *tables)


def proj_kernel(blocks, *refs):
    x_refs, weights, out_ref = refs[:blocks], refs[blocks:-1], refs[-1]
    rows = x_refs[0].shape[0]
    for h, weight_ref in enumerate(weights):
        cols = weight_ref.shape[1]
        for b, x_ref in enumerate(x_refs):
            out_ref[b * rows : (b + 1) * rows, h * cols : (h + 1) * cols] = dot(
                x_ref[...], weight_ref[...], NN
            ).astype(BF)


def proj(x_blocks, weights, part, cols):
    blocks, halves = len(x_blocks), len(weights)
    rows, width = x_blocks[0].shape
    out = sds((blocks * rows, halves * cols), BF)
    whole = lambda a: pl.BlockSpec(a.shape, lambda i: (0, 0))
    return pl.pallas_call(
        functools.partial(proj_kernel, blocks),
        grid=(1,),
        in_specs=[whole(x) for x in x_blocks]
        + [pl.BlockSpec((width, cols), lambda i: (0, part))] * halves,
        out_specs=whole(out),
        out_shape=out,
        compiler_params=params(),
        cost_estimate=cost(2 * halves * blocks * rows * width * cols, [*x_blocks, out]),
        name="proj",
    )(*x_blocks, *weights)


def put_blocks(outs, block, values):
    outs[block % 2][0, block // 2] = values


def unproj_kernel(a_ref, *refs):
    weights, outs = refs[:-2], refs[-2:]
    _, pairs, rows, _ = outs[0].shape
    for b in range(2 * pairs):
        here = slice(b * rows, (b + 1) * rows)
        total = None
        for h, weight_ref in enumerate(weights):
            cols = weight_ref.shape[1]
            term = dot(a_ref[0, here, h * cols : (h + 1) * cols], weight_ref[...], NT)
            total = term if total is None else total + term
        put_blocks(outs, b, total.astype(BF))


def unproj(part, first, count, weights, place, blocks):
    halves = len(weights)
    _, tokens, cols = part.shape
    width = weights[0].shape[0]
    tile = 512
    rows = tokens // blocks
    outs = [sds((count, blocks // 2, rows, width), BF)] * 2
    return pl.pallas_call(
        unproj_kernel,
        grid=(count, width // tile),
        in_specs=[pl.BlockSpec((1, tokens, cols), lambda s, i: (first + s, 0, 0))]
        + [pl.BlockSpec((tile, cols // halves), lambda s, i: (i, place + s))] * halves,
        out_specs=[pl.BlockSpec((1, blocks // 2, rows, tile), lambda s, i: (s, 0, 0, i))] * 2,
        out_shape=outs,
        compiler_params=params(),
        cost_estimate=cost(2 * count * tokens * cols * width, outs),
        name="unproj",
    )(part, *weights)


def masked_scores(scalars, keys, query, block, blocks):
    rows = query.shape[0]
    raw = dot(keys, query, NT)
    lanes = lax.broadcasted_iota(jnp.int32, (1, rows), 1)
    limit = jnp.maximum(lanes + scalars[block], scalars[blocks] - 1)
    places = lax.broadcasted_iota(jnp.int32, (rows, rows), 0)
    kept = []
    for b in range(blocks):
        allowed = places <= limit - scalars[b]
        kept.append(jnp.where(allowed, raw[b * rows : (b + 1) * rows, :], -1e30))
    return jnp.concatenate(kept, axis=0)


def attend_kernel(blocks, scalars, query_ref, kv_ref, out_ref, log_ref):
    q_ref, k_ref, v_ref = query_ref.at[0], kv_ref.at[0], kv_ref.at[1]
    rows = q_ref.shape[0] // blocks
    factor = SCALE * LOG2E
    for b in range(blocks):
        here = slice(b * rows, (b + 1) * rows)
        scores = masked_scores(scalars, k_ref[...], q_ref[here, :], b, blocks)
        top = jnp.max(scores, axis=0, keepdims=True)
        probs = jnp.exp2((scores - top) * factor)
        total = jnp.sum(probs, axis=0, keepdims=True)
        mixed = dot(v_ref[...], probs.astype(BF), TN) / total
        out_ref[0, here, :] = mixed.T.astype(BF)
        log_ref[0, :, here] = top * factor + jnp.log2(total)


def attend(scalars, query, kv, blocks):
    _, tokens, cols = kv.shape
    heads = cols // HD
    outs = [sds((1, tokens, cols), BF), sds((heads, 1, tokens), F32)]
    return pl.pallas_call(
        functools.partial(attend_kernel, blocks),
        grid=(heads,),
        in_specs=[
            pl.BlockSpec(memory_space=pltpu.SMEM),
            pl.BlockSpec((1, tokens, HD), lambda h: (0, 0, h)),
            pl.BlockSpec((2, tokens, HD), lambda h: (0, 0, h)),
        ],
        out_specs=[
            pl.BlockSpec((1, tokens, HD), lambda h: (0, 0, h)),
            pl.BlockSpec((1, 1, tokens), lambda h: (h, 0, 0)),
        ],
        out_shape=outs,
        compiler_params=params(),
        cost_estimate=cost(8 * heads * tokens * tokens * HD, [query, kv, *outs]),
        name="attend",
    )(scalars, query, kv)


def attend_back_kernel(
    blocks, scalars, query_ref, kv_ref, g_ref, log_ref, cos_ref, sine_ref, grad_ref, sums_ref,
    key_acc, value_acc,
):
    q_ref, k_ref, v_ref = query_ref.at[0], kv_ref.at[0], kv_ref.at[1]
    rows = q_ref.shape[0] // blocks
    factor = SCALE * LOG2E
    sums = []
    query_sum = jnp.zeros((1, HD), F32)
    for b in range(blocks):
        here = slice(b * rows, (b + 1) * rows)
        query, grad = q_ref[here, :], g_ref[here, :]
        scores = masked_scores(scalars, k_ref[...], query, b, blocks)
        probs = jnp.exp2(scores * factor - log_ref[0, :, here])
        grad_probs = dot(v_ref[...], grad, NT)
        inner = jnp.sum(probs * grad_probs, axis=0, keepdims=True)
        grad_scores = (probs * (grad_probs - inner)).astype(BF)
        key_term = dot(grad_scores, query, NN)
        value_term = dot(probs.astype(BF), grad, NN)
        if b == 0:
            key_acc[...] = key_term
            value_acc[...] = value_term
        else:
            key_acc[...] += key_term
            value_acc[...] += value_term
        grad_query = dot(k_ref[...], grad_scores, TN).T * SCALE
        low = turn(grad_query, cos_ref[here, :], -sine_ref[here, :]).astype(BF)
        grad_ref[0, here, :] = low
        query_sum = query_sum + jnp.sum(low.astype(F32), axis=0, keepdims=True)
    low_key = turn(key_acc[...] * SCALE, cos_ref[...], -sine_ref[...]).astype(BF)
    grad_ref[1] = low_key
    low_value = value_acc[...].astype(BF)
    grad_ref[2] = low_value
    sums_ref[0, 0:1, :] = query_sum
    sums_ref[0, 1:2, :] = jnp.sum(low_key.astype(F32), axis=0, keepdims=True)
    sums_ref[0, 2:3, :] = jnp.sum(low_value.astype(F32), axis=0, keepdims=True)


def attend_back(scalars, query, kv, grad, log_total, tables, blocks):
    _, tokens, cols = kv.shape
    heads = cols // HD
    stacked = pl.BlockSpec((3, tokens, HD), lambda h: (0, 0, h))
    fixed = pl.BlockSpec((tokens, HD), lambda h: (0, 0))
    outs = [sds((3, tokens, cols), BF), sds((heads, 8, HD), F32)]
    return pl.pallas_call(
        functools.partial(attend_back_kernel, blocks),
        grid=(heads,),
        in_specs=[
            pl.BlockSpec(memory_space=pltpu.SMEM),
            pl.BlockSpec((1, tokens, HD), lambda h: (0, 0, h)),
            pl.BlockSpec((2, tokens, HD), lambda h: (0, 0, h)),
            pl.BlockSpec((tokens, HD), lambda h: (0, h)),
            pl.BlockSpec((1, 1, tokens), lambda h: (h, 0, 0)),
            fixed,
            fixed,
        ],
        out_specs=[stacked, pl.BlockSpec((1, 8, HD), lambda h: (h, 0, 0))],
        out_shape=outs,
        scratch_shapes=[pltpu.VMEM((tokens, HD), F32)] * 2,
        compiler_params=params(),
        cost_estimate=cost(16 * heads * tokens * tokens * HD, [query, kv, grad, *outs]),
        name="attend_back",
    )(scalars, query, kv, grad, log_total, *tables)


def total_of(refs, rows=slice(None)):
    total = None
    for ref in refs:
        term = (ref[0, 0, rows, :] if len(ref.shape) == 4 else ref[0, rows, :]).astype(F32)
        total = term if total is None else total + term
    return total


def term_spec(term, tile):
    width = term.shape[-1]
    if len(term.shape) == 4:
        return pl.BlockSpec((1, 1, tile, width), lambda i: (0, 0, i, 0))
    return pl.BlockSpec((1, tile, width), lambda i: (0, i, 0))


def middle_kernel(pieces, *refs):
    parts = refs[:pieces]
    res_ref, out_bias_ref, gain_ref, bias_ref, hid_ref, norm_ref = refs[pieces:]
    attn = (total_of(parts) + out_bias_ref[...]).astype(BF)
    hidden = res_ref[...] + attn.astype(F32)
    hid_ref[...] = hidden
    centred, rstd = centre(hidden)
    norm_ref[...] = (centred * rstd * gain_ref[3:4, :] + bias_ref[3:4, :]).astype(BF)


def middle(parts, residual, out_bias, gain, bias):
    tokens, width = residual.shape
    tile = 64
    block = pl.BlockSpec((tile, width), lambda i: (i, 0))
    whole = lambda a: pl.BlockSpec(a.shape, lambda i: (0, 0))
    outs = [sds((tokens, width), F32), sds((tokens, width), BF)]
    return pl.pallas_call(
        functools.partial(middle_kernel, len(parts)),
        grid=(tokens // tile,),
        in_specs=[term_spec(p, tile) for p in parts] + [block, whole(out_bias), whole(gain), whole(bias)],
        out_specs=[block] * 2,
        out_shape=outs,
        compiler_params=params(),
        cost_estimate=cost(20 * tokens * width, [*parts, residual, *outs]),
        name="middle",
    )(*parts, residual, out_bias, gain, bias)


def middle_back_kernel(pieces, *refs):
    parts = refs[:pieces]
    hid_ref, layer_ref, gain_ref = refs[pieces : pieces + 3]
    grad_ref, low_ref, sums_ref = refs[pieces + 3 :]
    grad = total_of(parts).astype(BF).astype(F32)
    centred, rstd = centre(hid_ref[...])
    hat = centred * rstd
    scaled = grad * gain_ref[3:4, :]
    grad_hidden = layer_ref[...] + rstd * (
        scaled
        - jnp.mean(scaled, axis=-1, keepdims=True)
        - hat * jnp.mean(scaled * hat, axis=-1, keepdims=True)
    )
    grad_ref[...] = grad_hidden
    low = grad_hidden.astype(BF)
    low_ref[...] = low

    @pl.when(pl.program_id(0) == 0)
    def _():
        sums_ref[...] = jnp.zeros_like(sums_ref)

    sums_ref[0:1, :] += jnp.sum(grad * hat, axis=0, keepdims=True)
    sums_ref[1:2, :] += jnp.sum(grad, axis=0, keepdims=True)
    sums_ref[2:3, :] += jnp.sum(low.astype(F32), axis=0, keepdims=True)


def middle_back(parts, hidden, grad_layer, gain):
    tokens, width = hidden.shape
    tile = 64
    block = pl.BlockSpec((tile, width), lambda i: (i, 0))
    outs = [sds((tokens, width), F32), sds((tokens, width), BF), sds((8, width), F32)]
    return pl.pallas_call(
        functools.partial(middle_back_kernel, len(parts)),
        grid=(tokens // tile,),
        in_specs=[term_spec(p, tile) for p in parts] + [block] * 2 + [pl.BlockSpec(gain.shape, lambda i: (0, 0))],
        out_specs=[block] * 2 + [pl.BlockSpec((8, width), lambda i: (0, 0))],
        out_shape=outs,
        compiler_params=params(),
        cost_estimate=cost(30 * tokens * width, [*parts, hidden, grad_layer, *outs]),
        name="middle_back",
    )(*parts, hidden, grad_layer, gain)


def gelu_pair(values):
    tail = 0.5 * (1.0 + lax.erf(values * (0.5**0.5)))
    slope = tail + values * jnp.exp2(values * values * (-0.5 * LOG2E)) * 0.3989422804014327
    return values * tail, slope


def expand_block(x_refs, weight_ref, extra_ref, back, act_ref, second_ref, columns, act_columns):
    rows = x_refs[0].shape[0]
    total = None
    for b, x_ref in enumerate(x_refs):
        here = slice(b * rows, (b + 1) * rows)
        up = dot(x_ref[...], weight_ref[...], NN)
        if back:
            low = (up * extra_ref[here, columns].astype(F32)).astype(BF)
            part = jnp.sum(low.astype(F32), axis=0, keepdims=True)
            total = part if total is None else total + part
        else:
            act, slope = gelu_pair(up + extra_ref[...])
            low = act.astype(BF)
            second_ref[here, columns] = slope.astype(BF)
        act_ref[here, act_columns] = low
    if back:
        second_ref[...] = total


def expand_kernel(blocks, *refs):
    x_refs = refs[:blocks]
    weight_ref, bias_ref, act_ref, slope_ref = refs[blocks:]
    every = slice(None)
    expand_block(x_refs, weight_ref, bias_ref, False, act_ref, slope_ref, every, every)


def expand(x_blocks, weight, bias):
    blocks = len(x_blocks)
    rows, width = x_blocks[0].shape
    tokens = blocks * rows
    hidden = bias.shape[1]
    tile = 256
    whole = pl.BlockSpec((rows, width), lambda i: (0, 0))
    column = pl.BlockSpec((tokens, tile), lambda i: (0, i))
    outs = [sds((tokens, hidden), BF)] * 2
    return pl.pallas_call(
        functools.partial(expand_kernel, blocks),
        grid=(hidden // tile,),
        in_specs=[whole] * blocks
        + [
            pl.BlockSpec((width, tile), lambda i: (0, i)),
            pl.BlockSpec((1, tile), lambda i: (0, i)),
        ],
        out_specs=[column] * 2,
        out_shape=outs,
        compiler_params=params(),
        cost_estimate=cost(2 * tokens * width * hidden, [*x_blocks, *outs]),
        name="expand",
    )(*x_blocks, weight, bias)


def feed_kernel(blocks, ready, steps, tile, back, *refs):
    halves = len(steps)
    x_refs = refs[:blocks]
    refs = refs[blocks:]
    done_refs, refs = refs[:ready], refs[ready:]
    n_new = halves - ready
    first_refs, refs = refs[:n_new], refs[n_new:]
    extra_refs, refs = refs[:n_new], refs[n_new:]
    second_refs, refs = refs[:halves], refs[halves:]
    act_refs, refs = refs[:n_new], refs[n_new:]
    other_refs, refs = refs[:n_new], refs[n_new:]
    outs, held = refs[:2], refs[2]
    step = pl.program_id(0)
    hidden = held.shape[1] // max(n_new, 1)
    per = hidden // tile
    every = slice(None)
    for n in range(n_new):
        for i in range(per):

            @pl.when(step == n * per + i)
            def _():
                columns = slice(i * tile, (i + 1) * tile)
                expand_block(
                    x_refs, first_refs[n], extra_refs[n], back, act_refs[n], other_refs[n],
                    every, every,
                )
                held[:, n * hidden + i * tile : n * hidden + (i + 1) * tile] = act_refs[n][...]

    @pl.when(step >= n_new * per)
    def _():
        _, pairs, rows, _ = outs[0].shape
        for b in range(2 * pairs):
            here = slice(b * rows, (b + 1) * rows)
            total = None
            for h in range(halves):
                if h < ready:
                    a = done_refs[h][here, :]
                else:
                    a = held[here, (h - ready) * hidden : (h - ready + 1) * hidden]
                term = dot(a, second_refs[h][...], NT)
                total = term if total is None else total + term
            put_blocks(outs, b, total.astype(BF))


def feed(x_blocks, done, weights, first_part, extras, back):
    blocks, halves, ready = len(x_blocks), len(weights), len(done)
    rows, width = x_blocks[0].shape
    tokens = blocks * rows
    n_new = halves - ready
    hidden = weights[0].shape[1] // 2
    tile, out_tile = 256, 512
    per = hidden // tile
    grid = n_new * per + width // out_tile
    second_part = 1 - first_part
    whole = lambda a: pl.BlockSpec(a.shape, lambda i: (0, 0))
    within = lambda i, n: jnp.clip(i - n * per, 0, per - 1)
    late = lambda i: jnp.maximum(i - n_new * per, 0)
    first_specs, extra_specs, act_specs, other_specs = [], [], [], []
    for n in range(n_new):
        column = pl.BlockSpec((tokens, tile), lambda i, n=n: (0, within(i, n)))
        line = pl.BlockSpec((1, tile), lambda i, n=n: (0, within(i, n)))
        first_specs.append(
            pl.BlockSpec((width, tile), lambda i, n=n: (0, first_part * per + within(i, n)))
        )
        extra_specs.append(column if back else line)
        act_specs.append(column)
        other_specs.append(line if back else column)
    outs = (
        [sds((tokens, hidden), BF)] * n_new
        + [sds((1, hidden), F32) if back else sds((tokens, hidden), BF)] * n_new
        + [sds((1, blocks // 2, rows, width), BF)] * 2
    )
    found = pl.pallas_call(
        functools.partial(feed_kernel, blocks, ready, [per] * halves, tile, back),
        grid=(grid,),
        in_specs=[whole(x) for x in x_blocks]
        + [whole(d) for d in done]
        + first_specs
        + extra_specs
        + [pl.BlockSpec((out_tile, hidden), lambda i: (late(i), second_part))] * halves,
        out_specs=act_specs
        + other_specs
        + [pl.BlockSpec((1, blocks // 2, rows, out_tile), lambda i: (0, 0, 0, late(i)))] * 2,
        out_shape=outs,
        scratch_shapes=[pltpu.VMEM((tokens, n_new * hidden), BF)],
        compiler_params=params(),
        cost_estimate=cost(2 * tokens * width * hidden * (n_new + halves), [*x_blocks, *outs]),
        name="feed_back" if back else "feed",
    )(*x_blocks, *done, *weights[ready:], *extras, *weights)
    return found[:n_new], found[n_new : 2 * n_new], found[2 * n_new :]


def weight_grad_kernel(blocks, *refs):
    left = jnp.concatenate([r[...] for r in refs[:blocks]], axis=0)
    out_ref = refs[-1]
    start = 0
    for right in refs[blocks:-1]:
        cols = right.shape[1]
        out_ref[:, start : start + cols] = dot(left, right[...], TN).astype(BF)
        start += cols


def weight_grad(lefts, rights):
    rows, width = lefts[0].shape
    tile = 512
    out = sds((width, sum(r.shape[1] for r in rights)), BF)
    return pl.pallas_call(
        functools.partial(weight_grad_kernel, len(lefts)),
        grid=(width // tile,),
        in_specs=[pl.BlockSpec((rows, tile), lambda i: (0, i))] * len(lefts)
        + [pl.BlockSpec(r.shape, lambda i: (0, 0)) for r in rights],
        out_specs=pl.BlockSpec((tile, out.shape[1]), lambda i: (i, 0)),
        out_shape=out,
        compiler_params=params(),
        cost_estimate=cost(
            2 * rows * len(lefts) * width * out.shape[1], [*rights, *lefts, out]
        ),
        name="weight_grad",
    )(*lefts, *rights)


def piece_places(order, pieces):
    places = []
    for k in range(pieces):
        place = 0
        for bit in order:
            place = 2 * place + ((k >> bit) & 1)
        places.append(place)
    return places


def piece_grad_kernel(blocks, halves, table, *refs):
    firsts, rests, attn = (refs[n * blocks : (n + 1) * blocks] for n in range(3))
    grad_ref, head_ref = refs[3 * blocks : 3 * blocks + 2]
    outs = refs[3 * blocks + 2 :]
    cols = head_ref.shape[2] // halves
    for group in range(4):
        if group == 0:
            left = [r[0] for r in firsts]
        elif group < 3:
            left = [r[group - 1] for r in rests]
        else:
            left = [r[...] for r in attn]
        right = grad_ref[group] if group < 3 else head_ref[0]
        grad = dot(jnp.concatenate(left, axis=0), right, TN).astype(BF)
        first = (group % 2) * cols
        for h in range(halves):
            outs[(group // 2) * halves + h][:, first : first + cols] = grad[
                :, h * cols : (h + 1) * cols
            ]


def piece_grad(rank, pieces, orders, firsts, rests, grads, attn, head, halves):
    blocks = len(firsts)
    _, rows, width = firsts[0].shape
    cols = head.shape[2] // halves
    feats = width // pieces
    table = jnp.concatenate(
        [
            jnp.arange(pieces, dtype=jnp.int32)[None] ^ rank,
            jnp.array([piece_places(order, pieces) for order in orders], jnp.int32),
        ],
        axis=0,
    )
    outs = [sds((width, 2 * cols), BF)] * (2 * halves)
    found = pl.pallas_call(
        functools.partial(piece_grad_kernel, blocks, halves),
        grid_spec=pltpu.PrefetchScalarGridSpec(
            num_scalar_prefetch=1,
            grid=(pieces,),
            in_specs=[pl.BlockSpec((1, rows, feats), lambda i, t: (0, 0, t[0, i]))] * blocks
            + [pl.BlockSpec((2, rows, feats), lambda i, t: (0, 0, t[0, i]))] * blocks
            + [pl.BlockSpec((rows, feats), lambda i, t: (0, t[0, i]))] * blocks
            + [pl.BlockSpec(grads.shape, lambda i, t: (0, 0, 0))]
            + [pl.BlockSpec(head.shape, lambda i, t: (0, 0, 0))],
            out_specs=[
                pl.BlockSpec((feats, 2 * cols), lambda i, t, p=p: (t[p + 1, i], 0))
                for p in range(2)
                for _ in range(halves)
            ],
        ),
        out_shape=outs,
        compiler_params=params(),
        cost_estimate=cost(
            8 * rows * blocks * width * cols * halves, [*firsts, *rests, grads, *attn, head, *outs]
        ),
        name="piece_grad",
    )(table, *firsts, *rests, *attn, grads, head)
    return [found[p * halves : (p + 1) * halves] for p in range(2)]


def mixing_kernel(pieces, *refs):
    parts = refs[:pieces]
    hid_ref, down_bias_ref, gain_ref, in_ref, out_w_ref, og_ref, cg_ref = refs[
        pieces : pieces + 7
    ]
    layer_ref, coeff_ref, grad_ref, low_ref, sums_ref, in_grad_ref, out_grad_ref = refs[
        pieces + 7 :
    ]
    down = (total_of(parts) + down_bias_ref[...]).astype(BF)
    layer = hid_ref[...] + down.astype(F32)
    layer_ref[...] = layer
    rms = lax.rsqrt(jnp.mean(layer * layer, axis=-1, keepdims=True) + EPS_RMS)
    unit = layer * rms
    gain = gain_ref[...]
    scaled = unit * gain
    act, slope = gelu_pair(dot(scaled, in_ref[...], NN, FINEST))
    coeff_ref[...] = dot(act, out_w_ref[...], NN, FINEST)
    coeff_grad = cg_ref[...]
    grad_pre = dot(coeff_grad, out_w_ref[...], NT, FINEST) * slope
    grad_scaled = dot(grad_pre, in_ref[...], NT, FINEST)
    grad_unit = grad_scaled * gain
    grad_layer = (
        rms * (grad_unit - unit * jnp.mean(grad_unit * unit, axis=-1, keepdims=True))
        + og_ref[...].astype(F32)
    )
    grad_ref[...] = grad_layer
    low = grad_layer.astype(BF)
    low_ref[...] = low

    @pl.when(pl.program_id(0) == 0)
    def _():
        sums_ref[...] = jnp.zeros_like(sums_ref)
        in_grad_ref[...] = jnp.zeros_like(in_grad_ref)
        out_grad_ref[...] = jnp.zeros_like(out_grad_ref)

    sums_ref[0:1, :] += jnp.sum(low.astype(F32), axis=0, keepdims=True)
    sums_ref[1:2, :] += jnp.sum(grad_scaled * unit, axis=0, keepdims=True)
    in_grad_ref[...] += dot(grad_pre, scaled, TN, FINEST)
    out_grad_ref[...] += dot(act, coeff_grad, TN, FINEST)


def mixing(parts, hidden, down_bias, gain, mix_in, mix_out, out_grad, coeff_grad):
    tokens, width = hidden.shape
    tile = 128
    block = pl.BlockSpec((tile, width), lambda i: (i, 0))
    whole = lambda a: pl.BlockSpec(a.shape, lambda i: (0, 0))
    narrow = pl.BlockSpec((tile, coeff_grad.shape[1]), lambda i: (i, 0))
    outs = [
        sds((tokens, width), F32),
        sds(coeff_grad.shape, F32),
        sds((tokens, width), F32),
        sds((tokens, width), BF),
        sds((8, width), F32),
        sds((mix_in.shape[1], width), F32),
        sds(mix_out.shape, F32),
    ]
    return pl.pallas_call(
        functools.partial(mixing_kernel, len(parts)),
        grid=(tokens // tile,),
        in_specs=[term_spec(p, tile) for p in parts]
        + [block]
        + [whole(a) for a in (down_bias, gain, mix_in, mix_out)]
        + [block, narrow],
        out_specs=[block, narrow, block, block] + [whole(a) for a in outs[4:]],
        out_shape=outs,
        compiler_params=params(),
        cost_estimate=cost(3000 * tokens * width, [*parts, hidden, out_grad, *outs]),
        name="mixing",
    )(*parts, hidden, down_bias, gain, mix_in, mix_out, out_grad, coeff_grad)


def swap(values, axis, bits):
    size = lax.axis_size(axis)
    return lax.ppermute(values, axis, [(i, i ^ bits) for i in range(size)])


def send_tokens(values):
    return swap(values, "core", 1), [
        swap(values, "zl", k) for k in range(1, lax.axis_size("zl"))
    ]


def token_blocks(values, beside, arrived):
    blocks = [values, beside]
    for part in arrived:
        blocks += [part, swap(part, "core", 1)]
    return blocks


def chip_sums(own, theirs):
    got = swap(theirs, "core", 1)
    sums = [
        (own[:, k].astype(F32) + got[:, k].astype(F32)).astype(BF)
        for k in range(1, own.shape[1])
    ]
    return [own, got], sums


def send_sums(sums):
    return [swap(part, "zl", k + 1) for k, part in enumerate(sums)]


def together(first, second):
    both = lax.optimization_barrier((*first, *second))
    return list(both[: len(first)]), list(both[len(first) :])


def halves_of(values):
    return [values] + [swap(values, "zh", h) for h in range(1, lax.axis_size("zh"))]


def tree(terms):
    while len(terms) > 1:
        terms = [a + b for a, b in zip(terms[::2], terms[1::2])]
    return terms[0]


def sum_parts(values, axes):
    size = lax.axis_size(axes)
    return [values] + [
        lax.ppermute(values, axes, [(i, i ^ k) for i in range(size)]) for k in range(1, size)
    ]


def exchange_orders():
    bits = list(range(lax.axis_size("row").bit_length() - 1))
    return [bits, bits[1:] + bits[:1]]


def gather_pieces(values, order):
    held = {0: values}
    for bit in order:
        for k in list(held):
            held[k ^ (1 << bit)] = swap(held[k], "row", 1 << bit)
    return [held[k] for k in range(len(held))]


def send_half(values, bit):
    return swap(values[values.shape[0] // 2 :], "row", 1 << bit)


def add_half(values, got):
    return values[: got.shape[0]].astype(F32) + got.astype(F32)


def gather_weight(values):
    return lax.all_gather(values, "row", axis=0, tiled=True)


def scatter_rows(grad):
    return lax.psum_scatter(grad, "row", scatter_dimension=0, tiled=True)


def other_halves(mine, halves):
    cols = mine.shape[1] // halves
    return [swap(mine[:, h * cols : (h + 1) * cols], "zh", h) for h in range(1, halves)]


def total_grad(mine, others):
    total = mine.astype(F32)
    for other in others:
        total = total + other.astype(F32)
    return total


def after(values, *earlier):
    return lax.optimization_barrier((values, *earlier))


def on_device(
    layer_stack, mix_coeffs, prefix, ln_gain, ln_bias, qkv_weight, qkv_bias, out_weight,
    out_bias, up_weight, up_bias, down_weight, down_bias, mix_gain, mix_in, mix_out, out_grad,
    coeff_grad,
):
    tokens, width = layer_stack.shape[1:]
    halves = lax.axis_size("zh")
    group = lax.axis_size("zl") * 2
    cols = qkv_bias.shape[1]
    feats = qkv_weight.shape[1]
    place = lax.axis_index("zl") * 2 + lax.axis_index("core")

    attn_local = jnp.concatenate(
        [qkv_weight[s] for s in range(3)] + [out_weight.T], axis=1
    )
    biases = halves_of(jnp.concatenate([qkv_bias.reshape(1, -1), up_bias.reshape(1, -1)], axis=1))
    attn_local, biases[-1] = after(attn_local, biases[-1])
    qkv_biases = [x[:, : 3 * cols].reshape(3, 1, cols) for x in biases]
    up_biases = [x[:, 3 * cols :] for x in biases]
    attn_halves = halves_of(attn_local)
    orders = exchange_orders()
    rank = lax.axis_index("row")
    row_count = lax.axis_size("row")
    offsets = (rank ^ jnp.arange(row_count, dtype=jnp.int32)) * feats
    attn_full = [gather_weight(attn_halves[0])]
    feed_local = jnp.concatenate([up_weight, down_weight.T], axis=1)
    bases = (place ^ jnp.arange(group, dtype=jnp.int32)) * tokens
    prefix_here = lax.dynamic_slice_in_dim(prefix, lax.axis_index("zh"), 1, 0)
    scalars = jnp.concatenate([bases, prefix_here])
    positions = (bases[:, None] + jnp.arange(tokens, dtype=jnp.int32)[None, :]).reshape(-1)
    inv_freq = 10000.0 ** (-(jnp.arange(ROT // 2, dtype=F32) * 2.0) / ROT)
    angles = positions.astype(F32)[:, None] * inv_freq[None, :]
    cos_half, sine_half = jnp.cos(angles), jnp.sin(angles)
    rest = jnp.zeros((positions.shape[0], HD - ROT), F32)
    tables = (
        jnp.concatenate([cos_half, cos_half, rest + 1.0], axis=1),
        jnp.concatenate([-sine_half, sine_half, rest], axis=1),
    )

    mix_flat = mix_coeffs.reshape(tokens, -1)
    query_in, kv_in, residual = front(layer_stack, mix_flat, ln_gain, ln_bias)
    query_beside, query_arrived = send_tokens(query_in)
    kv_beside, kv_arrived = send_tokens(kv_in)
    for h in range(1, halves):
        (attn_halves[h],), query_arrived = together([attn_halves[h]], query_arrived)
        attn_full.append(gather_weight(attn_halves[h]))
    feed_full = [gather_weight(after(feed_local, attn_halves[-1])[0])]
    feed_halves, kv_arrived = together(halves_of(feed_local)[1:], kv_arrived)
    query_all = token_blocks(query_in, query_beside, query_arrived)
    kv_all = token_blocks(kv_in, kv_beside, kv_arrived)
    query = qkv_proj(query_all, attn_full, 0, qkv_biases, tables)
    kv = qkv_proj(kv_all, attn_full, 1, qkv_biases, tables)
    head, log_total = attend(scalars, query, kv, group)
    feed_halves, (head,) = together(feed_halves, [head])
    feed_full += [gather_weight(held) for held in feed_halves]
    terms, sums = chip_sums(*unproj(head, 0, 1, attn_full, 3, group))
    arrived = send_sums(sums)
    hidden, normed2 = middle(
        terms + arrived, residual, out_bias.reshape(1, -1), ln_gain, ln_bias
    )
    normed2_all = token_blocks(normed2, *send_tokens(normed2))
    act, slope = zip(expand(normed2_all, feed_full[0], up_biases[0]))
    new_act, new_slope, (own, theirs) = feed(
        normed2_all, act, feed_full, 0, up_biases[1:], False
    )
    act, slope = [*act, *new_act], [*slope, *new_slope]
    terms, sums = chip_sums(own, theirs)
    layer_out, coeff_out, grad_layer, grad_down, mix_sums, mix_in_part, mix_out_part = mixing(
        terms + send_sums(sums), hidden, down_bias.reshape(1, -1), mix_gain.reshape(1, -1),
        mix_in, mix_out, out_grad, coeff_grad,
    )

    mixed = mix_in_part.shape[0]
    early = jnp.concatenate(
        [
            mix_in_part,
            mix_sums[:2],
            jnp.pad(mix_out_part.reshape(1, -1), ((0, 0), (0, width - mix_out.size))),
        ],
        axis=0,
    )
    rounds = [("core", 1)]
    for axis in ("row", "zl", "zh"):
        rounds += [(axis, 1 << bit) for bit in range(lax.axis_size(axis).bit_length() - 1)]
    beside, arrived = send_tokens(grad_down)
    (got,), (beside,) = together([swap(early, *rounds[0])], [beside])
    early = early + got
    (got,), arrived = together([swap(early, *rounds[1])], arrived)
    early = early + got
    grad_down_all = token_blocks(grad_down, beside, arrived)
    got = swap(early, *rounds[2])
    down_wide = weight_grad(grad_down_all, act)
    got, down_wide, grad_down_all[0] = after(got, down_wide, grad_down_all[0])
    early = early + got
    down_mine = scatter_rows(down_wide)
    got = swap(early, *rounds[3])
    grad_up, up_bias_part, (own, theirs) = feed(grad_down_all, (), feed_full, 1, slope, True)
    got, theirs, late_grad = after(got, theirs, grad_up[0])
    early = early + got
    terms, sums = chip_sums(own, theirs)
    arrived = send_sums(sums)
    got = swap(early, *rounds[4])
    up_wide = weight_grad(normed2_all, (late_grad, *grad_up[1:]))
    (got, up_wide), arrived = together([got, up_wide], arrived)
    early = early + got
    for more in rounds[5:]:
        early = early + swap(early, *more)
    up_mine = scatter_rows(up_wide)
    grad_hidden, grad_attn, mid_sums = middle_back(terms + arrived, hidden, grad_layer, ln_gain)
    grad_attn_all = token_blocks(grad_attn, *send_tokens(grad_attn))
    grad_heads = proj(grad_attn_all, attn_full, 3, cols)
    half_cols = down_mine.shape[1] // halves
    down_parts = [
        [down_mine[:, h * half_cols + n * half_cols // 2 : h * half_cols + (n + 1) * half_cols // 2] for n in range(2)]
        for h in range(halves)
    ]
    crossing = [swap(down_parts[h][0], "zh", h) for h in range(1, halves)]
    grads, bias_sums = attend_back(scalars, query, kv, grad_heads, log_total, tables, group)
    early_parts, (grads,) = together(crossing, [grads])
    crossing = [swap(down_parts[h][1], "zh", h) for h in range(1, halves)]
    kv_terms, kv_sums = chip_sums(*unproj(grads, 1, 2, attn_full, 1, group))
    own, theirs = unproj(grads, 0, 1, attn_full, 0, group)
    late_parts, (own, theirs) = together(crossing, [own, theirs])
    down_others = [
        jnp.concatenate([a, b], axis=1) for a, b in zip(early_parts, late_parts)
    ]
    query_terms, query_sums = chip_sums(own, theirs)
    (late_head, *kv_sums), query_sums = together([head, *kv_sums], query_sums)
    attn_parts = piece_grad(
        rank, row_count, orders, query_all, kv_all, grads, grad_attn_all, late_head, halves
    )
    kv_crossing, query_crossing = send_sums(kv_sums), send_sums(query_sums)
    norm = lambda streams, terms: norm_back(streams, terms, layer_stack, mix_flat, ln_gain)
    near = [attn_parts[p][0] for p in range(2)]
    far = [attn_parts[p][h] for h in range(1, halves) for p in range(2)]
    which = [p for h in range(1, halves) for p in range(2)]
    steps = len(orders[0])
    got = [send_half(v, orders[p][0]) for v, p in zip(far, which)]
    got, (*kv_crossing, near[0], near[1]) = together(got, [*kv_crossing, *near])
    far = [add_half(v, g).astype(BF) for v, g in zip(far, got)]
    got = [send_half(v, orders[p][1]) for v, p in zip(far, which)]
    near_got = [send_half(v, orders[p][0]) for p, v in enumerate(near)]
    kv_grads, kv_sums = norm((1, 2), kv_terms + kv_crossing)
    got, (kv_grads,) = together(got, [kv_grads])
    far = [add_half(v, g).astype(BF) for v, g in zip(far, got)]
    for n in range(2, steps):
        got = [send_half(v, orders[p][n]) for v, p in zip(far, which)]
        far = [add_half(v, g).astype(BF) for v, g in zip(far, got)]
    up_others = other_halves(up_mine, halves)
    query_crossing, near_got = together(query_crossing, near_got)
    near = [add_half(v, g) for v, g in zip(near, near_got)]
    for n in range(1, steps):
        near = [v.astype(BF) for v in near]
        near_got = [send_half(v, orders[p][n]) for p, v in enumerate(near)]
        if n == 1:
            query_grads, query_sums = norm((0,), query_terms + query_crossing)
            near_got, (query_grads, *up_others) = together(near_got, [query_grads, *up_others])
        near = [add_half(v, g) for v, g in zip(near, near_got)]
    stream_grads = (query_grads, kv_grads, grad_hidden)
    sums = [query_sums[0], kv_sums[0], kv_sums[1]]
    attn_others = [swap(v, "zh", n // 2 + 1) for n, v in enumerate(far)]
    mix_in_grad = early[:mixed].T
    down_bias_grad, mix_gain_grad = early[mixed], early[mixed + 1]
    mix_out_grad = early[mixed + 2, : mix_out.size].reshape(mix_out.shape)
    heads = cols // HD
    bias_line = lax.broadcasted_iota(jnp.int32, (halves * group, 1), 0)
    zh = lax.axis_index("zh")
    bias_rows = 0.0
    for h in range(halves):
        here = bias_sums[h * heads : (h + 1) * heads, :3].transpose(1, 0, 2).reshape(1, -1)
        line = jnp.concatenate([here, up_bias_part[h]], axis=1)
        bias_rows = bias_rows + jnp.where(bias_line == (zh ^ h) * group + place, line, 0.0)
    late = jnp.concatenate(
            [
                *[part[0:8].sum(axis=0, keepdims=True) for part in sums],
                mid_sums[0:1],
                *[part[8:16].sum(axis=0, keepdims=True) for part in sums],
                mid_sums[1:3],
                jnp.pad(bias_rows, ((0, 0), (0, width - bias_rows.shape[1]))),
            ],
            axis=0,
    )
    late = tree(sum_parts(late, ("row",)))
    late = tree(sum_parts(late, ("zl", "core")))
    late = sum_parts(late, ("zh",))
    stack_grad, coeffs_grad = stack_back(stream_grads, layer_stack, mix_flat)
    late, (stack_grad, *attn_others) = together(late, [stack_grad, *attn_others])
    late = tree(late)
    half_cols = up_mine.shape[1] // halves
    down_grad = total_grad(down_mine[:, :half_cols], down_others).T
    up_grad = total_grad(up_mine[:, :half_cols], up_others)
    attn_grad = [total_grad(near[p], attn_others[p::2]) for p in range(2)]
    qkv_grad = jnp.stack(
        [attn_grad[0][:, :cols], attn_grad[0][:, cols:], attn_grad[1][:, :cols]], axis=0
    )
    out_w_grad = attn_grad[1][:, cols:].T

    bias_grad = lax.dynamic_slice_in_dim(late, 9 + zh * group + place, 1, 0)
    qkv_bias_grad = bias_grad[0, : 3 * cols].reshape(3, cols)
    up_bias_grad = bias_grad[0, 3 * cols : 3 * cols + up_bias.shape[0]]
    return (
        layer_out,
        coeff_out,
        stack_grad,
        coeffs_grad.reshape(mix_coeffs.shape),
        late[0:4],
        late[4:8],
        qkv_grad,
        qkv_bias_grad,
        out_w_grad,
        late[8],
        up_grad,
        up_bias_grad,
        down_grad,
        down_bias_grad,
        mix_gain_grad,
        mix_in_grad,
        mix_out_grad,
    )


def solution(mesh):
    rows, cols = mesh.shape["row"], mesh.shape["col"]
    col = ("zh", "zl", "core")

    def run(*args):
        seqs = args[2].shape[0] // rows
        fine = Mesh(mesh.devices.reshape(rows, seqs, cols // (2 * seqs), 2), ALL)
        in_specs = (
            P(None, ALL, None),
            P(ALL, None, None),
            P("row"),
            P(),
            P(),
            P(None, "row", col),
            P(None, col),
            P(col, "row"),
            P(),
            P("row", col),
            P(col),
            P(col, "row"),
            P(),
            P(),
            P(),
            P(),
            P(ALL, None),
            P(ALL, None),
        )
        out_specs = (
            P(ALL, None),
            P(ALL, None),
            P(None, ALL, None),
            P(ALL, None, None),
            P(),
            P(),
            P(None, "row", col),
            P(None, col),
            P(col, "row"),
            P(),
            P("row", col),
            P(col),
            P(col, "row"),
            P(),
            P(),
            P(),
            P(),
        )
        return jax.shard_map(
            on_device, mesh=fine, in_specs=in_specs, out_specs=out_specs, check_vma=False
        )(*args)

    return run
```

```python
import functools

import jax
import jax.numpy as jnp
from jax import lax
from jax.experimental import pallas as pl
from jax.experimental.pallas import tpu as pltpu
from jax.sharding import Mesh, PartitionSpec as P

HD = 128
ROT = 32
LEN = 1024
EPS_LAYER = 1e-05
EPS_RMS = 1e-06
BF = jnp.bfloat16
F32 = jnp.float32
FINEST = lax.Precision.HIGHEST
LOG2E = 1.4426950408889634
SCALE = HD**-0.5
VMEM_CAP = 56 * 1024 * 1024
ALL = ("row", "zh", "zl", "core")

NN = (((1,), (0,)), ((), ()))
NT = (((1,), (1,)), ((), ()))
TN = (((0,), (0,)), ((), ()))


def dot(a, b, dims, precision=None):
    return lax.dot_general(a, b, dims, precision=precision, preferred_element_type=F32)


def params():
    return pltpu.CompilerParams(vmem_limit_bytes=VMEM_CAP)


def cost(flops, arrays, weight=8):
    moved = sum(int(a.size) * a.dtype.itemsize for a in arrays)
    return pl.CostEstimate(
        flops=int(weight * flops), bytes_accessed=int(weight * moved), transcendentals=0
    )


def sds(shape, dtype):
    return jax.ShapeDtypeStruct(shape, dtype)


def mix_stream(stack_ref, coeffs, s, rows):
    total = None
    for j in range(8):
        term = coeffs[:, 8 * s + j : 8 * s + j + 1] * stack_ref[j, rows, :].astype(F32)
        total = term if total is None else total + term
    return total


def centre(values):
    centred = values - jnp.mean(values, axis=-1, keepdims=True)
    spread = jnp.mean(centred * centred, axis=-1, keepdims=True)
    return centred, lax.rsqrt(spread + EPS_LAYER)


def front_kernel(stack_ref, mix_ref, gain_ref, bias_ref, first_ref, rest_ref, res_ref):
    chunk = 16

    def step(i, carry):
        rows = pl.ds(pl.multiple_of(i * chunk, chunk), chunk)
        coeffs = mix_ref[rows, :]
        for s in range(3):
            centred, rstd = centre(mix_stream(stack_ref, coeffs, s, rows))
            normed = centred * rstd * gain_ref[s : s + 1, :] + bias_ref[s : s + 1, :]
            if s == 0:
                first_ref[0, rows, :] = normed.astype(BF)
            else:
                rest_ref[s - 1, rows, :] = normed.astype(BF)
        res_ref[rows, :] = mix_stream(stack_ref, coeffs, 3, rows)
        return carry

    lax.fori_loop(0, stack_ref.shape[1] // chunk, step, 0)


def front(stack, mix, gain, bias):
    n_in, tokens, width = stack.shape
    tile = 32
    row_block = lambda i: (i, 0)
    outs = [sds((n, tokens, width), BF) for n in (1, 2)] + [sds((tokens, width), F32)]
    return pl.pallas_call(
        front_kernel,
        grid=(tokens // tile,),
        in_specs=[
            pl.BlockSpec((n_in, tile, width), lambda i: (0, i, 0)),
            pl.BlockSpec((tile, mix.shape[1]), row_block),
            pl.BlockSpec(gain.shape, lambda i: (0, 0)),
            pl.BlockSpec(bias.shape, lambda i: (0, 0)),
        ],
        out_specs=[
            pl.BlockSpec((1, tile, width), lambda i: (0, i, 0)),
            pl.BlockSpec((2, tile, width), lambda i: (0, i, 0)),
            pl.BlockSpec((tile, width), row_block),
        ],
        out_shape=outs,
        compiler_params=params(),
        cost_estimate=cost(70 * tokens * width, [stack, *outs]),
        name="front",
    )(stack, mix, gain, bias)


def norm_back_kernel(streams, pieces, *refs):
    parts = refs[:pieces]
    stack_ref, mix_ref, gain_ref, grad_ref, sums_ref = refs[pieces:]
    chunk = 16
    width = grad_ref.shape[2]

    @pl.when(pl.program_id(0) == 0)
    def _():
        sums_ref[...] = jnp.zeros_like(sums_ref)

    def step(i, carry):
        rows = pl.ds(pl.multiple_of(i * chunk, chunk), chunk)
        coeffs = mix_ref[rows, :]
        for n, s in enumerate(streams):
            centred, rstd = centre(mix_stream(stack_ref, coeffs, s, rows))
            hat = centred * rstd
            grad = None
            for part in parts:
                term = (part[0, n, rows, :] if len(part.shape) == 4 else part[n, rows, :]).astype(
                    F32
                )
                grad = term if grad is None else grad + term
            grad = grad.astype(BF).astype(F32)
            sums_ref[n, 0:8, :] += jnp.sum((grad * hat).reshape(chunk // 8, 8, width), axis=0)
            sums_ref[n, 8:16, :] += jnp.sum(grad.reshape(chunk // 8, 8, width), axis=0)
            scaled = grad * gain_ref[s : s + 1, :]
            grad_ref[n, rows, :] = rstd * (
                scaled
                - jnp.mean(scaled, axis=-1, keepdims=True)
                - hat * jnp.mean(scaled * hat, axis=-1, keepdims=True)
            )
        return carry

    lax.fori_loop(0, grad_ref.shape[1] // chunk, step, 0)


def norm_back(streams, parts, stack, mix, gain):
    n_in, tokens, width = stack.shape
    count = len(streams)
    tile = 32
    row_block = lambda i: (i, 0)
    outs = [sds((count, tokens, width), F32), sds((count, 16, width), F32)]
    specs = [
        pl.BlockSpec((1, count, tile, width), lambda i: (0, 0, i, 0))
        if len(p.shape) == 4
        else pl.BlockSpec((count, tile, width), lambda i: (0, i, 0))
        for p in parts
    ]
    return pl.pallas_call(
        functools.partial(norm_back_kernel, streams, len(parts)),
        grid=(tokens // tile,),
        in_specs=specs
        + [
            pl.BlockSpec((n_in, tile, width), lambda i: (0, i, 0)),
            pl.BlockSpec((tile, mix.shape[1]), row_block),
            pl.BlockSpec(gain.shape, lambda i: (0, 0)),
        ],
        out_specs=[
            pl.BlockSpec((count, tile, width), lambda i: (0, i, 0)),
            pl.BlockSpec((count, 16, width), lambda i: (0, 0, 0)),
        ],
        out_shape=outs,
        compiler_params=params(),
        cost_estimate=cost(40 * count * tokens * width, [stack, *parts, *outs], 0.05),
        name="norm_back",
    )(*parts, stack, mix, gain)


def stack_back_kernel(*refs):
    first_ref, rest_ref, last_ref = refs[:3]
    grads = [first_ref.at[0], rest_ref.at[0], rest_ref.at[1], last_ref]
    stack_ref, mix_ref, stack_out, coeff_out = refs[3:]
    chunk = 8

    def step(i, carry):
        rows = pl.ds(pl.multiple_of(i * 2 * chunk, 2 * chunk), 2 * chunk)
        for part in range(2):
            own = pl.ds(pl.multiple_of(i * 2 * chunk + part * chunk, chunk), chunk)
            coeffs = mix_ref[own, :]
            lanes = lax.broadcasted_iota(jnp.int32, coeffs.shape, 1)
            gathered = jnp.zeros(coeffs.shape, F32)
            for j in range(8):
                given = stack_ref[j, rows, :].astype(F32)[part * chunk : (part + 1) * chunk]
                total = None
                for s in range(4):
                    grad = grads[s][own, :]
                    term = coeffs[:, 8 * s + j : 8 * s + j + 1] * grad
                    total = term if total is None else total + term
                    inner = jnp.sum(grad * given, axis=-1, keepdims=True)
                    gathered = jnp.where(lanes == 8 * s + j, inner, gathered)
                stack_out[j, own, :] = total
            coeff_out[own, :] = gathered
        return carry

    lax.fori_loop(0, coeff_out.shape[0] // (2 * chunk), step, 0)


def stack_back(grads, stack, mix):
    n_in, tokens, width = stack.shape
    tile = 32
    row_block = lambda i: (i, 0)
    outs = [sds(stack.shape, F32), sds(mix.shape, F32)]
    return pl.pallas_call(
        stack_back_kernel,
        grid=(tokens // tile,),
        in_specs=[
            pl.BlockSpec((1, tile, width), lambda i: (0, i, 0)),
            pl.BlockSpec((2, tile, width), lambda i: (0, i, 0)),
            pl.BlockSpec((tile, width), row_block),
        ]
        + [
            pl.BlockSpec((n_in, tile, width), lambda i: (0, i, 0)),
            pl.BlockSpec((tile, mix.shape[1]), row_block),
        ],
        out_specs=[
            pl.BlockSpec((n_in, tile, width), lambda i: (0, i, 0)),
            pl.BlockSpec((tile, mix.shape[1]), row_block),
        ],
        out_shape=outs,
        compiler_params=params(),
        cost_estimate=cost(130 * tokens * width, [stack, *grads, *outs]),
        name="stack_back",
    )(*grads, stack, mix)


def turn(values, cos_table, sine_table):
    lanes = lax.broadcasted_iota(jnp.int32, values.shape, 1)
    half = ROT // 2
    swapped = jnp.where(
        lanes < half, pltpu.roll(values, HD - half, 1), pltpu.roll(values, half, 1)
    )
    return values * cos_table + swapped * sine_table


def qkv_kernel(blocks, halves, first, count, *refs):
    x_refs, weights, biases = refs[:blocks], refs[blocks : blocks + halves], refs[blocks + halves : blocks + 2 * halves]
    cos_ref, sine_ref, out_ref = refs[blocks + 2 * halves :]
    rows = x_refs[0].shape[1]
    cols = weights[0].shape[1]
    step = pl.program_id(0)

    def work(rotary):
        for b, x_ref in enumerate(x_refs):
            here = slice(b * rows, (b + 1) * rows)
            for h in range(halves):
                total = dot(x_ref[0], weights[h][...], NN) + biases[h][0]
                for n in range(cols // HD):
                    values = total[:, n * HD : (n + 1) * HD]
                    if rotary:
                        values = turn(values, cos_ref[here, :], sine_ref[here, :])
                    start = h * cols + n * HD
                    out_ref[0, here, start : start + HD] = values.astype(BF)

    for n in range(count):
        pl.when(step == n)(lambda n=n: work(first + n < 2))


def qkv_proj(x_blocks, weights, first, biases, tables):
    blocks, halves = len(x_blocks), len(weights)
    count, rows, width = x_blocks[0].shape
    cols = biases[0].shape[2]
    tokens = blocks * rows
    out = sds((count, tokens, halves * cols), BF)
    table = pl.BlockSpec((tokens, HD), lambda s: (0, 0))
    return pl.pallas_call(
        functools.partial(qkv_kernel, blocks, halves, first, count),
        grid=(count,),
        in_specs=[pl.BlockSpec((1, rows, width), lambda s: (s, 0, 0))] * blocks
        + [pl.BlockSpec((width, cols), lambda s: (0, first + s))] * halves
        + [pl.BlockSpec((1, 1, cols), lambda s: (first + s, 0, 0))] * halves
        + [table, table],
        out_specs=pl.BlockSpec((1, tokens, halves * cols), lambda s: (s, 0, 0)),
        out_shape=out,
        compiler_params=params(),
        cost_estimate=cost(2 * count * halves * tokens * width * cols, [*x_blocks, out]),
        name="qkv_proj",
    )(*x_blocks, *weights, *biases, *tables)


def proj_kernel(blocks, *refs):
    x_refs, weights, out_ref = refs[:blocks], refs[blocks:-1], refs[-1]
    rows = x_refs[0].shape[0]
    for h, weight_ref in enumerate(weights):
        cols = weight_ref.shape[1]
        for b, x_ref in enumerate(x_refs):
            out_ref[b * rows : (b + 1) * rows, h * cols : (h + 1) * cols] = dot(
                x_ref[...], weight_ref[...], NN
            ).astype(BF)


def proj(x_blocks, weights, part, cols):
    blocks, halves = len(x_blocks), len(weights)
    rows, width = x_blocks[0].shape
    out = sds((blocks * rows, halves * cols), BF)
    whole = lambda a: pl.BlockSpec(a.shape, lambda i: (0, 0))
    return pl.pallas_call(
        functools.partial(proj_kernel, blocks),
        grid=(1,),
        in_specs=[whole(x) for x in x_blocks]
        + [pl.BlockSpec((width, cols), lambda i: (0, part))] * halves,
        out_specs=whole(out),
        out_shape=out,
        compiler_params=params(),
        cost_estimate=cost(2 * halves * blocks * rows * width * cols, [*x_blocks, out]),
        name="proj",
    )(*x_blocks, *weights)


def put_blocks(outs, block, values):
    outs[block % 2][block // 2, 0] = values


def unproj_kernel(a_ref, *refs):
    weights, outs = refs[:-2], refs[-2:]
    pairs, _, rows, _ = outs[0].shape
    total = None
    for h, weight_ref in enumerate(weights):
        cols = weight_ref.shape[1]
        term = dot(a_ref[0, :, h * cols : (h + 1) * cols], weight_ref[...], NT)
        total = term if total is None else total + term
    for b in range(2 * pairs):
        put_blocks(outs, b, total[b * rows : (b + 1) * rows].astype(BF))


def unproj(part, first, count, weights, place, blocks):
    halves = len(weights)
    _, tokens, cols = part.shape
    width = weights[0].shape[0]
    tile = 512
    rows = tokens // blocks
    outs = [sds((blocks // 2, count, rows, width), BF)] * 2
    return pl.pallas_call(
        unproj_kernel,
        grid=(count, width // tile),
        in_specs=[pl.BlockSpec((1, tokens, cols), lambda s, i: (first + s, 0, 0))]
        + [pl.BlockSpec((tile, cols // halves), lambda s, i: (i, place + s))] * halves,
        out_specs=[pl.BlockSpec((blocks // 2, 1, rows, tile), lambda s, i: (0, s, 0, i))] * 2,
        out_shape=outs,
        compiler_params=params(),
        cost_estimate=cost(2 * count * tokens * cols * width, outs),
        name="unproj",
    )(part, *weights)


def masked_scores(scalars, keys, query, block, blocks):
    rows = query.shape[0]
    raw = dot(keys, query, NT)
    lanes = lax.broadcasted_iota(jnp.int32, (1, rows), 1)
    limit = jnp.maximum(lanes + scalars[block], scalars[blocks] - 1)
    places = lax.broadcasted_iota(jnp.int32, (rows, rows), 0)
    kept = []
    for b in range(blocks):
        allowed = places <= limit - scalars[b]
        kept.append(jnp.where(allowed, raw[b * rows : (b + 1) * rows, :], -1e30))
    return jnp.concatenate(kept, axis=0)


def attend_kernel(blocks, scalars, query_ref, kv_ref, out_ref, log_ref):
    q_ref, k_ref, v_ref = query_ref.at[0], kv_ref.at[0], kv_ref.at[1]
    rows = q_ref.shape[0] // blocks
    factor = SCALE * LOG2E
    for b in range(blocks):
        here = slice(b * rows, (b + 1) * rows)
        scores = masked_scores(scalars, k_ref[...], q_ref[here, :], b, blocks)
        top = jnp.max(scores, axis=0, keepdims=True)
        probs = jnp.exp2((scores - top) * factor)
        total = jnp.sum(probs, axis=0, keepdims=True)
        mixed = dot(v_ref[...], probs.astype(BF), TN) / total
        out_ref[0, here, :] = mixed.T.astype(BF)
        log_ref[0, :, here] = top * factor + jnp.log2(total)


def attend(scalars, query, kv, blocks):
    _, tokens, cols = kv.shape
    heads = cols // HD
    outs = [sds((1, tokens, cols), BF), sds((heads, 1, tokens), F32)]
    return pl.pallas_call(
        functools.partial(attend_kernel, blocks),
        grid=(heads,),
        in_specs=[
            pl.BlockSpec(memory_space=pltpu.SMEM),
            pl.BlockSpec((1, tokens, HD), lambda h: (0, 0, h)),
            pl.BlockSpec((2, tokens, HD), lambda h: (0, 0, h)),
        ],
        out_specs=[
            pl.BlockSpec((1, tokens, HD), lambda h: (0, 0, h)),
            pl.BlockSpec((1, 1, tokens), lambda h: (h, 0, 0)),
        ],
        out_shape=outs,
        compiler_params=params(),
        cost_estimate=cost(8 * heads * tokens * tokens * HD, [query, kv, *outs]),
        name="attend",
    )(scalars, query, kv)


def attend_back_kernel(
    blocks, scalars, query_ref, kv_ref, g_ref, log_ref, cos_ref, sine_ref, grad_ref, sums_ref,
    key_acc, value_acc,
):
    q_ref, k_ref, v_ref = query_ref.at[0], kv_ref.at[0], kv_ref.at[1]
    rows = q_ref.shape[0] // blocks
    factor = SCALE * LOG2E
    sums = []
    query_sum = jnp.zeros((1, HD), F32)
    for b in range(blocks):
        here = slice(b * rows, (b + 1) * rows)
        query, grad = q_ref[here, :], g_ref[here, :]
        scores = masked_scores(scalars, k_ref[...], query, b, blocks)
        probs = jnp.exp2(scores * factor - log_ref[0, :, here])
        grad_probs = dot(v_ref[...], grad, NT)
        inner = jnp.sum(probs * grad_probs, axis=0, keepdims=True)
        grad_scores = (probs * (grad_probs - inner)).astype(BF)
        key_term = dot(grad_scores, query, NN)
        value_term = dot(probs.astype(BF), grad, NN)
        if b == 0:
            key_acc[...] = key_term
            value_acc[...] = value_term
        else:
            key_acc[...] += key_term
            value_acc[...] += value_term
        grad_query = dot(k_ref[...], grad_scores, TN).T * SCALE
        low = turn(grad_query, cos_ref[here, :], -sine_ref[here, :]).astype(BF)
        grad_ref[0, here, :] = low
        query_sum = query_sum + jnp.sum(low.astype(F32), axis=0, keepdims=True)
    low_key = turn(key_acc[...] * SCALE, cos_ref[...], -sine_ref[...]).astype(BF)
    grad_ref[1] = low_key
    low_value = value_acc[...].astype(BF)
    grad_ref[2] = low_value
    sums_ref[0, 0:1, :] = query_sum
    sums_ref[0, 1:2, :] = jnp.sum(low_key.astype(F32), axis=0, keepdims=True)
    sums_ref[0, 2:3, :] = jnp.sum(low_value.astype(F32), axis=0, keepdims=True)


def attend_back(scalars, query, kv, grad, log_total, tables, blocks):
    _, tokens, cols = kv.shape
    heads = cols // HD
    stacked = pl.BlockSpec((3, tokens, HD), lambda h: (0, 0, h))
    fixed = pl.BlockSpec((tokens, HD), lambda h: (0, 0))
    outs = [sds((3, tokens, cols), BF), sds((heads, 8, HD), F32)]
    return pl.pallas_call(
        functools.partial(attend_back_kernel, blocks),
        grid=(heads,),
        in_specs=[
            pl.BlockSpec(memory_space=pltpu.SMEM),
            pl.BlockSpec((1, tokens, HD), lambda h: (0, 0, h)),
            pl.BlockSpec((2, tokens, HD), lambda h: (0, 0, h)),
            pl.BlockSpec((tokens, HD), lambda h: (0, h)),
            pl.BlockSpec((1, 1, tokens), lambda h: (h, 0, 0)),
            fixed,
            fixed,
        ],
        out_specs=[stacked, pl.BlockSpec((1, 8, HD), lambda h: (h, 0, 0))],
        out_shape=outs,
        scratch_shapes=[pltpu.VMEM((tokens, HD), F32)] * 2,
        compiler_params=params(),
        cost_estimate=cost(16 * heads * tokens * tokens * HD, [query, kv, grad, *outs]),
        name="attend_back",
    )(scalars, query, kv, grad, log_total, *tables)


def total_of(refs, rows=slice(None)):
    total = None
    for ref in refs:
        term = (ref[0, 0, rows, :] if len(ref.shape) == 4 else ref[0, rows, :]).astype(F32)
        total = term if total is None else total + term
    return total


def term_spec(term, tile):
    width = term.shape[-1]
    if len(term.shape) == 4:
        return pl.BlockSpec((1, 1, tile, width), lambda i: (0, 0, i, 0))
    return pl.BlockSpec((1, tile, width), lambda i: (0, i, 0))


def middle_kernel(pieces, *refs):
    parts = refs[:pieces]
    res_ref, out_bias_ref, gain_ref, bias_ref, hid_ref, norm_ref = refs[pieces:]
    attn = (total_of(parts) + out_bias_ref[...]).astype(BF)
    hidden = res_ref[...] + attn.astype(F32)
    hid_ref[...] = hidden
    centred, rstd = centre(hidden)
    norm_ref[...] = (centred * rstd * gain_ref[3:4, :] + bias_ref[3:4, :]).astype(BF)


def middle(parts, residual, out_bias, gain, bias):
    tokens, width = residual.shape
    tile = 64
    block = pl.BlockSpec((tile, width), lambda i: (i, 0))
    whole = lambda a: pl.BlockSpec(a.shape, lambda i: (0, 0))
    outs = [sds((tokens, width), F32), sds((tokens, width), BF)]
    return pl.pallas_call(
        functools.partial(middle_kernel, len(parts)),
        grid=(tokens // tile,),
        in_specs=[term_spec(p, tile) for p in parts] + [block, whole(out_bias), whole(gain), whole(bias)],
        out_specs=[block] * 2,
        out_shape=outs,
        compiler_params=params(),
        cost_estimate=cost(20 * tokens * width, [*parts, residual, *outs]),
        name="middle",
    )(*parts, residual, out_bias, gain, bias)


def middle_back_kernel(pieces, *refs):
    parts = refs[:pieces]
    hid_ref, layer_ref, gain_ref = refs[pieces : pieces + 3]
    grad_ref, low_ref, sums_ref = refs[pieces + 3 :]
    grad = total_of(parts).astype(BF).astype(F32)
    centred, rstd = centre(hid_ref[...])
    hat = centred * rstd
    scaled = grad * gain_ref[3:4, :]
    grad_hidden = layer_ref[...] + rstd * (
        scaled
        - jnp.mean(scaled, axis=-1, keepdims=True)
        - hat * jnp.mean(scaled * hat, axis=-1, keepdims=True)
    )
    grad_ref[...] = grad_hidden
    low = grad_hidden.astype(BF)
    low_ref[...] = low

    @pl.when(pl.program_id(0) == 0)
    def _():
        sums_ref[...] = jnp.zeros_like(sums_ref)

    sums_ref[0:1, :] += jnp.sum(grad * hat, axis=0, keepdims=True)
    sums_ref[1:2, :] += jnp.sum(grad, axis=0, keepdims=True)
    sums_ref[2:3, :] += jnp.sum(low.astype(F32), axis=0, keepdims=True)


def middle_back(parts, hidden, grad_layer, gain):
    tokens, width = hidden.shape
    tile = 64
    block = pl.BlockSpec((tile, width), lambda i: (i, 0))
    outs = [sds((tokens, width), F32), sds((tokens, width), BF), sds((8, width), F32)]
    return pl.pallas_call(
        functools.partial(middle_back_kernel, len(parts)),
        grid=(tokens // tile,),
        in_specs=[term_spec(p, tile) for p in parts] + [block] * 2 + [pl.BlockSpec(gain.shape, lambda i: (0, 0))],
        out_specs=[block] * 2 + [pl.BlockSpec((8, width), lambda i: (0, 0))],
        out_shape=outs,
        compiler_params=params(),
        cost_estimate=cost(30 * tokens * width, [*parts, hidden, grad_layer, *outs]),
        name="middle_back",
    )(*parts, hidden, grad_layer, gain)


def gelu_pair(values):
    tail = 0.5 * (1.0 + lax.erf(values * (0.5**0.5)))
    slope = tail + values * jnp.exp2(values * values * (-0.5 * LOG2E)) * 0.3989422804014327
    return values * tail, slope


def fill(x_refs, held):
    rows = x_refs[0].shape[0]

    @pl.when(pl.program_id(0) == 0)
    def _():
        for b, x_ref in enumerate(x_refs):
            held[b * rows : (b + 1) * rows, :] = x_ref[...]


def expand_block(x_held, weight_ref, extra_ref, back, act_ref, second_ref):
    up = dot(x_held[...], weight_ref[...], NN)
    if back:
        low = (up * extra_ref[...].astype(F32)).astype(BF)
        second_ref[...] = jnp.sum(low.astype(F32), axis=0, keepdims=True)
    else:
        act, slope = gelu_pair(up + extra_ref[...])
        low = act.astype(BF)
        second_ref[...] = slope.astype(BF)
    act_ref[...] = low
    return low


def expand_kernel(blocks, *refs):
    x_refs = refs[:blocks]
    weight_ref, bias_ref, act_ref, slope_ref, x_held = refs[blocks:]
    fill(x_refs, x_held)
    expand_block(x_held, weight_ref, bias_ref, False, act_ref, slope_ref)


def expand(x_blocks, weight, bias):
    blocks = len(x_blocks)
    rows, width = x_blocks[0].shape
    tokens = blocks * rows
    hidden = bias.shape[1]
    tile = 256
    whole = pl.BlockSpec((rows, width), lambda i: (0, 0))
    column = pl.BlockSpec((tokens, tile), lambda i: (0, i))
    outs = [sds((tokens, hidden), BF)] * 2
    return pl.pallas_call(
        functools.partial(expand_kernel, blocks),
        grid=(hidden // tile,),
        in_specs=[whole] * blocks
        + [
            pl.BlockSpec((width, tile), lambda i: (0, i)),
            pl.BlockSpec((1, tile), lambda i: (0, i)),
        ],
        out_specs=[column] * 2,
        out_shape=outs,
        scratch_shapes=[pltpu.VMEM((tokens, width), BF)],
        compiler_params=params(),
        cost_estimate=cost(2 * tokens * width * hidden, [*x_blocks, *outs]),
        name="expand",
    )(*x_blocks, weight, bias)


def feed_kernel(blocks, ready, steps, tile, back, *refs):
    halves = len(steps)
    x_refs = refs[:blocks]
    refs = refs[blocks:]
    done_refs, refs = refs[:ready], refs[ready:]
    n_new = halves - ready
    first_refs, refs = refs[:n_new], refs[n_new:]
    extra_refs, refs = refs[:n_new], refs[n_new:]
    second_refs, refs = refs[:halves], refs[halves:]
    act_refs, refs = refs[:n_new], refs[n_new:]
    other_refs, refs = refs[:n_new], refs[n_new:]
    outs, held, x_held = refs[:2], refs[2], refs[3]
    fill(x_refs, x_held)
    step = pl.program_id(0)
    hidden = held.shape[1] // max(n_new, 1)
    per = hidden // tile
    for n in range(n_new):
        for i in range(per):

            @pl.when(step == n * per + i)
            def _():
                held[:, n * hidden + i * tile : n * hidden + (i + 1) * tile] = expand_block(
                    x_held, first_refs[n], extra_refs[n], back, act_refs[n], other_refs[n]
                )

    @pl.when(step >= n_new * per)
    def _():
        pairs, _, rows, _ = outs[0].shape
        total = None
        for h in range(halves):
            if h < ready:
                a = done_refs[h][...]
            else:
                a = held[:, (h - ready) * hidden : (h - ready + 1) * hidden]
            term = dot(a, second_refs[h][...], NT)
            total = term if total is None else total + term
        for b in range(2 * pairs):
            put_blocks(outs, b, total[b * rows : (b + 1) * rows].astype(BF))


def feed(x_blocks, done, weights, first_part, extras, back):
    blocks, halves, ready = len(x_blocks), len(weights), len(done)
    rows, width = x_blocks[0].shape
    tokens = blocks * rows
    n_new = halves - ready
    hidden = weights[0].shape[1] // 2
    tile, out_tile = 256, 512
    per = hidden // tile
    grid = n_new * per + width // out_tile
    second_part = 1 - first_part
    whole = lambda a: pl.BlockSpec(a.shape, lambda i: (0, 0))
    within = lambda i, n: jnp.clip(i - n * per, 0, per - 1)
    late = lambda i: jnp.maximum(i - n_new * per, 0)
    first_specs, extra_specs, act_specs, other_specs = [], [], [], []
    for n in range(n_new):
        column = pl.BlockSpec((tokens, tile), lambda i, n=n: (0, within(i, n)))
        line = pl.BlockSpec((1, tile), lambda i, n=n: (0, within(i, n)))
        first_specs.append(
            pl.BlockSpec((width, tile), lambda i, n=n: (0, first_part * per + within(i, n)))
        )
        extra_specs.append(column if back else line)
        act_specs.append(column)
        other_specs.append(line if back else column)
    outs = (
        [sds((tokens, hidden), BF)] * n_new
        + [sds((1, hidden), F32) if back else sds((tokens, hidden), BF)] * n_new
        + [sds((blocks // 2, 1, rows, width), BF)] * 2
    )
    found = pl.pallas_call(
        functools.partial(feed_kernel, blocks, ready, [per] * halves, tile, back),
        grid=(grid,),
        in_specs=[whole(x) for x in x_blocks]
        + [whole(d) for d in done]
        + first_specs
        + extra_specs
        + [pl.BlockSpec((out_tile, hidden), lambda i: (late(i), second_part))] * halves,
        out_specs=act_specs
        + other_specs
        + [pl.BlockSpec((blocks // 2, 1, rows, out_tile), lambda i: (0, 0, 0, late(i)))] * 2,
        out_shape=outs,
        scratch_shapes=[
            pltpu.VMEM((tokens, n_new * hidden), BF),
            pltpu.VMEM((tokens, width), BF),
        ],
        compiler_params=params(),
        cost_estimate=cost(2 * tokens * width * hidden * (n_new + halves), [*x_blocks, *outs]),
        name="feed_back" if back else "feed",
    )(*x_blocks, *done, *weights[ready:], *extras, *weights)
    return found[:n_new], found[n_new : 2 * n_new], found[2 * n_new :]


def weight_grad_kernel(blocks, halves, *refs):
    left = jnp.concatenate([r[...] for r in refs[:blocks]], axis=0)
    rank_ref, out_ref = refs[-2], refs[-1]
    for h, right in enumerate(refs[blocks:-2]):
        out_ref[0, pl.ds(rank_ref[0] ^ h, 1)] = dot(left, right[...], TN).astype(BF)[None]


def weight_grad(lefts, rights, feats, rank):
    rows, width = lefts[0].shape
    halves, cols = len(rights), rights[0].shape[1]
    out = sds((width // feats, halves, feats, cols), BF)
    return pl.pallas_call(
        functools.partial(weight_grad_kernel, len(lefts), halves),
        grid=(width // feats,),
        in_specs=[pl.BlockSpec((rows, feats), lambda i: (0, i))] * len(lefts)
        + [pl.BlockSpec(r.shape, lambda i: (0, 0)) for r in rights]
        + [pl.BlockSpec(memory_space=pltpu.SMEM)],
        out_specs=pl.BlockSpec((1, halves, feats, cols), lambda i: (i, 0, 0, 0)),
        out_shape=out,
        compiler_params=params(),
        cost_estimate=cost(2 * rows * len(lefts) * width * halves * cols, [*rights, *lefts, out]),
        name="weight_grad",
    )(*lefts, *rights, rank)


def piece_places(order, pieces):
    places = []
    for k in range(pieces):
        place = 0
        for bit in order:
            place = 2 * place + ((k >> bit) & 1)
        places.append(place)
    return places


def piece_grad_kernel(blocks, halves, table, *refs):
    firsts, rests, attn = (refs[n * blocks : (n + 1) * blocks] for n in range(3))
    grad_ref, head_ref = refs[3 * blocks : 3 * blocks + 2]
    outs = refs[3 * blocks + 2 :]
    cols = head_ref.shape[2] // halves
    for group in range(4):
        if group == 0:
            left = [r[0] for r in firsts]
        elif group < 3:
            left = [r[group - 1] for r in rests]
        else:
            left = [r[...] for r in attn]
        right = grad_ref[group] if group < 3 else head_ref[0]
        grad = dot(jnp.concatenate(left, axis=0), right, TN).astype(BF)
        first = (group % 2) * cols
        for h in range(halves):
            outs[(group // 2) * halves + h][:, first : first + cols] = grad[
                :, h * cols : (h + 1) * cols
            ]


def piece_grad(rank, pieces, orders, firsts, rests, grads, attn, head, halves):
    blocks = len(firsts)
    _, rows, width = firsts[0].shape
    cols = head.shape[2] // halves
    feats = width // pieces
    table = jnp.concatenate(
        [
            jnp.arange(pieces, dtype=jnp.int32)[None] ^ rank,
            jnp.array([piece_places(order, pieces) for order in orders], jnp.int32),
        ],
        axis=0,
    )
    outs = [sds((width, 2 * cols), BF)] * (2 * halves)
    found = pl.pallas_call(
        functools.partial(piece_grad_kernel, blocks, halves),
        grid_spec=pltpu.PrefetchScalarGridSpec(
            num_scalar_prefetch=1,
            grid=(pieces,),
            in_specs=[pl.BlockSpec((1, rows, feats), lambda i, t: (0, 0, t[0, i]))] * blocks
            + [pl.BlockSpec((2, rows, feats), lambda i, t: (0, 0, t[0, i]))] * blocks
            + [pl.BlockSpec((rows, feats), lambda i, t: (0, t[0, i]))] * blocks
            + [pl.BlockSpec(grads.shape, lambda i, t: (0, 0, 0))]
            + [pl.BlockSpec(head.shape, lambda i, t: (0, 0, 0))],
            out_specs=[
                pl.BlockSpec((feats, 2 * cols), lambda i, t, p=p: (t[p + 1, i], 0))
                for p in range(2)
                for _ in range(halves)
            ],
        ),
        out_shape=outs,
        compiler_params=params(),
        cost_estimate=cost(
            8 * rows * blocks * width * cols * halves,
            [*firsts, *rests, grads, *attn, head, *outs],
            0.05,
        ),
        name="piece_grad",
    )(table, *firsts, *rests, *attn, grads, head)
    return [found[p * halves : (p + 1) * halves] for p in range(2)]


def mixing_kernel(pieces, *refs):
    parts = refs[:pieces]
    hid_ref, down_bias_ref, gain_ref, in_ref, out_w_ref, og_ref, cg_ref = refs[
        pieces : pieces + 7
    ]
    layer_ref, coeff_ref, grad_ref, low_ref, sums_ref, in_grad_ref, out_grad_ref = refs[
        pieces + 7 :
    ]
    down = (total_of(parts) + down_bias_ref[...]).astype(BF)
    layer = hid_ref[...] + down.astype(F32)
    layer_ref[...] = layer
    rms = lax.rsqrt(jnp.mean(layer * layer, axis=-1, keepdims=True) + EPS_RMS)
    unit = layer * rms
    gain = gain_ref[...]
    scaled = unit * gain
    act, slope = gelu_pair(dot(scaled, in_ref[...], NN, FINEST))
    coeff_ref[...] = dot(act, out_w_ref[...], NN, FINEST)
    coeff_grad = cg_ref[...]
    grad_pre = dot(coeff_grad, out_w_ref[...], NT, FINEST) * slope
    grad_scaled = dot(grad_pre, in_ref[...], NT, FINEST)
    grad_unit = grad_scaled * gain
    grad_layer = (
        rms * (grad_unit - unit * jnp.mean(grad_unit * unit, axis=-1, keepdims=True))
        + og_ref[...].astype(F32)
    )
    grad_ref[...] = grad_layer
    low = grad_layer.astype(BF)
    low_ref[...] = low

    @pl.when(pl.program_id(0) == 0)
    def _():
        sums_ref[...] = jnp.zeros_like(sums_ref)
        in_grad_ref[...] = jnp.zeros_like(in_grad_ref)
        out_grad_ref[...] = jnp.zeros_like(out_grad_ref)

    sums_ref[0:1, :] += jnp.sum(low.astype(F32), axis=0, keepdims=True)
    sums_ref[1:2, :] += jnp.sum(grad_scaled * unit, axis=0, keepdims=True)
    in_grad_ref[...] += dot(grad_pre, scaled, TN, FINEST)
    out_grad_ref[...] += dot(act, coeff_grad, TN, FINEST)


def mixing(parts, hidden, down_bias, gain, mix_in, mix_out, out_grad, coeff_grad):
    tokens, width = hidden.shape
    tile = 128
    block = pl.BlockSpec((tile, width), lambda i: (i, 0))
    whole = lambda a: pl.BlockSpec(a.shape, lambda i: (0, 0))
    narrow = pl.BlockSpec((tile, coeff_grad.shape[1]), lambda i: (i, 0))
    outs = [
        sds((tokens, width), F32),
        sds(coeff_grad.shape, F32),
        sds((tokens, width), F32),
        sds((tokens, width), BF),
        sds((8, width), F32),
        sds((mix_in.shape[1], width), F32),
        sds(mix_out.shape, F32),
    ]
    return pl.pallas_call(
        functools.partial(mixing_kernel, len(parts)),
        grid=(tokens // tile,),
        in_specs=[term_spec(p, tile) for p in parts]
        + [block]
        + [whole(a) for a in (down_bias, gain, mix_in, mix_out)]
        + [block, narrow],
        out_specs=[block, narrow, block, block] + [whole(a) for a in outs[4:]],
        out_shape=outs,
        compiler_params=params(),
        cost_estimate=cost(3000 * tokens * width, [*parts, hidden, out_grad, *outs]),
        name="mixing",
    )(*parts, hidden, down_bias, gain, mix_in, mix_out, out_grad, coeff_grad)


def swap(values, axis, bits):
    size = lax.axis_size(axis)
    return lax.ppermute(values, axis, [(i, i ^ bits) for i in range(size)])


def send_tokens(values):
    return swap(values, "core", 1), [
        swap(values, "zl", k) for k in range(1, lax.axis_size("zl"))
    ]


def token_blocks(values, beside, arrived):
    blocks = [values, beside]
    for part in arrived:
        blocks += [part, swap(part, "core", 1)]
    return blocks


def chip_sums(own, got):
    return [
        (own[k].astype(F32) + got[k].astype(F32)).astype(BF) for k in range(1, own.shape[0])
    ]


def send_sums(sums):
    return [swap(part, "zl", k + 1) for k, part in enumerate(sums)]


def together(first, second):
    both = lax.optimization_barrier((*first, *second))
    return list(both[: len(first)]), list(both[len(first) :])


def halves_of(values):
    return [values] + [swap(values, "zh", h) for h in range(1, lax.axis_size("zh"))]


def exchange_orders():
    bits = list(range(lax.axis_size("row").bit_length() - 1))
    return [bits, bits[1:] + bits[:1]]


def gather_pieces(values, order):
    held = {0: values}
    for bit in order:
        for k in list(held):
            held[k ^ (1 << bit)] = swap(held[k], "row", 1 << bit)
    return [held[k] for k in range(len(held))]


def send_half(values, bit):
    return swap(values[values.shape[0] // 2 :], "row", 1 << bit)


def add_half(values, got):
    return values[: got.shape[0]].astype(F32) + got.astype(F32)


def gather_weight(values):
    return lax.all_gather(values, "row", axis=0, tiled=True)


def scatter_weight(grad):
    mine = lax.psum_scatter(grad, "row", scatter_dimension=0, tiled=False)
    return lax.psum_scatter(mine, "zh", scatter_dimension=0, tiled=False)


def total_grad(mine, others):
    total = mine.astype(F32)
    for other in others:
        total = total + other.astype(F32)
    return total


def after(values, *earlier):
    return lax.optimization_barrier((values, *earlier))


def on_device(
    layer_stack, mix_coeffs, prefix, ln_gain, ln_bias, qkv_weight, qkv_bias, out_weight,
    out_bias, up_weight, up_bias, down_weight, down_bias, mix_gain, mix_in, mix_out, out_grad,
    coeff_grad,
):
    tokens, width = layer_stack.shape[1:]
    halves = lax.axis_size("zh")
    group = lax.axis_size("zl") * 2
    cols = qkv_bias.shape[1]
    feats = qkv_weight.shape[1]
    place = lax.axis_index("zl") * 2 + lax.axis_index("core")

    attn_local = jnp.concatenate(
        [qkv_weight[s] for s in range(3)] + [out_weight.T], axis=1
    )
    biases = halves_of(jnp.concatenate([qkv_bias.reshape(1, -1), up_bias.reshape(1, -1)], axis=1))
    attn_local, biases[-1] = after(attn_local, biases[-1])
    qkv_biases = [x[:, : 3 * cols].reshape(3, 1, cols) for x in biases]
    up_biases = [x[:, 3 * cols :] for x in biases]
    attn_halves = halves_of(attn_local)
    orders = exchange_orders()
    rank = lax.axis_index("row")
    row_count = lax.axis_size("row")
    offsets = (rank ^ jnp.arange(row_count, dtype=jnp.int32)) * feats
    attn_full = [gather_weight(attn_halves[0])]
    feed_local = jnp.concatenate([up_weight, down_weight.T], axis=1)
    bases = (place ^ jnp.arange(group, dtype=jnp.int32)) * tokens
    prefix_here = lax.dynamic_slice_in_dim(prefix, lax.axis_index("zh"), 1, 0)
    scalars = jnp.concatenate([bases, prefix_here])
    positions = (bases[:, None] + jnp.arange(tokens, dtype=jnp.int32)[None, :]).reshape(-1)
    inv_freq = 10000.0 ** (-(jnp.arange(ROT // 2, dtype=F32) * 2.0) / ROT)
    angles = positions.astype(F32)[:, None] * inv_freq[None, :]
    cos_half, sine_half = jnp.cos(angles), jnp.sin(angles)
    rest = jnp.zeros((positions.shape[0], HD - ROT), F32)
    tables = (
        jnp.concatenate([cos_half, cos_half, rest + 1.0], axis=1),
        jnp.concatenate([-sine_half, sine_half, rest], axis=1),
    )

    mix_flat = mix_coeffs.reshape(tokens, -1)
    query_in, kv_in, residual = front(layer_stack, mix_flat, ln_gain, ln_bias)
    query_beside, query_arrived = send_tokens(query_in)
    kv_beside, kv_arrived = send_tokens(kv_in)
    for h in range(1, halves):
        (attn_halves[h],), query_arrived = together([attn_halves[h]], query_arrived)
        attn_full.append(gather_weight(attn_halves[h]))
    feed_full = [gather_weight(after(feed_local, attn_halves[-1])[0])]
    feed_halves, kv_arrived = together(halves_of(feed_local)[1:], kv_arrived)
    kv_arrived, (*tables, scalars) = together(kv_arrived, [*tables, scalars])
    query_all = token_blocks(query_in, query_beside, query_arrived)
    kv_all = token_blocks(kv_in, kv_beside, kv_arrived)
    query = qkv_proj(query_all, attn_full, 0, qkv_biases, tables)
    kv = qkv_proj(kv_all, attn_full, 1, qkv_biases, tables)
    head, log_total = attend(scalars, query, kv, group)
    feed_halves, (head,) = together(feed_halves, [head])
    feed_full += [gather_weight(held) for held in feed_halves]
    own, theirs = unproj(head, 0, 1, attn_full, 3, group)
    terms = [own, swap(theirs, "core", 1)]
    arrived = send_sums(chip_sums(*terms))
    hidden, normed2 = middle(
        terms + arrived, residual, out_bias.reshape(1, -1), ln_gain, ln_bias
    )
    normed2_all = token_blocks(normed2, *send_tokens(normed2))
    act, slope = zip(expand(normed2_all, feed_full[0], up_biases[0]))
    new_act, new_slope, (own, theirs) = feed(
        normed2_all, act, feed_full, 0, up_biases[1:], False
    )
    act, slope = [*act, *new_act], [*slope, *new_slope]
    terms = [own, swap(theirs, "core", 1)]
    layer_out, coeff_out, grad_layer, grad_down, mix_sums, mix_in_part, mix_out_part = mixing(
        terms + send_sums(chip_sums(*terms)), hidden, down_bias.reshape(1, -1), mix_gain.reshape(1, -1),
        mix_in, mix_out, out_grad, coeff_grad,
    )

    mixed = mix_in_part.shape[0]
    early = jnp.concatenate(
        [
            mix_in_part,
            mix_sums[:2],
            jnp.pad(mix_out_part.reshape(1, -1), ((0, 0), (0, width - mix_out.size))),
        ],
        axis=0,
    )
    rounds = [("core", 1)]
    for axis in ("row", "zh", "zl"):
        rounds += [(axis, 1 << bit) for bit in range(lax.axis_size(axis).bit_length() - 1)]
    beside, arrived = send_tokens(grad_down)
    (got,), (beside,) = together([swap(early, *rounds[0])], [beside])
    early = early + got
    (got,), arrived = together([swap(early, *rounds[1])], arrived)
    early = early + got
    grad_down_all = token_blocks(grad_down, beside, arrived)
    got = swap(early, *rounds[2])
    half_rank = lax.axis_index("zh").reshape(1)
    down_wide = weight_grad(grad_down_all, act, feats, half_rank)
    got, down_wide, grad_down_all[0] = after(got, down_wide, grad_down_all[0])
    early = early + got
    down_mine = scatter_weight(down_wide)
    got = swap(early, *rounds[3])
    grad_up, up_bias_part, (own, theirs) = feed(grad_down_all, (), feed_full, 1, slope, True)
    got, theirs, late_grad = after(got, theirs, grad_up[0])
    early = early + got
    terms = [own, swap(theirs, "core", 1)]
    arrived = send_sums(chip_sums(*terms))
    up_wide = weight_grad(normed2_all, (late_grad, *grad_up[1:]), feats, half_rank)
    (up_wide,), arrived = together([up_wide], arrived)
    up_mine = scatter_weight(up_wide)
    grad_hidden, grad_attn, mid_sums = middle_back(terms + arrived, hidden, grad_layer, ln_gain)
    grad_attn_all = token_blocks(grad_attn, *send_tokens(grad_attn))
    grad_heads = proj(grad_attn_all, attn_full, 3, cols)
    got = swap(early, *rounds[4])
    grads, bias_sums = attend_back(scalars, query, kv, grad_heads, log_total, tables, group)
    got, grads = after(got, grads)
    early = early + got
    for more in rounds[5:]:
        early = early + swap(early, *more)
    query_own, theirs = unproj(grads, 0, 1, attn_full, 0, group)
    grads, query_own = after(grads, query_own)
    query_got = swap(theirs, "core", 1)
    kv_own, theirs = unproj(grads, 1, 2, attn_full, 1, group)
    query_got, kv_own = after(query_got, kv_own)
    query_crossing = send_sums(chip_sums(query_own, query_got))
    kv_got = swap(theirs, "core", 1)
    kv_sums = chip_sums(kv_own, kv_got)
    late_head, *kv_sums = after(head, *kv_sums)
    kv_crossing = send_sums(kv_sums)
    attn_parts = piece_grad(
        rank, row_count, orders, query_all, kv_all, grads, grad_attn_all, late_head, halves
    )
    norm = lambda streams, terms: norm_back(streams, terms, layer_stack, mix_flat, ln_gain)
    near = [attn_parts[p][0] for p in range(2)]
    far = [attn_parts[p][h] for h in range(1, halves) for p in range(2)]
    which = [p for h in range(1, halves) for p in range(2)]
    steps = len(orders[0])
    got = [send_half(v, orders[p][0]) for v, p in zip(far, which)]
    query_grads, query_sums = norm((0,), [query_own, query_got, *query_crossing])
    got, (query_grads, *near) = together(got, [query_grads, *near])
    far = [add_half(v, g).astype(BF) for v, g in zip(far, got)]
    got = [send_half(v, orders[p][1]) for v, p in zip(far, which)]
    near_got = [send_half(v, orders[p][0]) for p, v in enumerate(near)]
    got, kv_crossing = together(got, kv_crossing)
    far = [add_half(v, g).astype(BF) for v, g in zip(far, got)]
    for n in range(2, steps):
        got = [send_half(v, orders[p][n]) for v, p in zip(far, which)]
        far = [add_half(v, g).astype(BF) for v, g in zip(far, got)]
    attn_others = [swap(v, "zh", n // 2 + 1) for n, v in enumerate(far)]
    kv_grads, kv_sums = norm((1, 2), [kv_own, kv_got, *kv_crossing])
    near_got, (kv_grads,) = together(near_got, [kv_grads])
    near = [add_half(v, g) for v, g in zip(near, near_got)]
    stream_grads = (query_grads, kv_grads, grad_hidden)
    sums = [query_sums[0], kv_sums[0], kv_sums[1]]
    mix_in_grad = early[:mixed].T
    down_bias_grad, mix_gain_grad = early[mixed], early[mixed + 1]
    mix_out_grad = early[mixed + 2, : mix_out.size].reshape(mix_out.shape)
    heads = cols // HD
    bias_line = lax.broadcasted_iota(jnp.int32, (halves * group, 1), 0)
    zh = lax.axis_index("zh")
    bias_rows = 0.0
    for h in range(halves):
        here = bias_sums[h * heads : (h + 1) * heads, :3].transpose(1, 0, 2).reshape(1, -1)
        line = jnp.concatenate([here, up_bias_part[h]], axis=1)
        bias_rows = bias_rows + jnp.where(bias_line == (zh ^ h) * group + place, line, 0.0)
    late = jnp.concatenate(
            [
                *[part[0:8].sum(axis=0, keepdims=True) for part in sums],
                mid_sums[0:1],
                *[part[8:16].sum(axis=0, keepdims=True) for part in sums],
                mid_sums[1:3],
                jnp.pad(bias_rows, ((0, 0), (0, width - bias_rows.shape[1]))),
            ],
            axis=0,
    )
    near = [v.astype(BF) for v in near]
    near_got = [send_half(v, orders[p][1]) for p, v in enumerate(near)]
    got = swap(late, *rounds[1])
    stack_grad, coeffs_grad = stack_back(stream_grads, layer_stack, mix_flat)
    (got, attn_others[0], *near_got), (stack_grad,) = together(
        [got, attn_others[0], *near_got], [stack_grad]
    )
    late = late + got
    got, attn_others[1] = after(swap(late, *rounds[2]), attn_others[1])
    late = late + got
    near = [add_half(v, g) for v, g in zip(near, near_got)]
    for n in range(2, steps):
        near = [v.astype(BF) for v in near]
        near_got = [send_half(v, orders[p][n]) for p, v in enumerate(near)]
        near = [add_half(v, g) for v, g in zip(near, near_got)]
    rest = rounds[3:] + rounds[:1]
    for more in [r for r in rest if r[0] != "zh"] + [r for r in rest if r[0] == "zh"]:
        late = late + swap(late, *more)
    down_grad = down_mine.astype(F32).T
    up_grad = up_mine.astype(F32)
    attn_grad = [total_grad(near[p], attn_others[p::2]) for p in range(2)]
    qkv_grad = jnp.stack(
        [attn_grad[0][:, :cols], attn_grad[0][:, cols:], attn_grad[1][:, :cols]], axis=0
    )
    out_w_grad = attn_grad[1][:, cols:].T

    bias_grad = lax.dynamic_slice_in_dim(late, 9 + zh * group + place, 1, 0)
    qkv_bias_grad = bias_grad[0, : 3 * cols].reshape(3, cols)
    up_bias_grad = bias_grad[0, 3 * cols : 3 * cols + up_bias.shape[0]]
    return (
        layer_out,
        coeff_out,
        stack_grad,
        coeffs_grad.reshape(mix_coeffs.shape),
        late[0:4],
        late[4:8],
        qkv_grad,
        qkv_bias_grad,
        out_w_grad,
        late[8],
        up_grad,
        up_bias_grad,
        down_grad,
        down_bias_grad,
        mix_gain_grad,
        mix_in_grad,
        mix_out_grad,
    )


def solution(mesh):
    rows, cols = mesh.shape["row"], mesh.shape["col"]
    col = ("zh", "zl", "core")

    def run(*args):
        seqs = args[2].shape[0] // rows
        fine = Mesh(mesh.devices.reshape(rows, seqs, cols // (2 * seqs), 2), ALL)
        in_specs = (
            P(None, ALL, None),
            P(ALL, None, None),
            P("row"),
            P(),
            P(),
            P(None, "row", col),
            P(None, col),
            P(col, "row"),
            P(),
            P("row", col),
            P(col),
            P(col, "row"),
            P(),
            P(),
            P(),
            P(),
            P(ALL, None),
            P(ALL, None),
        )
        out_specs = (
            P(ALL, None),
            P(ALL, None),
            P(None, ALL, None),
            P(ALL, None, None),
            P(),
            P(),
            P(None, "row", col),
            P(None, col),
            P(col, "row"),
            P(),
            P("row", col),
            P(col),
            P(col, "row"),
            P(),
            P(),
            P(),
            P(),
        )
        return jax.shard_map(
            on_device, mesh=fine, in_specs=in_specs, out_specs=out_specs, check_vma=False
        )(*args)

    return run
```

```python
import functools

import jax
import jax.numpy as jnp
from jax import lax
from jax.experimental import pallas as pl
from jax.experimental.pallas import tpu as pltpu
from jax.sharding import Mesh, PartitionSpec as P

HD = 128
ROT = 32
LEN = 1024
EPS_LAYER = 1e-05
EPS_RMS = 1e-06
BF = jnp.bfloat16
F32 = jnp.float32
FINEST = lax.Precision.HIGHEST
LOG2E = 1.4426950408889634
SCALE = HD**-0.5
VMEM_CAP = 56 * 1024 * 1024
ALL = ("row", "zh", "zl", "core")

NN = (((1,), (0,)), ((), ()))
NT = (((1,), (1,)), ((), ()))
TN = (((0,), (0,)), ((), ()))


def dot(a, b, dims, precision=None):
    return lax.dot_general(a, b, dims, precision=precision, preferred_element_type=F32)


def params():
    return pltpu.CompilerParams(vmem_limit_bytes=VMEM_CAP)


def cost(flops, arrays, weight=8):
    moved = sum(int(a.size) * a.dtype.itemsize for a in arrays)
    return pl.CostEstimate(
        flops=int(weight * flops), bytes_accessed=int(weight * moved), transcendentals=0
    )


def sds(shape, dtype):
    return jax.ShapeDtypeStruct(shape, dtype)


def mix_stream(stack_ref, coeffs, s, rows):
    total = None
    for j in range(8):
        term = coeffs[:, 8 * s + j : 8 * s + j + 1] * stack_ref[j, rows, :].astype(F32)
        total = term if total is None else total + term
    return total


def centre(values):
    centred = values - jnp.mean(values, axis=-1, keepdims=True)
    spread = jnp.mean(centred * centred, axis=-1, keepdims=True)
    return centred, lax.rsqrt(spread + EPS_LAYER)


def front_kernel(stack_ref, mix_ref, gain_ref, bias_ref, first_ref, rest_ref, res_ref):
    chunk = 16

    def step(i, carry):
        rows = pl.ds(pl.multiple_of(i * chunk, chunk), chunk)
        coeffs = mix_ref[rows, :]
        for s in range(3):
            centred, rstd = centre(mix_stream(stack_ref, coeffs, s, rows))
            normed = centred * rstd * gain_ref[s : s + 1, :] + bias_ref[s : s + 1, :]
            if s == 0:
                first_ref[0, rows, :] = normed.astype(BF)
            else:
                rest_ref[s - 1, rows, :] = normed.astype(BF)
        res_ref[rows, :] = mix_stream(stack_ref, coeffs, 3, rows)
        return carry

    lax.fori_loop(0, stack_ref.shape[1] // chunk, step, 0)


def front(stack, mix, gain, bias):
    n_in, tokens, width = stack.shape
    tile = 32
    row_block = lambda i: (i, 0)
    outs = [sds((n, tokens, width), BF) for n in (1, 2)] + [sds((tokens, width), F32)]
    return pl.pallas_call(
        front_kernel,
        grid=(tokens // tile,),
        in_specs=[
            pl.BlockSpec((n_in, tile, width), lambda i: (0, i, 0)),
            pl.BlockSpec((tile, mix.shape[1]), row_block),
            pl.BlockSpec(gain.shape, lambda i: (0, 0)),
            pl.BlockSpec(bias.shape, lambda i: (0, 0)),
        ],
        out_specs=[
            pl.BlockSpec((1, tile, width), lambda i: (0, i, 0)),
            pl.BlockSpec((2, tile, width), lambda i: (0, i, 0)),
            pl.BlockSpec((tile, width), row_block),
        ],
        out_shape=outs,
        compiler_params=params(),
        cost_estimate=cost(70 * tokens * width, [stack, *outs]),
        name="front",
    )(stack, mix, gain, bias)


def norm_back_kernel(streams, pieces, *refs):
    parts = refs[:pieces]
    stack_ref, mix_ref, gain_ref, grad_ref, sums_ref = refs[pieces:]
    chunk = 16
    width = grad_ref.shape[2]

    @pl.when(pl.program_id(0) == 0)
    def _():
        sums_ref[...] = jnp.zeros_like(sums_ref)

    def step(i, carry):
        rows = pl.ds(pl.multiple_of(i * chunk, chunk), chunk)
        coeffs = mix_ref[rows, :]
        for n, s in enumerate(streams):
            centred, rstd = centre(mix_stream(stack_ref, coeffs, s, rows))
            hat = centred * rstd
            grad = None
            for part in parts:
                term = (part[0, n, rows, :] if len(part.shape) == 4 else part[n, rows, :]).astype(
                    F32
                )
                grad = term if grad is None else grad + term
            grad = grad.astype(BF).astype(F32)
            sums_ref[n, 0:8, :] += jnp.sum((grad * hat).reshape(chunk // 8, 8, width), axis=0)
            sums_ref[n, 8:16, :] += jnp.sum(grad.reshape(chunk // 8, 8, width), axis=0)
            scaled = grad * gain_ref[s : s + 1, :]
            grad_ref[n, rows, :] = rstd * (
                scaled
                - jnp.mean(scaled, axis=-1, keepdims=True)
                - hat * jnp.mean(scaled * hat, axis=-1, keepdims=True)
            )
        return carry

    lax.fori_loop(0, grad_ref.shape[1] // chunk, step, 0)


def norm_back(streams, parts, stack, mix, gain):
    n_in, tokens, width = stack.shape
    count = len(streams)
    tile = 32
    row_block = lambda i: (i, 0)
    outs = [sds((count, tokens, width), F32), sds((count, 16, width), F32)]
    specs = [
        pl.BlockSpec((1, count, tile, width), lambda i: (0, 0, i, 0))
        if len(p.shape) == 4
        else pl.BlockSpec((count, tile, width), lambda i: (0, i, 0))
        for p in parts
    ]
    return pl.pallas_call(
        functools.partial(norm_back_kernel, streams, len(parts)),
        grid=(tokens // tile,),
        in_specs=specs
        + [
            pl.BlockSpec((n_in, tile, width), lambda i: (0, i, 0)),
            pl.BlockSpec((tile, mix.shape[1]), row_block),
            pl.BlockSpec(gain.shape, lambda i: (0, 0)),
        ],
        out_specs=[
            pl.BlockSpec((count, tile, width), lambda i: (0, i, 0)),
            pl.BlockSpec((count, 16, width), lambda i: (0, 0, 0)),
        ],
        out_shape=outs,
        compiler_params=params(),
        cost_estimate=cost(40 * count * tokens * width, [stack, *parts, *outs], 0.05),
        name="norm_back",
    )(*parts, stack, mix, gain)


def stack_back_kernel(*refs):
    first_ref, rest_ref, last_ref = refs[:3]
    grads = [first_ref.at[0], rest_ref.at[0], rest_ref.at[1], last_ref]
    stack_ref, mix_ref, stack_out, coeff_out = refs[3:]
    chunk = 8

    def step(i, carry):
        rows = pl.ds(pl.multiple_of(i * 2 * chunk, 2 * chunk), 2 * chunk)
        for part in range(2):
            own = pl.ds(pl.multiple_of(i * 2 * chunk + part * chunk, chunk), chunk)
            coeffs = mix_ref[own, :]
            lanes = lax.broadcasted_iota(jnp.int32, coeffs.shape, 1)
            gathered = jnp.zeros(coeffs.shape, F32)
            for j in range(8):
                given = stack_ref[j, rows, :].astype(F32)[part * chunk : (part + 1) * chunk]
                total = None
                for s in range(4):
                    grad = grads[s][own, :]
                    term = coeffs[:, 8 * s + j : 8 * s + j + 1] * grad
                    total = term if total is None else total + term
                    inner = jnp.sum(grad * given, axis=-1, keepdims=True)
                    gathered = jnp.where(lanes == 8 * s + j, inner, gathered)
                stack_out[j, own, :] = total
            coeff_out[own, :] = gathered
        return carry

    lax.fori_loop(0, coeff_out.shape[0] // (2 * chunk), step, 0)


def stack_back(grads, stack, mix):
    n_in, tokens, width = stack.shape
    tile = 32
    row_block = lambda i: (i, 0)
    outs = [sds(stack.shape, F32), sds(mix.shape, F32)]
    return pl.pallas_call(
        stack_back_kernel,
        grid=(tokens // tile,),
        in_specs=[
            pl.BlockSpec((1, tile, width), lambda i: (0, i, 0)),
            pl.BlockSpec((2, tile, width), lambda i: (0, i, 0)),
            pl.BlockSpec((tile, width), row_block),
        ]
        + [
            pl.BlockSpec((n_in, tile, width), lambda i: (0, i, 0)),
            pl.BlockSpec((tile, mix.shape[1]), row_block),
        ],
        out_specs=[
            pl.BlockSpec((n_in, tile, width), lambda i: (0, i, 0)),
            pl.BlockSpec((tile, mix.shape[1]), row_block),
        ],
        out_shape=outs,
        compiler_params=params(),
        cost_estimate=cost(130 * tokens * width, [stack, *grads, *outs]),
        name="stack_back",
    )(*grads, stack, mix)


def turn(values, cos_table, sine_table):
    lanes = lax.broadcasted_iota(jnp.int32, values.shape, 1)
    half = ROT // 2
    swapped = jnp.where(
        lanes < half, pltpu.roll(values, HD - half, 1), pltpu.roll(values, half, 1)
    )
    return values * cos_table + swapped * sine_table


def qkv_kernel(blocks, halves, first, count, *refs):
    x_refs, weights, biases = refs[:blocks], refs[blocks : blocks + halves], refs[blocks + halves : blocks + 2 * halves]
    cos_ref, sine_ref, out_ref = refs[blocks + 2 * halves :]
    rows = x_refs[0].shape[1]
    cols = weights[0].shape[1]
    step = pl.program_id(0)

    def work(rotary):
        for b, x_ref in enumerate(x_refs):
            here = slice(b * rows, (b + 1) * rows)
            for h in range(halves):
                total = dot(x_ref[0], weights[h][...], NN) + biases[h][0]
                for n in range(cols // HD):
                    values = total[:, n * HD : (n + 1) * HD]
                    if rotary:
                        values = turn(values, cos_ref[here, :], sine_ref[here, :])
                    start = h * cols + n * HD
                    out_ref[0, here, start : start + HD] = values.astype(BF)

    for n in range(count):
        pl.when(step == n)(lambda n=n: work(first + n < 2))


def qkv_proj(x_blocks, weights, first, biases, tables):
    blocks, halves = len(x_blocks), len(weights)
    count, rows, width = x_blocks[0].shape
    cols = biases[0].shape[2]
    tokens = blocks * rows
    out = sds((count, tokens, halves * cols), BF)
    table = pl.BlockSpec((tokens, HD), lambda s: (0, 0))
    return pl.pallas_call(
        functools.partial(qkv_kernel, blocks, halves, first, count),
        grid=(count,),
        in_specs=[pl.BlockSpec((1, rows, width), lambda s: (s, 0, 0))] * blocks
        + [pl.BlockSpec((width, cols), lambda s: (0, first + s))] * halves
        + [pl.BlockSpec((1, 1, cols), lambda s: (first + s, 0, 0))] * halves
        + [table, table],
        out_specs=pl.BlockSpec((1, tokens, halves * cols), lambda s: (s, 0, 0)),
        out_shape=out,
        compiler_params=params(),
        cost_estimate=cost(2 * count * halves * tokens * width * cols, [*x_blocks, out]),
        name="qkv_proj",
    )(*x_blocks, *weights, *biases, *tables)


def proj_kernel(blocks, *refs):
    x_refs, weights, out_ref = refs[:blocks], refs[blocks:-1], refs[-1]
    rows = x_refs[0].shape[0]
    for h, weight_ref in enumerate(weights):
        cols = weight_ref.shape[1]
        for b, x_ref in enumerate(x_refs):
            out_ref[b * rows : (b + 1) * rows, h * cols : (h + 1) * cols] = dot(
                x_ref[...], weight_ref[...], NN
            ).astype(BF)


def proj(x_blocks, weights, part, cols):
    blocks, halves = len(x_blocks), len(weights)
    rows, width = x_blocks[0].shape
    out = sds((blocks * rows, halves * cols), BF)
    whole = lambda a: pl.BlockSpec(a.shape, lambda i: (0, 0))
    return pl.pallas_call(
        functools.partial(proj_kernel, blocks),
        grid=(1,),
        in_specs=[whole(x) for x in x_blocks]
        + [pl.BlockSpec((width, cols), lambda i: (0, part))] * halves,
        out_specs=whole(out),
        out_shape=out,
        compiler_params=params(),
        cost_estimate=cost(2 * halves * blocks * rows * width * cols, [*x_blocks, out]),
        name="proj",
    )(*x_blocks, *weights)


def put_blocks(outs, block, values):
    outs[block % 2][block // 2, 0] = values


def unproj_kernel(a_ref, *refs):
    weights, outs = refs[:-2], refs[-2:]
    pairs, _, rows, _ = outs[0].shape
    total = None
    for h, weight_ref in enumerate(weights):
        cols = weight_ref.shape[1]
        term = dot(a_ref[0, :, h * cols : (h + 1) * cols], weight_ref[...], NT)
        total = term if total is None else total + term
    for b in range(2 * pairs):
        put_blocks(outs, b, total[b * rows : (b + 1) * rows].astype(BF))


def unproj(part, first, count, weights, place, blocks):
    halves = len(weights)
    _, tokens, cols = part.shape
    width = weights[0].shape[0]
    tile = 512
    rows = tokens // blocks
    outs = [sds((blocks // 2, count, rows, width), BF)] * 2
    return pl.pallas_call(
        unproj_kernel,
        grid=(count, width // tile),
        in_specs=[pl.BlockSpec((1, tokens, cols), lambda s, i: (first + s, 0, 0))]
        + [pl.BlockSpec((tile, cols // halves), lambda s, i: (i, place + s))] * halves,
        out_specs=[pl.BlockSpec((blocks // 2, 1, rows, tile), lambda s, i: (0, s, 0, i))] * 2,
        out_shape=outs,
        compiler_params=params(),
        cost_estimate=cost(2 * count * tokens * cols * width, outs, 0.02),
        name="unproj",
    )(part, *weights)


def masked_scores(scalars, keys, query, block, blocks):
    rows = query.shape[0]
    raw = dot(keys, query, NT)
    lanes = lax.broadcasted_iota(jnp.int32, (1, rows), 1)
    limit = jnp.maximum(lanes + scalars[block], scalars[blocks] - 1)
    places = lax.broadcasted_iota(jnp.int32, (rows, rows), 0)
    kept = []
    for b in range(blocks):
        allowed = places <= limit - scalars[b]
        kept.append(jnp.where(allowed, raw[b * rows : (b + 1) * rows, :], -1e30))
    return jnp.concatenate(kept, axis=0)


def attend_kernel(blocks, scalars, query_ref, kv_ref, out_ref, log_ref):
    q_ref, k_ref, v_ref = query_ref.at[0], kv_ref.at[0], kv_ref.at[1]
    rows = q_ref.shape[0] // blocks
    factor = SCALE * LOG2E
    for b in range(blocks):
        here = slice(b * rows, (b + 1) * rows)
        scores = masked_scores(scalars, k_ref[...], q_ref[here, :], b, blocks)
        top = jnp.max(scores, axis=0, keepdims=True)
        probs = jnp.exp2((scores - top) * factor)
        total = jnp.sum(probs, axis=0, keepdims=True)
        mixed = dot(v_ref[...], probs.astype(BF), TN) / total
        out_ref[0, here, :] = mixed.T.astype(BF)
        log_ref[0, :, here] = top * factor + jnp.log2(total)


def attend(scalars, query, kv, blocks):
    _, tokens, cols = kv.shape
    heads = cols // HD
    outs = [sds((1, tokens, cols), BF), sds((heads, 1, tokens), F32)]
    return pl.pallas_call(
        functools.partial(attend_kernel, blocks),
        grid=(heads,),
        in_specs=[
            pl.BlockSpec(memory_space=pltpu.SMEM),
            pl.BlockSpec((1, tokens, HD), lambda h: (0, 0, h)),
            pl.BlockSpec((2, tokens, HD), lambda h: (0, 0, h)),
        ],
        out_specs=[
            pl.BlockSpec((1, tokens, HD), lambda h: (0, 0, h)),
            pl.BlockSpec((1, 1, tokens), lambda h: (h, 0, 0)),
        ],
        out_shape=outs,
        compiler_params=params(),
        cost_estimate=cost(8 * heads * tokens * tokens * HD, [query, kv, *outs]),
        name="attend",
    )(scalars, query, kv)


def attend_back_kernel(
    blocks, scalars, query_ref, kv_ref, g_ref, log_ref, cos_ref, sine_ref, grad_ref, sums_ref,
    key_acc, value_acc,
):
    q_ref, k_ref, v_ref = query_ref.at[0], kv_ref.at[0], kv_ref.at[1]
    rows = q_ref.shape[0] // blocks
    factor = SCALE * LOG2E
    sums = []
    query_sum = jnp.zeros((1, HD), F32)
    for b in range(blocks):
        here = slice(b * rows, (b + 1) * rows)
        query, grad = q_ref[here, :], g_ref[here, :]
        scores = masked_scores(scalars, k_ref[...], query, b, blocks)
        probs = jnp.exp2(scores * factor - log_ref[0, :, here])
        grad_probs = dot(v_ref[...], grad, NT)
        inner = jnp.sum(probs * grad_probs, axis=0, keepdims=True)
        grad_scores = (probs * (grad_probs - inner)).astype(BF)
        key_term = dot(grad_scores, query, NN)
        value_term = dot(probs.astype(BF), grad, NN)
        if b == 0:
            key_acc[...] = key_term
            value_acc[...] = value_term
        else:
            key_acc[...] += key_term
            value_acc[...] += value_term
        grad_query = dot(k_ref[...], grad_scores, TN).T * SCALE
        low = turn(grad_query, cos_ref[here, :], -sine_ref[here, :]).astype(BF)
        grad_ref[0, here, :] = low
        query_sum = query_sum + jnp.sum(low.astype(F32), axis=0, keepdims=True)
    low_key = turn(key_acc[...] * SCALE, cos_ref[...], -sine_ref[...]).astype(BF)
    grad_ref[1] = low_key
    low_value = value_acc[...].astype(BF)
    grad_ref[2] = low_value
    sums_ref[0, 0:1, :] = query_sum
    sums_ref[0, 1:2, :] = jnp.sum(low_key.astype(F32), axis=0, keepdims=True)
    sums_ref[0, 2:3, :] = jnp.sum(low_value.astype(F32), axis=0, keepdims=True)


def attend_back(scalars, query, kv, grad, log_total, tables, blocks):
    _, tokens, cols = kv.shape
    heads = cols // HD
    stacked = pl.BlockSpec((3, tokens, HD), lambda h: (0, 0, h))
    fixed = pl.BlockSpec((tokens, HD), lambda h: (0, 0))
    outs = [sds((3, tokens, cols), BF), sds((heads, 8, HD), F32)]
    return pl.pallas_call(
        functools.partial(attend_back_kernel, blocks),
        grid=(heads,),
        in_specs=[
            pl.BlockSpec(memory_space=pltpu.SMEM),
            pl.BlockSpec((1, tokens, HD), lambda h: (0, 0, h)),
            pl.BlockSpec((2, tokens, HD), lambda h: (0, 0, h)),
            pl.BlockSpec((tokens, HD), lambda h: (0, h)),
            pl.BlockSpec((1, 1, tokens), lambda h: (h, 0, 0)),
            fixed,
            fixed,
        ],
        out_specs=[stacked, pl.BlockSpec((1, 8, HD), lambda h: (h, 0, 0))],
        out_shape=outs,
        scratch_shapes=[pltpu.VMEM((tokens, HD), F32)] * 2,
        compiler_params=params(),
        cost_estimate=cost(16 * heads * tokens * tokens * HD, [query, kv, grad, *outs], 0.02),
        name="attend_back",
    )(scalars, query, kv, grad, log_total, *tables)


def total_of(refs, rows=slice(None)):
    total = None
    for ref in refs:
        term = (ref[0, 0, rows, :] if len(ref.shape) == 4 else ref[0, rows, :]).astype(F32)
        total = term if total is None else total + term
    return total


def term_spec(term, tile):
    width = term.shape[-1]
    if len(term.shape) == 4:
        return pl.BlockSpec((1, 1, tile, width), lambda i: (0, 0, i, 0))
    return pl.BlockSpec((1, tile, width), lambda i: (0, i, 0))


def middle_kernel(pieces, *refs):
    parts = refs[:pieces]
    res_ref, out_bias_ref, gain_ref, bias_ref, hid_ref, norm_ref = refs[pieces:]
    attn = (total_of(parts) + out_bias_ref[...]).astype(BF)
    hidden = res_ref[...] + attn.astype(F32)
    hid_ref[...] = hidden
    centred, rstd = centre(hidden)
    norm_ref[...] = (centred * rstd * gain_ref[3:4, :] + bias_ref[3:4, :]).astype(BF)


def middle(parts, residual, out_bias, gain, bias):
    tokens, width = residual.shape
    tile = 64
    block = pl.BlockSpec((tile, width), lambda i: (i, 0))
    whole = lambda a: pl.BlockSpec(a.shape, lambda i: (0, 0))
    outs = [sds((tokens, width), F32), sds((tokens, width), BF)]
    return pl.pallas_call(
        functools.partial(middle_kernel, len(parts)),
        grid=(tokens // tile,),
        in_specs=[term_spec(p, tile) for p in parts] + [block, whole(out_bias), whole(gain), whole(bias)],
        out_specs=[block] * 2,
        out_shape=outs,
        compiler_params=params(),
        cost_estimate=cost(20 * tokens * width, [*parts, residual, *outs]),
        name="middle",
    )(*parts, residual, out_bias, gain, bias)


def middle_back_kernel(pieces, *refs):
    parts = refs[:pieces]
    hid_ref, layer_ref, gain_ref = refs[pieces : pieces + 3]
    grad_ref, low_ref, sums_ref = refs[pieces + 3 :]
    grad = total_of(parts).astype(BF).astype(F32)
    centred, rstd = centre(hid_ref[...])
    hat = centred * rstd
    scaled = grad * gain_ref[3:4, :]
    grad_hidden = layer_ref[...] + rstd * (
        scaled
        - jnp.mean(scaled, axis=-1, keepdims=True)
        - hat * jnp.mean(scaled * hat, axis=-1, keepdims=True)
    )
    grad_ref[...] = grad_hidden
    low = grad_hidden.astype(BF)
    low_ref[...] = low

    @pl.when(pl.program_id(0) == 0)
    def _():
        sums_ref[...] = jnp.zeros_like(sums_ref)

    sums_ref[0:1, :] += jnp.sum(grad * hat, axis=0, keepdims=True)
    sums_ref[1:2, :] += jnp.sum(grad, axis=0, keepdims=True)
    sums_ref[2:3, :] += jnp.sum(low.astype(F32), axis=0, keepdims=True)


def middle_back(parts, hidden, grad_layer, gain):
    tokens, width = hidden.shape
    tile = 64
    block = pl.BlockSpec((tile, width), lambda i: (i, 0))
    outs = [sds((tokens, width), F32), sds((tokens, width), BF), sds((8, width), F32)]
    return pl.pallas_call(
        functools.partial(middle_back_kernel, len(parts)),
        grid=(tokens // tile,),
        in_specs=[term_spec(p, tile) for p in parts] + [block] * 2 + [pl.BlockSpec(gain.shape, lambda i: (0, 0))],
        out_specs=[block] * 2 + [pl.BlockSpec((8, width), lambda i: (0, 0))],
        out_shape=outs,
        compiler_params=params(),
        cost_estimate=cost(30 * tokens * width, [*parts, hidden, grad_layer, *outs]),
        name="middle_back",
    )(*parts, hidden, grad_layer, gain)


def gelu_pair(values):
    tail = 0.5 * (1.0 + lax.erf(values * (0.5**0.5)))
    slope = tail + values * jnp.exp2(values * values * (-0.5 * LOG2E)) * 0.3989422804014327
    return values * tail, slope


def fill(x_refs, held):
    rows = x_refs[0].shape[0]

    @pl.when(pl.program_id(0) == 0)
    def _():
        for b, x_ref in enumerate(x_refs):
            held[b * rows : (b + 1) * rows, :] = x_ref[...]


def expand_block(x_held, weight_ref, extra_ref, back, act_ref, second_ref):
    up = dot(x_held[...], weight_ref[...], NN)
    if back:
        low = (up * extra_ref[...].astype(F32)).astype(BF)
        second_ref[...] = jnp.sum(low.astype(F32), axis=0, keepdims=True)
    else:
        act, slope = gelu_pair(up + extra_ref[...])
        low = act.astype(BF)
        second_ref[...] = slope.astype(BF)
    act_ref[...] = low
    return low


def expand_kernel(blocks, *refs):
    x_refs = refs[:blocks]
    weight_ref, bias_ref, act_ref, slope_ref, x_held = refs[blocks:]
    fill(x_refs, x_held)
    expand_block(x_held, weight_ref, bias_ref, False, act_ref, slope_ref)


def expand(x_blocks, weight, bias):
    blocks = len(x_blocks)
    rows, width = x_blocks[0].shape
    tokens = blocks * rows
    hidden = bias.shape[1]
    tile = 256
    whole = pl.BlockSpec((rows, width), lambda i: (0, 0))
    column = pl.BlockSpec((tokens, tile), lambda i: (0, i))
    outs = [sds((tokens, hidden), BF)] * 2
    return pl.pallas_call(
        functools.partial(expand_kernel, blocks),
        grid=(hidden // tile,),
        in_specs=[whole] * blocks
        + [
            pl.BlockSpec((width, tile), lambda i: (0, i)),
            pl.BlockSpec((1, tile), lambda i: (0, i)),
        ],
        out_specs=[column] * 2,
        out_shape=outs,
        scratch_shapes=[pltpu.VMEM((tokens, width), BF)],
        compiler_params=params(),
        cost_estimate=cost(2 * tokens * width * hidden, [*x_blocks, *outs]),
        name="expand",
    )(*x_blocks, weight, bias)


def feed_kernel(blocks, ready, steps, tile, back, *refs):
    halves = len(steps)
    x_refs = refs[:blocks]
    refs = refs[blocks:]
    done_refs, refs = refs[:ready], refs[ready:]
    n_new = halves - ready
    first_refs, refs = refs[:n_new], refs[n_new:]
    extra_refs, refs = refs[:n_new], refs[n_new:]
    second_refs, refs = refs[:halves], refs[halves:]
    act_refs, refs = refs[:n_new], refs[n_new:]
    other_refs, refs = refs[:n_new], refs[n_new:]
    outs, held, x_held = refs[:2], refs[2], refs[3]
    fill(x_refs, x_held)
    step = pl.program_id(0)
    hidden = held.shape[1] // max(n_new, 1)
    per = hidden // tile
    for n in range(n_new):
        for i in range(per):

            @pl.when(step == n * per + i)
            def _():
                held[:, n * hidden + i * tile : n * hidden + (i + 1) * tile] = expand_block(
                    x_held, first_refs[n], extra_refs[n], back, act_refs[n], other_refs[n]
                )

    @pl.when(step >= n_new * per)
    def _():
        pairs, _, rows, _ = outs[0].shape
        total = None
        for h in range(halves):
            if h < ready:
                a = done_refs[h][...]
            else:
                a = held[:, (h - ready) * hidden : (h - ready + 1) * hidden]
            term = dot(a, second_refs[h][...], NT)
            total = term if total is None else total + term
        for b in range(2 * pairs):
            put_blocks(outs, b, total[b * rows : (b + 1) * rows].astype(BF))


def feed(x_blocks, done, weights, first_part, extras, back):
    blocks, halves, ready = len(x_blocks), len(weights), len(done)
    rows, width = x_blocks[0].shape
    tokens = blocks * rows
    n_new = halves - ready
    hidden = weights[0].shape[1] // 2
    tile, out_tile = 256, 512
    per = hidden // tile
    grid = n_new * per + width // out_tile
    second_part = 1 - first_part
    whole = lambda a: pl.BlockSpec(a.shape, lambda i: (0, 0))
    within = lambda i, n: jnp.clip(i - n * per, 0, per - 1)
    late = lambda i: jnp.maximum(i - n_new * per, 0)
    first_specs, extra_specs, act_specs, other_specs = [], [], [], []
    for n in range(n_new):
        column = pl.BlockSpec((tokens, tile), lambda i, n=n: (0, within(i, n)))
        line = pl.BlockSpec((1, tile), lambda i, n=n: (0, within(i, n)))
        first_specs.append(
            pl.BlockSpec((width, tile), lambda i, n=n: (0, first_part * per + within(i, n)))
        )
        extra_specs.append(column if back else line)
        act_specs.append(column)
        other_specs.append(line if back else column)
    outs = (
        [sds((tokens, hidden), BF)] * n_new
        + [sds((1, hidden), F32) if back else sds((tokens, hidden), BF)] * n_new
        + [sds((blocks // 2, 1, rows, width), BF)] * 2
    )
    found = pl.pallas_call(
        functools.partial(feed_kernel, blocks, ready, [per] * halves, tile, back),
        grid=(grid,),
        in_specs=[whole(x) for x in x_blocks]
        + [whole(d) for d in done]
        + first_specs
        + extra_specs
        + [pl.BlockSpec((out_tile, hidden), lambda i: (late(i), second_part))] * halves,
        out_specs=act_specs
        + other_specs
        + [pl.BlockSpec((blocks // 2, 1, rows, out_tile), lambda i: (0, 0, 0, late(i)))] * 2,
        out_shape=outs,
        scratch_shapes=[
            pltpu.VMEM((tokens, n_new * hidden), BF),
            pltpu.VMEM((tokens, width), BF),
        ],
        compiler_params=params(),
        cost_estimate=cost(2 * tokens * width * hidden * (n_new + halves), [*x_blocks, *outs]),
        name="feed_back" if back else "feed",
    )(*x_blocks, *done, *weights[ready:], *extras, *weights)
    return found[:n_new], found[n_new : 2 * n_new], found[2 * n_new :]


def weight_grad_kernel(blocks, halves, *refs):
    left = jnp.concatenate([r[...] for r in refs[:blocks]], axis=0)
    rank_ref, out_ref = refs[-2], refs[-1]
    for h, right in enumerate(refs[blocks:-2]):
        out_ref[0, pl.ds(rank_ref[0] ^ h, 1)] = dot(left, right[...], TN).astype(BF)[None]


def weight_grad(lefts, rights, feats, rank):
    rows, width = lefts[0].shape
    halves, cols = len(rights), rights[0].shape[1]
    out = sds((width // feats, halves, feats, cols), BF)
    return pl.pallas_call(
        functools.partial(weight_grad_kernel, len(lefts), halves),
        grid=(width // feats,),
        in_specs=[pl.BlockSpec((rows, feats), lambda i: (0, i))] * len(lefts)
        + [pl.BlockSpec(r.shape, lambda i: (0, 0)) for r in rights]
        + [pl.BlockSpec(memory_space=pltpu.SMEM)],
        out_specs=pl.BlockSpec((1, halves, feats, cols), lambda i: (i, 0, 0, 0)),
        out_shape=out,
        compiler_params=params(),
        cost_estimate=cost(2 * rows * len(lefts) * width * halves * cols, [*rights, *lefts, out]),
        name="weight_grad",
    )(*lefts, *rights, rank)


def piece_places(order, pieces):
    places = []
    for k in range(pieces):
        place = 0
        for bit in order:
            place = 2 * place + ((k >> bit) & 1)
        places.append(place)
    return places


def piece_grad_kernel(blocks, halves, table, *refs):
    firsts, rests, attn = (refs[n * blocks : (n + 1) * blocks] for n in range(3))
    grad_ref, head_ref = refs[3 * blocks : 3 * blocks + 2]
    outs = refs[3 * blocks + 2 :]
    cols = head_ref.shape[2] // halves
    for group in range(4):
        if group == 0:
            left = [r[0] for r in firsts]
        elif group < 3:
            left = [r[group - 1] for r in rests]
        else:
            left = [r[...] for r in attn]
        right = grad_ref[group] if group < 3 else head_ref[0]
        grad = dot(jnp.concatenate(left, axis=0), right, TN).astype(BF)
        first = (group % 2) * cols
        for h in range(halves):
            outs[(group // 2) * halves + h][:, first : first + cols] = grad[
                :, h * cols : (h + 1) * cols
            ]


def piece_grad(rank, pieces, orders, firsts, rests, grads, attn, head, halves):
    blocks = len(firsts)
    _, rows, width = firsts[0].shape
    cols = head.shape[2] // halves
    feats = width // pieces
    table = jnp.concatenate(
        [
            jnp.arange(pieces, dtype=jnp.int32)[None] ^ rank,
            jnp.array([piece_places(order, pieces) for order in orders], jnp.int32),
        ],
        axis=0,
    )
    outs = [sds((width, 2 * cols), BF)] * (2 * halves)
    found = pl.pallas_call(
        functools.partial(piece_grad_kernel, blocks, halves),
        grid_spec=pltpu.PrefetchScalarGridSpec(
            num_scalar_prefetch=1,
            grid=(pieces,),
            in_specs=[pl.BlockSpec((1, rows, feats), lambda i, t: (0, 0, t[0, i]))] * blocks
            + [pl.BlockSpec((2, rows, feats), lambda i, t: (0, 0, t[0, i]))] * blocks
            + [pl.BlockSpec((rows, feats), lambda i, t: (0, t[0, i]))] * blocks
            + [pl.BlockSpec(grads.shape, lambda i, t: (0, 0, 0))]
            + [pl.BlockSpec(head.shape, lambda i, t: (0, 0, 0))],
            out_specs=[
                pl.BlockSpec((feats, 2 * cols), lambda i, t, p=p: (t[p + 1, i], 0))
                for p in range(2)
                for _ in range(halves)
            ],
        ),
        out_shape=outs,
        compiler_params=params(),
        cost_estimate=cost(
            8 * rows * blocks * width * cols * halves,
            [*firsts, *rests, grads, *attn, head, *outs],
            0.05,
        ),
        name="piece_grad",
    )(table, *firsts, *rests, *attn, grads, head)
    return [found[p * halves : (p + 1) * halves] for p in range(2)]


def mixing_kernel(pieces, *refs):
    parts = refs[:pieces]
    hid_ref, down_bias_ref, gain_ref, in_ref, out_w_ref, og_ref, cg_ref = refs[
        pieces : pieces + 7
    ]
    layer_ref, coeff_ref, grad_ref, low_ref, sums_ref, in_grad_ref, out_grad_ref = refs[
        pieces + 7 :
    ]
    down = (total_of(parts) + down_bias_ref[...]).astype(BF)
    layer = hid_ref[...] + down.astype(F32)
    layer_ref[...] = layer
    rms = lax.rsqrt(jnp.mean(layer * layer, axis=-1, keepdims=True) + EPS_RMS)
    unit = layer * rms
    gain = gain_ref[...]
    scaled = unit * gain
    act, slope = gelu_pair(dot(scaled, in_ref[...], NN, FINEST))
    coeff_ref[...] = dot(act, out_w_ref[...], NN, FINEST)
    coeff_grad = cg_ref[...]
    grad_pre = dot(coeff_grad, out_w_ref[...], NT, FINEST) * slope
    grad_scaled = dot(grad_pre, in_ref[...], NT, FINEST)
    grad_unit = grad_scaled * gain
    grad_layer = (
        rms * (grad_unit - unit * jnp.mean(grad_unit * unit, axis=-1, keepdims=True))
        + og_ref[...].astype(F32)
    )
    grad_ref[...] = grad_layer
    low = grad_layer.astype(BF)
    low_ref[...] = low

    @pl.when(pl.program_id(0) == 0)
    def _():
        sums_ref[...] = jnp.zeros_like(sums_ref)
        in_grad_ref[...] = jnp.zeros_like(in_grad_ref)
        out_grad_ref[...] = jnp.zeros_like(out_grad_ref)

    sums_ref[0:1, :] += jnp.sum(low.astype(F32), axis=0, keepdims=True)
    sums_ref[1:2, :] += jnp.sum(grad_scaled * unit, axis=0, keepdims=True)
    in_grad_ref[...] += dot(grad_pre, scaled, TN, FINEST)
    out_grad_ref[...] += dot(act, coeff_grad, TN, FINEST)


def mixing(parts, hidden, down_bias, gain, mix_in, mix_out, out_grad, coeff_grad):
    tokens, width = hidden.shape
    tile = 128
    block = pl.BlockSpec((tile, width), lambda i: (i, 0))
    whole = lambda a: pl.BlockSpec(a.shape, lambda i: (0, 0))
    narrow = pl.BlockSpec((tile, coeff_grad.shape[1]), lambda i: (i, 0))
    outs = [
        sds((tokens, width), F32),
        sds(coeff_grad.shape, F32),
        sds((tokens, width), F32),
        sds((tokens, width), BF),
        sds((8, width), F32),
        sds((mix_in.shape[1], width), F32),
        sds(mix_out.shape, F32),
    ]
    return pl.pallas_call(
        functools.partial(mixing_kernel, len(parts)),
        grid=(tokens // tile,),
        in_specs=[term_spec(p, tile) for p in parts]
        + [block]
        + [whole(a) for a in (down_bias, gain, mix_in, mix_out)]
        + [block, narrow],
        out_specs=[block, narrow, block, block] + [whole(a) for a in outs[4:]],
        out_shape=outs,
        compiler_params=params(),
        cost_estimate=cost(3000 * tokens * width, [*parts, hidden, out_grad, *outs]),
        name="mixing",
    )(*parts, hidden, down_bias, gain, mix_in, mix_out, out_grad, coeff_grad)


def swap(values, axis, bits):
    size = lax.axis_size(axis)
    return lax.ppermute(values, axis, [(i, i ^ bits) for i in range(size)])


def send_tokens(values):
    return swap(values, "core", 1), [
        swap(values, "zl", k) for k in range(1, lax.axis_size("zl"))
    ]


def token_blocks(values, beside, arrived):
    blocks = [values, beside]
    for part in arrived:
        blocks += [part, swap(part, "core", 1)]
    return blocks


def chip_sums(own, got):
    return [
        (own[k].astype(F32) + got[k].astype(F32)).astype(BF) for k in range(1, own.shape[0])
    ]


def send_sums(sums):
    return [swap(part, "zl", k + 1) for k, part in enumerate(sums)]


def together(first, second):
    both = lax.optimization_barrier((*first, *second))
    return list(both[: len(first)]), list(both[len(first) :])


def halves_of(values):
    return [values] + [swap(values, "zh", h) for h in range(1, lax.axis_size("zh"))]


def exchange_orders():
    bits = list(range(lax.axis_size("row").bit_length() - 1))
    return [bits, bits[1:] + bits[:1]]


def gather_pieces(values, order):
    held = {0: values}
    for bit in order:
        for k in list(held):
            held[k ^ (1 << bit)] = swap(held[k], "row", 1 << bit)
    return [held[k] for k in range(len(held))]


def send_half(values, bit):
    return swap(values[values.shape[0] // 2 :], "row", 1 << bit)


def add_half(values, got):
    return values[: got.shape[0]].astype(F32) + got.astype(F32)


def gather_weight(values):
    return lax.all_gather(values, "row", axis=0, tiled=True)


def scatter_weight(grad):
    mine = lax.psum_scatter(grad, "row", scatter_dimension=0, tiled=False)
    return lax.psum_scatter(mine, "zh", scatter_dimension=0, tiled=False)


def total_grad(mine, others):
    total = mine.astype(F32)
    for other in others:
        total = total + other.astype(F32)
    return total


def after(values, *earlier):
    return lax.optimization_barrier((values, *earlier))


def on_device(
    layer_stack, mix_coeffs, prefix, ln_gain, ln_bias, qkv_weight, qkv_bias, out_weight,
    out_bias, up_weight, up_bias, down_weight, down_bias, mix_gain, mix_in, mix_out, out_grad,
    coeff_grad,
):
    tokens, width = layer_stack.shape[1:]
    halves = lax.axis_size("zh")
    group = lax.axis_size("zl") * 2
    cols = qkv_bias.shape[1]
    feats = qkv_weight.shape[1]
    place = lax.axis_index("zl") * 2 + lax.axis_index("core")

    attn_local = jnp.concatenate(
        [qkv_weight[s] for s in range(3)] + [out_weight.T], axis=1
    )
    biases = halves_of(jnp.concatenate([qkv_bias.reshape(1, -1), up_bias.reshape(1, -1)], axis=1))
    attn_local, biases[-1] = after(attn_local, biases[-1])
    qkv_biases = [x[:, : 3 * cols].reshape(3, 1, cols) for x in biases]
    up_biases = [x[:, 3 * cols :] for x in biases]
    attn_halves = halves_of(attn_local)
    orders = exchange_orders()
    rank = lax.axis_index("row")
    row_count = lax.axis_size("row")
    offsets = (rank ^ jnp.arange(row_count, dtype=jnp.int32)) * feats
    attn_full = [gather_weight(attn_halves[0])]
    feed_local = jnp.concatenate([up_weight, down_weight.T], axis=1)
    bases = (place ^ jnp.arange(group, dtype=jnp.int32)) * tokens
    prefix_here = lax.dynamic_slice_in_dim(prefix, lax.axis_index("zh"), 1, 0)
    scalars = jnp.concatenate([bases, prefix_here])
    positions = (bases[:, None] + jnp.arange(tokens, dtype=jnp.int32)[None, :]).reshape(-1)
    inv_freq = 10000.0 ** (-(jnp.arange(ROT // 2, dtype=F32) * 2.0) / ROT)
    angles = positions.astype(F32)[:, None] * inv_freq[None, :]
    cos_half, sine_half = jnp.cos(angles), jnp.sin(angles)
    rest = jnp.zeros((positions.shape[0], HD - ROT), F32)
    tables = (
        jnp.concatenate([cos_half, cos_half, rest + 1.0], axis=1),
        jnp.concatenate([-sine_half, sine_half, rest], axis=1),
    )

    mix_flat = mix_coeffs.reshape(tokens, -1)
    query_in, kv_in, residual = front(layer_stack, mix_flat, ln_gain, ln_bias)
    query_beside, query_arrived = send_tokens(query_in)
    kv_beside, kv_arrived = send_tokens(kv_in)
    for h in range(1, halves):
        (attn_halves[h],), query_arrived = together([attn_halves[h]], query_arrived)
        attn_full.append(gather_weight(attn_halves[h]))
    feed_full = [gather_weight(after(feed_local, attn_halves[-1])[0])]
    feed_halves, kv_arrived = together(halves_of(feed_local)[1:], kv_arrived)
    kv_arrived, (*tables, scalars) = together(kv_arrived, [*tables, scalars])
    query_all = token_blocks(query_in, query_beside, query_arrived)
    kv_all = token_blocks(kv_in, kv_beside, kv_arrived)
    query = qkv_proj(query_all, attn_full, 0, qkv_biases, tables)
    kv = qkv_proj(kv_all, attn_full, 1, qkv_biases, tables)
    head, log_total = attend(scalars, query, kv, group)
    feed_halves, (head,) = together(feed_halves, [head])
    feed_full += [gather_weight(held) for held in feed_halves]
    own, theirs = unproj(head, 0, 1, attn_full, 3, group)
    terms = [own, swap(theirs, "core", 1)]
    arrived = send_sums(chip_sums(*terms))
    hidden, normed2 = middle(
        terms + arrived, residual, out_bias.reshape(1, -1), ln_gain, ln_bias
    )
    normed2_all = token_blocks(normed2, *send_tokens(normed2))
    act, slope = zip(expand(normed2_all, feed_full[0], up_biases[0]))
    new_act, new_slope, (own, theirs) = feed(
        normed2_all, act, feed_full, 0, up_biases[1:], False
    )
    act, slope = [*act, *new_act], [*slope, *new_slope]
    terms = [own, swap(theirs, "core", 1)]
    layer_out, coeff_out, grad_layer, grad_down, mix_sums, mix_in_part, mix_out_part = mixing(
        terms + send_sums(chip_sums(*terms)), hidden, down_bias.reshape(1, -1), mix_gain.reshape(1, -1),
        mix_in, mix_out, out_grad, coeff_grad,
    )

    mixed = mix_in_part.shape[0]
    early = jnp.concatenate(
        [
            mix_in_part,
            mix_sums[:2],
            jnp.pad(mix_out_part.reshape(1, -1), ((0, 0), (0, width - mix_out.size))),
        ],
        axis=0,
    )
    rounds = [("core", 1)]
    for axis in ("row", "zh", "zl"):
        rounds += [(axis, 1 << bit) for bit in range(lax.axis_size(axis).bit_length() - 1)]
    beside, arrived = send_tokens(grad_down)
    (got,), (beside,) = together([swap(early, *rounds[0])], [beside])
    early = early + got
    (got,), arrived = together([swap(early, *rounds[1])], arrived)
    early = early + got
    grad_down_all = token_blocks(grad_down, beside, arrived)
    got = swap(early, *rounds[2])
    half_rank = lax.axis_index("zh").reshape(1)
    down_wide = weight_grad(grad_down_all, act, feats, half_rank)
    got, down_wide, grad_down_all[0] = after(got, down_wide, grad_down_all[0])
    early = early + got
    down_mine = scatter_weight(down_wide)
    got = swap(early, *rounds[3])
    grad_up, up_bias_part, (own, theirs) = feed(grad_down_all, (), feed_full, 1, slope, True)
    got, theirs, late_grad = after(got, theirs, grad_up[0])
    early = early + got
    terms = [own, swap(theirs, "core", 1)]
    arrived = send_sums(chip_sums(*terms))
    up_wide = weight_grad(normed2_all, (late_grad, *grad_up[1:]), feats, half_rank)
    (up_wide,), arrived = together([up_wide], arrived)
    up_mine = scatter_weight(up_wide)
    grad_hidden, grad_attn, mid_sums = middle_back(terms + arrived, hidden, grad_layer, ln_gain)
    grad_attn_all = token_blocks(grad_attn, *send_tokens(grad_attn))
    grad_heads = proj(grad_attn_all, attn_full, 3, cols)
    got = swap(early, *rounds[4])
    grads, bias_sums = attend_back(scalars, query, kv, grad_heads, log_total, tables, group)
    got, grads = after(got, grads)
    early = early + got
    for more in rounds[5:]:
        early = early + swap(early, *more)
    query_own, theirs = unproj(grads, 0, 1, attn_full, 0, group)
    grads, query_own = after(grads, query_own)
    query_got = swap(theirs, "core", 1)
    kv_own, theirs = unproj(grads, 1, 2, attn_full, 1, group)
    query_got, kv_own = after(query_got, kv_own)
    query_crossing = send_sums(chip_sums(query_own, query_got))
    kv_got = swap(theirs, "core", 1)
    kv_sums = chip_sums(kv_own, kv_got)
    late_head, *kv_sums = after(head, *kv_sums)
    kv_crossing = send_sums(kv_sums)
    attn_parts = piece_grad(
        rank, row_count, orders, query_all, kv_all, grads, grad_attn_all, late_head, halves
    )
    norm = lambda streams, terms: norm_back(streams, terms, layer_stack, mix_flat, ln_gain)
    near = [attn_parts[p][0] for p in range(2)]
    far = [attn_parts[p][h] for h in range(1, halves) for p in range(2)]
    which = [p for h in range(1, halves) for p in range(2)]
    steps = len(orders[0])
    got = [send_half(v, orders[p][0]) for v, p in zip(far, which)]
    query_grads, query_sums = norm((0,), [query_own, query_got, *query_crossing])
    got, (query_grads, *near) = together(got, [query_grads, *near])
    far = [add_half(v, g).astype(BF) for v, g in zip(far, got)]
    got = [send_half(v, orders[p][1]) for v, p in zip(far, which)]
    near_got = [send_half(v, orders[p][0]) for p, v in enumerate(near)]
    got, kv_crossing = together(got, kv_crossing)
    far = [add_half(v, g).astype(BF) for v, g in zip(far, got)]
    for n in range(2, steps):
        got = [send_half(v, orders[p][n]) for v, p in zip(far, which)]
        far = [add_half(v, g).astype(BF) for v, g in zip(far, got)]
    attn_others = [swap(v, "zh", n // 2 + 1) for n, v in enumerate(far)]
    kv_grads, kv_sums = norm((1, 2), [kv_own, kv_got, *kv_crossing])
    near_got, (kv_grads,) = together(near_got, [kv_grads])
    near = [add_half(v, g) for v, g in zip(near, near_got)]
    stream_grads = (query_grads, kv_grads, grad_hidden)
    sums = [query_sums[0], kv_sums[0], kv_sums[1]]
    mix_in_grad = early[:mixed].T
    down_bias_grad, mix_gain_grad = early[mixed], early[mixed + 1]
    mix_out_grad = early[mixed + 2, : mix_out.size].reshape(mix_out.shape)
    heads = cols // HD
    bias_line = lax.broadcasted_iota(jnp.int32, (halves * group, 1), 0)
    zh = lax.axis_index("zh")
    bias_rows = 0.0
    for h in range(halves):
        here = bias_sums[h * heads : (h + 1) * heads, :3].transpose(1, 0, 2).reshape(1, -1)
        line = jnp.concatenate([here, up_bias_part[h]], axis=1)
        bias_rows = bias_rows + jnp.where(bias_line == (zh ^ h) * group + place, line, 0.0)
    late = jnp.concatenate(
            [
                *[part[0:8].sum(axis=0, keepdims=True) for part in sums],
                mid_sums[0:1],
                *[part[8:16].sum(axis=0, keepdims=True) for part in sums],
                mid_sums[1:3],
                jnp.pad(bias_rows, ((0, 0), (0, width - bias_rows.shape[1]))),
            ],
            axis=0,
    )
    near = [v.astype(BF) for v in near]
    near_got = [send_half(v, orders[p][1]) for p, v in enumerate(near)]
    got = swap(late, *rounds[1])
    stack_grad, coeffs_grad = stack_back(stream_grads, layer_stack, mix_flat)
    (got, attn_others[0], *near_got), (stack_grad,) = together(
        [got, attn_others[0], *near_got], [stack_grad]
    )
    late = late + got
    got, attn_others[1] = after(swap(late, *rounds[2]), attn_others[1])
    late = late + got
    near = [add_half(v, g) for v, g in zip(near, near_got)]
    for n in range(2, steps):
        near = [v.astype(BF) for v in near]
        near_got = [send_half(v, orders[p][n]) for p, v in enumerate(near)]
        near = [add_half(v, g) for v, g in zip(near, near_got)]
    rest = rounds[3:] + rounds[:1]
    for more in [r for r in rest if r[0] != "zh"] + [r for r in rest if r[0] == "zh"]:
        late = late + swap(late, *more)
    down_grad = down_mine.astype(F32).T
    up_grad = up_mine.astype(F32)
    attn_grad = [total_grad(near[p], attn_others[p::2]) for p in range(2)]
    qkv_grad = jnp.stack(
        [attn_grad[0][:, :cols], attn_grad[0][:, cols:], attn_grad[1][:, :cols]], axis=0
    )
    out_w_grad = attn_grad[1][:, cols:].T

    bias_grad = lax.dynamic_slice_in_dim(late, 9 + zh * group + place, 1, 0)
    qkv_bias_grad = bias_grad[0, : 3 * cols].reshape(3, cols)
    up_bias_grad = bias_grad[0, 3 * cols : 3 * cols + up_bias.shape[0]]
    return (
        layer_out,
        coeff_out,
        stack_grad,
        coeffs_grad.reshape(mix_coeffs.shape),
        late[0:4],
        late[4:8],
        qkv_grad,
        qkv_bias_grad,
        out_w_grad,
        late[8],
        up_grad,
        up_bias_grad,
        down_grad,
        down_bias_grad,
        mix_gain_grad,
        mix_in_grad,
        mix_out_grad,
    )


def solution(mesh):
    rows, cols = mesh.shape["row"], mesh.shape["col"]
    col = ("zh", "zl", "core")

    def run(*args):
        seqs = args[2].shape[0] // rows
        fine = Mesh(mesh.devices.reshape(rows, seqs, cols // (2 * seqs), 2), ALL)
        in_specs = (
            P(None, ALL, None),
            P(ALL, None, None),
            P("row"),
            P(),
            P(),
            P(None, "row", col),
            P(None, col),
            P(col, "row"),
            P(),
            P("row", col),
            P(col),
            P(col, "row"),
            P(),
            P(),
            P(),
            P(),
            P(ALL, None),
            P(ALL, None),
        )
        out_specs = (
            P(ALL, None),
            P(ALL, None),
            P(None, ALL, None),
            P(ALL, None, None),
            P(),
            P(),
            P(None, "row", col),
            P(None, col),
            P(col, "row"),
            P(),
            P("row", col),
            P(col),
            P(col, "row"),
            P(),
            P(),
            P(),
            P(),
        )
        return jax.shard_map(
            on_device, mesh=fine, in_specs=in_specs, out_specs=out_specs, check_vma=False
        )(*args)

    return run
```
